32 devices in a mesh: dp: 8 (over z, y), tensor: 4 (over x, core).
Axes of the slice: x: 2, y: 2, z: 4, core: 2. Of those that a mesh axis runs over, the one named last changes fastest.
Arguments:
- tokens: bfloat16 [4096, 768], P('dp'), may hold values from -6 to 6
- w_qkv: bfloat16 [3, 768, 768], P(None, None, 'tensor'), may hold values from -0.21875 to 0.21875
- bias_qv: float32 [2, 768], P(None, 'tensor'), may hold values from -3 to 3
- w_out: bfloat16 [768, 768], P('tensor'), may hold values from -0.875 to 0.875
- bias_out: float32 [768], replicated, may hold values from -3 to 3
- gain_one: float32 [768], replicated, may hold values from 0.25 to 1.75
- shift_one: float32 [768], replicated, may hold values from -3 to 3
- w_up: bfloat16 [768, 3072], P(None, 'tensor'), may hold values from -0.21875 to 0.21875
- bias_up: float32 [3072], P('tensor'), may hold values from -3 to 3
- w_down: bfloat16 [3072, 768], P('tensor'), may hold values from -0.109375 to 0.109375
- bias_down: float32 [768], replicated, may hold values from -3 to 3
- gain_two: float32 [768], replicated, may hold values from 0.25 to 1.75
- shift_two: float32 [768], replicated, may hold values from -3 to 3
- cotangent: bfloat16 [4096, 768], P('dp'), may hold values from -6 to 6
- lengths: int32 [8], P('dp'), may hold values from 128 to 512, as said below
Outputs:
- output: bfloat16 [4096, 768], P('dp')
- grad_tokens: bfloat16 [4096, 768], P('dp')
- grad_w_qkv: float32 [3, 768, 768], P(None, 'dp', 'tensor')
- grad_bias_qv: float32 [2, 768], P(None, ('tensor', 'dp'))
- grad_w_out: float32 [768, 768], P('tensor', 'dp')
- grad_bias_out: float32 [768], P('dp')
- grad_gain_one: float32 [768], P('dp')
- grad_shift_one: float32 [768], P('dp')
- grad_w_up: float32 [768, 3072], P('dp', 'tensor')
- grad_bias_up: float32 [3072], P(('tensor', 'dp'))
- grad_w_down: float32 [3072, 768], P('tensor', 'dp')
- grad_bias_down: float32 [768], P('dp')
- grad_gain_two: float32 [768], P('dp')
- grad_shift_two: float32 [768], P('dp')
The draws below stay inside these ranges and needn't reach their ends.
Inputs may be any that keep to these rules, and one draw needn't show every extreme that they name: `lengths`: every value is at least 128; some sequence is exactly 512 long.
All inputs are finite; a program needn't handle non-finite values.
Results may differ from the reference program's by a relative error of at most 0.02.
The reference program's roundings to bfloat16 on the way count: a program that leaves them out, or rounds other values in their place, can miss the bound.
Values may be sent and summed in bfloat16 or wider, within the bound.
No kernel may reach another device: no remote copies, remote signals or barrier semaphores. Data moves between devices by JAX's collectives and lax.ppermute only.
A program may use at most 64 MiB of HBM per device.

```python
import math
import jax
import jax.numpy as jnp
from jax import lax

HEADS = 12
HEAD_DIM = 64
FF = 3072
D = 768
SEQ_LEN = 512
SEQS = 8
TOKENS = 4096


def draw_lengths(key, part):
    key = jax.random.fold_in(key, 7)
    first_key, second_key = jax.random.split(key)
    spread = jax.random.randint(first_key, (SEQS,), 0, SEQ_LEN + 1)
    seq_lengths = SEQ_LEN // 4 + spread * spread * 3 // (4 * SEQ_LEN)
    longest = jax.random.randint(second_key, (), 0, SEQS)
    return seq_lengths.at[longest].set(SEQ_LEN).astype(jnp.int32)


def raised(values, stream_key, source, target, shards_of, factor):
    def block_of(dim):
        return (jnp.arange(values.shape[dim]) // (values.shape[dim] // shards_of)).reshape((-1,) + (1,) * (values.ndim - 1 - dim))

    near = jax.random.permutation(stream_key, shards_of)[block_of(target)]
    other_side = (block_of(target) + shards_of // 2) % shards_of
    return jnp.where((block_of(source) == near) | (block_of(source) == other_side), factor * values, values)


def block_levels(rng, shape, cuts, smallest, high):
    loudness = 1.0
    for axis_at, blocks in cuts:
        draws = jax.random.uniform(jax.random.fold_in(jax.random.fold_in(rng, 6), axis_at), (blocks,), jnp.float32, smallest / len(cuts), high / len(cuts))
        loudness = loudness * jnp.repeat(jnp.exp(draws), shape[axis_at] // blocks).reshape((-1,) + (1,) * (len(shape) - 1 - axis_at))
    return loudness


def gaussian(key, extent, width, bound, shards=(), held_as=jnp.bfloat16):
    array = jax.random.normal(key, extent, jnp.float32) * width
    if len(shards) > 0:
        array = block_levels(key, extent, shards, -0.22, 0.18) * array
    return jnp.clip(array, min=-bound, max=bound).astype(held_as)


def gaussian_with(stream_key, dims, width, most, pieces, heavy, dtype=jnp.bfloat16):
    drawn = width * jax.random.normal(stream_key, dims, jnp.float32)
    if pieces:
        drawn = drawn * block_levels(stream_key, dims, pieces, -0.22, 0.18)
    return jnp.clip(raised(drawn, jax.random.fold_in(stream_key, 3), *heavy), -most, most).astype(dtype)


def setup_inputs(seed: int = 0) -> dict:
    splits = jax.random.split(jax.random.key(seed), 16)
    return {
        "tokens": gaussian(splits[0], (TOKENS, D), 1.0, 6.0, ((0, 8),)),
        "w_qkv": gaussian(splits[1], (3, D, D), D ** -0.5, 0.21875, ((2, 4),)),
        "bias_qv": gaussian(splits[2], (2, D), 0.5, 3.0, ((1, 4),), jnp.float32),
        "w_out": gaussian(splits[3], (D, D), (D // 16) ** -0.5, 0.875, ((0, 4),)),
        "bias_out": gaussian(splits[4], (D,), 0.5, 3.0, (), jnp.float32),
        "gain_one": jnp.clip(1.0 + 0.15 * jax.random.normal(splits[5], (D,), jnp.float32), 0.25, 1.75),
        "shift_one": gaussian(splits[6], (D,), 0.5, 3.0, (), jnp.float32),
        "w_up": gaussian(splits[7], (D, FF), D ** -0.5, 0.21875, ((1, 4),)),
        "bias_up": gaussian(splits[8], (FF,), 0.5, 3.0, ((0, 4),), jnp.float32),
        "w_down": gaussian(splits[9], (FF, D), FF ** -0.5, 0.109375, ((0, 4),)),
        "bias_down": gaussian(splits[10], (D,), 0.5, 3.0, (), jnp.float32),
        "gain_two": jnp.clip(1.0 + 0.15 * jax.random.normal(splits[11], (D,), jnp.float32), 0.25, 1.75),
        "shift_two": gaussian(splits[12], (D,), 0.5, 3.0, (), jnp.float32),
        "cotangent": gaussian_with(splits[13], (TOKENS, D), 1.0, 6.0, ((0, 8),), (0, 1, 8, 2.0)),
        "lengths": draw_lengths(jax.random.fold_in(splits[15], 71), 0),
    }


@jax.custom_vjp
def low(v):
    return lax.optimization_barrier(v.astype(jnp.bfloat16)).astype(jnp.float32)

@jax.custom_vjp
def low_back(v):
    return v

def low_keep(v):
    return (low(v), None)

def low_pass(kept, grad):
    return (grad,)

def back_keep(v):
    return (v, None)

def back_low(kept, grad):
    return (low(grad),)
low.defvjp(low_keep, low_pass)
low_back.defvjp(back_keep, back_low)
norm_epsilon = 1e-05

def normalize(resid, gain, shift):
    center = resid - lax.optimization_barrier(jnp.mean(resid, -1, keepdims=True))
    inverse = lax.rsqrt(lax.optimization_barrier(jnp.mean(center * center, -1, keepdims=True)) + norm_epsilon)
    return center * inverse * gain + shift

def encoder_layer(tokens, w_qkv, bias_qv, w_out, bias_out, gain_one, shift_one, w_up, bias_up, w_down, bias_down, gain_two, shift_two, valid_slot):
    highest = lax.Precision.HIGHEST
    group_size, seq_span, model_width = tokens.shape
    projected = jnp.einsum('gld,cde->cgle', tokens, w_qkv, precision=highest)
    query = low_back(low(projected[0] + bias_qv[0]))
    key_rows = low_back(low(projected[1]))
    value_rows = low_back(low(projected[2] + bias_qv[1]))
    head_shape = (group_size, seq_span, HEADS, HEAD_DIM)
    query = query.reshape(head_shape)
    key_rows = key_rows.reshape(head_shape)
    value_rows = value_rows.reshape(head_shape)
    scores = low_back(jnp.einsum('gqhd,gkhd->ghqk', query, key_rows, precision=highest) * HEAD_DIM ** (-0.5))
    scores = jnp.where(valid_slot[:, None, None, :], scores, -1e+30)
    peak_score = lax.optimization_barrier(jnp.max(scores, -1, keepdims=True))
    expo = jnp.exp(scores - peak_score)
    weights = low(expo / lax.optimization_barrier(jnp.sum(expo, -1, keepdims=True)))
    attended = jnp.einsum('ghqk,gkhd->gqhd', weights, value_rows, precision=highest)
    attended = low_back(low(attended.reshape(group_size, seq_span, model_width)))
    branch_attn = low_back(jnp.einsum('gld,de->gle', attended, w_out, precision=highest) + bias_out)
    hidden = normalize(tokens + branch_attn, gain_one, shift_one)
    pre_act = low_back(jnp.einsum('gld,df->glf', low(hidden), w_up, precision=highest) + bias_up)
    act_low = low(jax.nn.gelu(pre_act, approximate=False))
    branch_mlp = low_back(jnp.einsum('glf,fd->gld', act_low, w_down, precision=highest) + bias_down)
    result = normalize(hidden + branch_mlp, gain_two, shift_two)
    return jnp.where(valid_slot[:, :, None], result, 0.0)

def reference(tokens, w_qkv, bias_qv, w_out, bias_out, gain_one, shift_one, w_up, bias_up, w_down, bias_down, gain_two, shift_two, cotangent, lengths):
    params = (w_qkv.astype(jnp.float32), bias_qv.astype(jnp.float32), w_out.astype(jnp.float32), bias_out.astype(jnp.float32), gain_one.astype(jnp.float32), shift_one.astype(jnp.float32), w_up.astype(jnp.float32), bias_up.astype(jnp.float32), w_down.astype(jnp.float32), bias_down.astype(jnp.float32), gain_two.astype(jnp.float32), shift_two.astype(jnp.float32))
    seq_count = lengths.shape[0]
    group_size = math.gcd(seq_count, max(1, 4096 // SEQ_LEN))
    group_count = seq_count // group_size
    valid_slot = lax.broadcasted_iota(jnp.int32, (seq_count, SEQ_LEN), 1) < lengths.astype(jnp.int32)[:, None]
    tok_groups = tokens.astype(jnp.float32).reshape(group_count, group_size, SEQ_LEN, D)
    cot_groups = cotangent.astype(jnp.float32).reshape(group_count, group_size, SEQ_LEN, D)
    valid_groups = valid_slot.reshape(group_count, group_size, SEQ_LEN)

    def one_group(running, inputs):
        tok_group, cot_group, valid_group = inputs

        def forward(tok_arg, *weight_args):
            return encoder_layer(tok_arg, *weight_args, valid_group)
        result, pullback = jax.vjp(forward, tok_group, *params)
        gradient = pullback(cot_group)
        running = tuple((total + extra for total, extra in zip(running, gradient[1:])))
        return (running, (result, gradient[0]))
    zeros_init = tuple((jnp.zeros_like(param) for param in params))
    totals, (results, tok_grads) = lax.scan(one_group, zeros_init, (tok_groups, cot_groups, valid_groups))
    return (results.reshape(TOKENS, D).astype(jnp.bfloat16), tok_grads.reshape(TOKENS, D).astype(jnp.bfloat16), totals[0], totals[1], totals[2], totals[3], totals[4], totals[5], totals[6], totals[7], totals[8], totals[9], totals[10], totals[11])
```

```python
from functools import partial

import jax
import jax.numpy as jnp
from jax import lax
from jax.sharding import PartitionSpec as P

HEAD_DIM = 64

norm_epsilon = 1e-05

CORE_PAIRS = [(i, i ^ 1) for i in range(4)]
CHIP_PAIRS = [(i, i ^ 2) for i in range(4)]


def normalize(resid):
    center = resid - jnp.mean(resid, -1, keepdims=True)
    inverse = lax.rsqrt(jnp.mean(center * center, -1, keepdims=True) + norm_epsilon)
    return (center * inverse, inverse)


def norm_back(grad_norm, normed, inverse):
    mean_grad = jnp.mean(grad_norm, -1, keepdims=True)
    mean_proj = jnp.mean(grad_norm * normed, -1, keepdims=True)
    return inverse * (grad_norm - mean_grad - normed * mean_proj)


def half_rows(full, which):
    half = full.shape[0] // 2
    return lax.dynamic_slice_in_dim(full, which * half, half, 0)


def to_core(block):
    return lax.ppermute(block, "tensor", CORE_PAIRS)


def to_chip(block):
    return lax.ppermute(block, "tensor", CHIP_PAIRS)


def half_sum(row_input, weight, contract, core):
    def part(which):
        return lax.dot_general(
            half_rows(row_input, which),
            weight,
            (((1,), (contract,)), ((), ())),
            preferred_element_type=jnp.float32,
        )

    received = to_core(part(1 - core).astype(jnp.bfloat16))
    chip_sum = (part(core) + received.astype(jnp.float32)).astype(jnp.bfloat16)
    return chip_sum.astype(jnp.float32) + to_chip(chip_sum).astype(jnp.float32)


def whole_rows(own_half, core):
    other_half = to_core(own_half)
    half = own_half.shape[0]
    full = jnp.zeros((2 * half, own_half.shape[1]), own_half.dtype)
    full = lax.dynamic_update_slice_in_dim(full, own_half, core * half, 0)
    return lax.dynamic_update_slice_in_dim(full, other_half, (1 - core) * half, 0)


def sum_scatter(buffer, dp_size):
    bits = dp_size.bit_length() - 1
    if 1 << bits != dp_size:
        return lax.psum_scatter(buffer, "dp", scatter_dimension=0, tiled=False)
    mine = lax.axis_index("dp")
    held = buffer.reshape((2,) * bits + buffer.shape[1:])
    for bit in range(bits):
        axis = bits - 1 - bit
        side = (mine >> bit) & 1
        sent = lax.dynamic_index_in_dim(held, 1 - side, axis, keepdims=False)
        kept = lax.dynamic_index_in_dim(held, side, axis, keepdims=False)
        pairs = [(i, i ^ (1 << bit)) for i in range(dp_size)]
        received = lax.ppermute(sent.astype(jnp.bfloat16), "dp", pairs)
        held = kept.astype(jnp.float32) + received.astype(jnp.float32)
    return held


def small_scatter(vectors, dp_size):
    count, width = vectors.shape[0], vectors.shape[1] // dp_size
    blocks = vectors.reshape(count, dp_size, width).transpose(1, 0, 2)
    bits = dp_size.bit_length() - 1
    if 1 << bits != dp_size:
        return lax.psum_scatter(blocks, "dp", scatter_dimension=0, tiled=False)
    mine = lax.axis_index("dp")
    held = blocks.reshape((2,) * bits + blocks.shape[1:])
    for bit in range(bits):
        axis = bits - 1 - bit
        side = (mine >> bit) & 1
        sent = lax.dynamic_index_in_dim(held, 1 - side, axis, keepdims=False)
        kept = lax.dynamic_index_in_dim(held, side, axis, keepdims=False)
        pairs = [(i, i ^ (1 << bit)) for i in range(dp_size)]
        held = kept + lax.ppermute(sent, "dp", pairs)
    return held


def on_device(
    tokens,
    w_qkv,
    bias_qv,
    w_out,
    bias_out,
    gain_one,
    shift_one,
    w_up,
    bias_up,
    w_down,
    bias_down,
    gain_two,
    shift_two,
    cotangent,
    lengths,
):
    seq_count = lengths.shape[0]
    row_count, model_width = tokens.shape
    seq_span = row_count // seq_count
    local_width = w_qkv.shape[2]
    heads_here = local_width // HEAD_DIM
    score_scale = HEAD_DIM ** (-0.5)
    dp_size = lax.axis_size("dp")
    core = lax.axis_index("tensor") % 2
    block = model_width // dp_size

    position = lax.broadcasted_iota(jnp.int32, (seq_count, seq_span), 1)
    valid_slot = position < lengths[:, None]
    row_valid = valid_slot.reshape(row_count, 1)
    key_valid = valid_slot[:, None, None, :]
    projected = jnp.einsum("rd,cde->cre", tokens, w_qkv, preferred_element_type=jnp.float32)
    head_shape = (seq_count, seq_span, heads_here, HEAD_DIM)
    query_heads = (projected[0] + bias_qv[0]).astype(jnp.bfloat16).reshape(head_shape)
    key_heads = projected[1].astype(jnp.bfloat16).reshape(head_shape)
    value_heads = (projected[2] + bias_qv[1]).astype(jnp.bfloat16).reshape(head_shape)

    def score_block():
        raw_scores = (
            jnp.einsum(
                "sqhd,skhd->shqk", query_heads, key_heads, preferred_element_type=jnp.float32
            )
            * score_scale
        )
        return jnp.where(key_valid, raw_scores, -1e30)

    scores = score_block()
    peak_score = jnp.max(scores, -1, keepdims=True)
    expo = jnp.exp(scores - peak_score)
    denominator = jnp.sum(expo, -1, keepdims=True)
    probs_low = (expo / denominator).astype(jnp.bfloat16)
    log_total = peak_score + jnp.log(denominator)
    attended = (
        jnp.einsum("shqk,skhd->sqhd", probs_low, value_heads, preferred_element_type=jnp.float32)
        .astype(jnp.bfloat16)
        .reshape(row_count, local_width)
    )
    own_tokens = half_rows(tokens, core).astype(jnp.float32)
    branch_attn = half_sum(attended, w_out, 0, core) + bias_out
    normal_one, inverse_one = normalize(own_tokens + branch_attn)
    hidden = normal_one * gain_one + shift_one
    hidden_low = whole_rows(hidden.astype(jnp.bfloat16), core)
    pre_act = jnp.dot(hidden_low, w_up, preferred_element_type=jnp.float32) + bias_up
    act_low = jax.nn.gelu(pre_act, approximate=False).astype(jnp.bfloat16)
    branch_mlp = half_sum(act_low, w_down, 0, core) + bias_down
    valid_here = half_rows(row_valid, core)
    cot_here = half_rows(cotangent, core)
    normal_two, inverse_two = normalize(hidden + branch_mlp)
    output_low = jnp.where(valid_here, normal_two * gain_two + shift_two, 0.0).astype(jnp.bfloat16)
    grad_out = jnp.where(valid_here, cot_here.astype(jnp.float32), 0.0)
    grad_gain_two = jnp.sum(grad_out * normal_two, 0)
    grad_shift_two = jnp.sum(grad_out, 0)
    grad_resid_two = norm_back(grad_out * gain_two, normal_two, inverse_two)
    grad_mlp = whole_rows(grad_resid_two.astype(jnp.bfloat16), core)
    output_low = whole_rows(output_low, core)
    grad_bias_down = jnp.sum(grad_mlp.astype(jnp.float32), 0)
    grad_act = jnp.einsum("rd,fd->rf", grad_mlp, w_down, preferred_element_type=jnp.float32)
    gelu_value, gelu_pull = jax.vjp(partial(jax.nn.gelu, approximate=False), pre_act)
    grad_pre = gelu_pull(grad_act)[0].astype(jnp.bfloat16)
    grad_bias_up = jnp.sum(grad_pre.astype(jnp.float32), 0)
    grad_hidden = grad_resid_two + half_sum(grad_pre, w_up, 1, core)
    grad_w_down = jnp.einsum("rd,rf->df", grad_mlp, act_low, preferred_element_type=jnp.float32)
    grad_w_up = jnp.einsum("rd,rf->df", hidden_low, grad_pre, preferred_element_type=jnp.float32)
    sum_w_down = sum_scatter(grad_w_down.reshape(dp_size, block, -1), dp_size)
    sum_w_up = sum_scatter(grad_w_up.reshape(dp_size, block, -1), dp_size)

    grad_gain_one = jnp.sum(grad_hidden * normal_one, 0)
    grad_shift_one = jnp.sum(grad_hidden, 0)
    grad_resid_one = norm_back(grad_hidden * gain_one, normal_one, inverse_one)
    grad_attn = whole_rows(grad_resid_one.astype(jnp.bfloat16), core)
    half_vectors = jnp.stack([grad_gain_two, grad_shift_two, grad_gain_one, grad_shift_one])
    half_vectors = half_vectors + to_core(half_vectors)
    grad_bias_out = jnp.sum(grad_attn.astype(jnp.float32), 0)
    grad_w_out = jnp.einsum("rl,rd->dl", attended, grad_attn, preferred_element_type=jnp.float32)
    grad_attended = (
        jnp.einsum("rd,ld->rl", grad_attn, w_out, preferred_element_type=jnp.float32)
        .astype(jnp.bfloat16)
        .reshape(head_shape)
    )
    probs = jnp.exp(score_block() - log_total)
    grad_probs = jnp.einsum(
        "sqhd,skhd->shqk", grad_attended, value_heads, preferred_element_type=jnp.float32
    )
    grad_values = jnp.einsum(
        "shqk,sqhd->skhd",
        probs.astype(jnp.bfloat16),
        grad_attended,
        preferred_element_type=jnp.float32,
    )
    inner_sum = jnp.sum(grad_probs * probs, -1, keepdims=True)
    grad_scores = (probs * (grad_probs - inner_sum)).astype(jnp.bfloat16)
    grad_query = (
        jnp.einsum("shqk,skhd->sqhd", grad_scores, key_heads, preferred_element_type=jnp.float32)
        * score_scale
    )
    grad_keys = (
        jnp.einsum("shqk,sqhd->skhd", grad_scores, query_heads, preferred_element_type=jnp.float32)
        * score_scale
    )
    grad_proj = jnp.concatenate(
        [
            part.astype(jnp.bfloat16).reshape(row_count, local_width)
            for part in (grad_query, grad_keys, grad_values)
        ],
        1,
    )
    bias_sums = jnp.sum(grad_proj.astype(jnp.float32), 0).reshape(3, local_width)
    grad_bias_qv = jnp.stack([bias_sums[0], bias_sums[2]])
    grad_w_qkv = jnp.einsum("rd,re->de", tokens, grad_proj, preferred_element_type=jnp.float32)
    grad_w_attn = jnp.concatenate([grad_w_qkv, grad_w_out], 1)
    sum_w_attn = sum_scatter(grad_w_attn.reshape(dp_size, block, -1), dp_size)
    sum_w_qkv = sum_w_attn[:, : 3 * local_width].reshape(block, 3, local_width).transpose(1, 0, 2)
    sum_w_out = sum_w_attn[:, 3 * local_width :]
    w_flat = w_qkv.transpose(1, 0, 2).reshape(model_width, 3 * local_width)
    own_grad = (grad_resid_one + half_sum(grad_proj, w_flat, 1, core)).astype(jnp.bfloat16)
    token_total = whole_rows(own_grad, core)

    vectors = jnp.concatenate(
        [half_vectors, jnp.stack([grad_bias_down, grad_bias_out, grad_bias_up])], 0
    )
    sums = small_scatter(vectors, dp_size)
    sum_bias_qv = small_scatter(grad_bias_qv, dp_size)
    return (
        output_low,
        token_total,
        sum_w_qkv,
        sum_bias_qv,
        sum_w_out.T,
        sums[5],
        sums[2],
        sums[3],
        sum_w_up,
        sums[6],
        sum_w_down.T,
        sums[4],
        sums[0],
        sums[1],
    )


def solution(mesh):
    placed = (
        P("dp", None),
        P(None, None, "tensor"),
        P(None, "tensor"),
        P("tensor", None),
        P(),
        P(),
        P(),
        P(None, "tensor"),
        P("tensor"),
        P("tensor", None),
        P(),
        P(),
        P(),
        P("dp", None),
        P("dp"),
    )
    return jax.shard_map(
        on_device,
        mesh=mesh,
        in_specs=placed,
        out_specs=(
            P("dp", None),
            P("dp", None),
            P(None, "dp", "tensor"),
            P(None, ("tensor", "dp")),
            P("tensor", "dp"),
            P("dp"),
            P("dp"),
            P("dp"),
            P("dp", "tensor"),
            P(("tensor", "dp")),
            P("tensor", "dp"),
            P("dp"),
            P("dp"),
            P("dp"),
        ),
        check_vma=False,
    )
```

```python
import jax
import jax.numpy as jnp
import numpy as np
from jax import lax
from jax.experimental import pallas as pl
from jax.experimental.pallas import tpu as pltpu
from jax.sharding import PartitionSpec as P

HEAD_DIM = 64
NORM_EPSILON = 1e-05
CORES = 2
F32 = jnp.float32
LOW = jnp.bfloat16
MIB = 1 << 20

VECTOR_ROWS = 8
PAIR_ROWS = 2 * VECTOR_ROWS


def nn(left, right):
    return lax.dot_general(left, right, (((1,), (0,)), ((), ())), preferred_element_type=F32)


def nt(left, right):
    return lax.dot_general(left, right, (((1,), (1,)), ((), ())), preferred_element_type=F32)


def tn(left, right):
    return lax.dot_general(left, right, (((0,), (0,)), ((), ())), preferred_element_type=F32)


def normalize(resid):
    center = resid - jnp.mean(resid, -1, keepdims=True)
    inverse = lax.rsqrt(jnp.mean(center * center, -1, keepdims=True) + NORM_EPSILON)
    return center * inverse, inverse


def norm_back(grad_norm, normed, inverse):
    mean_grad = jnp.mean(grad_norm, -1, keepdims=True)
    mean_proj = jnp.mean(grad_norm * normed, -1, keepdims=True)
    return inverse * (grad_norm - mean_grad - normed * mean_proj)


def call(kernel, outs, scalars, *arrays, scratch=(), flops=0, mib=40):
    shapes = tuple(jax.ShapeDtypeStruct(shape, dtype) for shape, dtype in outs)
    moved = sum(a.size * a.dtype.itemsize for a in arrays)
    moved += sum(int(np.prod(s)) * jnp.dtype(d).itemsize for s, d in outs)
    whole = pl.BlockSpec(memory_space=pltpu.VMEM)
    return pl.pallas_call(
        kernel,
        out_shape=shapes,
        in_specs=[pl.BlockSpec(memory_space=pltpu.SMEM)] + [whole] * len(arrays),
        out_specs=tuple(whole for _ in outs),
        scratch_shapes=list(scratch),
        compiler_params=pltpu.CompilerParams(vmem_limit_bytes=mib * MIB),
        cost_estimate=pl.CostEstimate(flops=int(flops), bytes_accessed=int(moved), transcendentals=0),
    )(scalars, *arrays)


def attn_forward(info, tokens, w_qkv, bias_qv, w_out, q_o, k_o, v_o, att_o, send_o, keep_o):
    core, length = info[0], info[1]
    rows, width = q_o.shape
    half = rows // 2
    x = tokens[...]
    query = (nn(x, w_qkv[0]) + bias_qv[0:1, :]).astype(LOW)
    keys = nn(x, w_qkv[1]).astype(LOW)
    values = (nn(x, w_qkv[2]) + bias_qv[1:2, :]).astype(LOW)
    q_o[...] = query
    k_o[...] = keys
    v_o[...] = values
    head_of = lax.broadcasted_iota(jnp.int32, (rows, width), 1) // HEAD_DIM
    key_valid = lax.broadcasted_iota(jnp.int32, (rows, rows), 1) < length
    scaled = query.astype(F32) * HEAD_DIM ** -0.5
    value_full = values.astype(F32)
    total = jnp.zeros((rows, width), F32)
    for head in range(width // HEAD_DIM):
        here = head_of == head
        scores = nt(jnp.where(here, scaled, 0.0).astype(LOW), keys)
        scores = jnp.where(key_valid, scores, -1e30)
        expo = jnp.exp(scores - jnp.max(scores, -1, keepdims=True))
        probs = (expo * (1.0 / jnp.sum(expo, -1, keepdims=True))).astype(LOW)
        total = total + nn(probs, jnp.where(here, value_full, 0.0).astype(LOW))
    att_o[...] = total.astype(LOW)
    other_start = pl.multiple_of((1 - core) * half, half)
    own_start = pl.multiple_of(core * half, half)
    send_o[...] = nn(att_o[pl.ds(other_start, half), :], w_out[...]).astype(LOW)
    keep_o[...] = nn(att_o[pl.ds(own_start, half), :], w_out[...])


def mlp_forward(
    info, tokens, own, received, bias_out, gain_one, shift_one,
    up_own, up_other, bias_own, bias_other, down_own, down_other,
    pass_o, act_o, slope_own_o, slope_other_o, normed_o, inverse_o, part_o,
):
    half, width = own.shape
    units = up_own.shape[1]
    start = pl.multiple_of(info[0] * half, half)
    resid = tokens[pl.ds(start, half), :].astype(F32) + bias_out[...]
    resid = resid + (own[...].astype(F32) + received[...].astype(F32))
    normed, inverse = normalize(resid)
    normed_o[...] = normed
    inverse_o[...] = inverse
    hidden_low = (normed * gain_one[...] + shift_one[...]).astype(LOW)
    pass_o[:, :width] = hidden_low

    def units_of(up, bias, slope_o):
        pre = nn(hidden_low, up[...]) + bias[...]
        cdf = 0.5 * (1.0 + lax.erf(pre * 0.7071067811865476))
        slope_o[...] = cdf + pre * (jnp.exp(-0.5 * pre * pre) * 0.3989422804014327)
        return (pre * cdf).astype(LOW)

    act_other = units_of(up_other, bias_other, slope_other_o)
    pass_o[:, width : width + units] = act_other
    act_own = units_of(up_own, bias_own, slope_own_o)
    act_o[...] = act_own
    part_o[...] = (nn(act_own, down_own[...]) + nn(act_other, down_other[...])).astype(LOW)


def mlp_backward(
    info, cotangent, own, received, normed_one, gain_one, shift_one, bias_down, gain_two, shift_two,
    slope_own, slope_other, up_own, up_other, down_own, down_other,
    out_o, resid_o, pass_o, pre_o, part_o, sums_o,
):
    half, width = own.shape
    units = up_own.shape[1]
    core, length = info[0], info[1]
    start = pl.multiple_of(core * half, half)
    hidden = normed_one[...] * gain_one[...] + shift_one[...]
    branch = own[...].astype(F32) + received[...].astype(F32) + bias_down[...]
    normed, inverse = normalize(hidden + branch)
    valid = lax.broadcasted_iota(jnp.int32, (half, width), 0) + core * half < length
    out_o[...] = jnp.where(valid, normed * gain_two[...] + shift_two[...], 0.0).astype(LOW)
    grad_out = jnp.where(valid, cotangent[pl.ds(start, half), :].astype(F32), 0.0)
    sums_o[0:1, :] = jnp.sum(grad_out * normed, 0, keepdims=True)
    sums_o[1:2, :] = jnp.sum(grad_out, 0, keepdims=True)
    grad_resid = norm_back(grad_out * gain_two[...], normed, inverse)
    resid_o[...] = grad_resid
    grad_mlp = grad_resid.astype(LOW)
    pass_o[:, :width] = grad_mlp
    pre_other = (nt(grad_mlp, down_other[...]) * slope_other[...]).astype(LOW)
    pass_o[:, width : width + units] = pre_other
    pre_own = (nt(grad_mlp, down_own[...]) * slope_own[...]).astype(LOW)
    pre_o[...] = pre_own
    part_o[...] = (nt(pre_own, up_own[...]) + nt(pre_other, up_other[...])).astype(LOW)


def spread(blocks, grad):
    block = blocks.shape[1]
    for index in range(blocks.shape[0]):
        blocks[index] = grad[index * block : (index + 1) * block, :]


def mlp_weights(
    ids, fwd_own, fwd_other, act_own, bwd_own, bwd_other, pre_own,
    send_o, keep_o, sums_o, up_blocks, down_blocks,
):
    width = up_blocks.shape[2]
    model = fwd_own.shape[1] - width
    grad_mlp_own, grad_mlp_other = bwd_own[:, :model], bwd_other[:, :model]
    pre_other = bwd_other[:, model:]
    spread(down_blocks, tn(grad_mlp_own, act_own[...]) + tn(grad_mlp_other, fwd_other[:, model:]))
    spread(up_blocks, tn(fwd_own[:, :model], pre_own[...]) + tn(fwd_other[:, :model], pre_other))
    count = keep_o.shape[0]
    for index in range(count):
        source = ids[index + count]
        send_o[index, 0] = down_blocks[source].astype(LOW)
        send_o[index, 1] = up_blocks[source].astype(LOW)
    for index in range(count):
        source = ids[index]
        keep_o[index, 0] = down_blocks[source]
        keep_o[index, 1] = up_blocks[source]

    def column_sum(first, second):
        return jnp.sum(first.astype(F32), 0, keepdims=True) + jnp.sum(
            second.astype(F32), 0, keepdims=True
        )

    sums_o[0:1, :] = column_sum(grad_mlp_own, grad_mlp_other)
    sums_o[1:2, :] = column_sum(pre_own[...], pre_other)


def norm_one_back(info, resid_two, own, received, normed, inverse, gain_one, resid_o, low_o, sums_o):
    grad_hidden = resid_two[...] + (own[...].astype(F32) + received[...].astype(F32))
    sums_o[0:1, :] = jnp.sum(grad_hidden * normed[...], 0, keepdims=True)
    sums_o[1:2, :] = jnp.sum(grad_hidden, 0, keepdims=True)
    grad_resid = norm_back(grad_hidden * gain_one[...], normed[...], inverse[...])
    resid_o[...] = grad_resid
    low = grad_resid.astype(LOW)
    low_o[...] = low
    sums_o[2:3, :] = jnp.sum(low.astype(F32), 0, keepdims=True)


def split_pair(vectors):
    high = vectors.astype(LOW)
    return jnp.concatenate([high.astype(F32), vectors - high.astype(F32)], 0).astype(LOW)


def attn_backward(
    info, grad_own, grad_other, w_out, q_i, k_i, v_i, att_i, tokens, vectors,
    gq_o, gk_o, gv_o, send_o, keep_o, grad_attn, blocks, sums,
):
    core, length = info[0], info[1]
    rows, width = q_i.shape
    half = rows // 2
    grad_attn[pl.ds(pl.multiple_of(core * half, half), half), :] = grad_own[...]
    grad_attn[pl.ds(pl.multiple_of((1 - core) * half, half), half), :] = grad_other[...]
    grad_rows = grad_attn[...]
    grad_att = nt(grad_rows, w_out[...]).astype(LOW)
    scale = HEAD_DIM ** -0.5
    head_of = lax.broadcasted_iota(jnp.int32, (rows, width), 1) // HEAD_DIM
    key_valid = lax.broadcasted_iota(jnp.int32, (rows, rows), 0) < length
    query, keys, values = q_i[...], k_i[...], v_i[...]
    scaled = query.astype(F32) * scale
    scaled_keys = keys.astype(F32) * scale
    grad_att_full = grad_att.astype(F32)
    grad_q = jnp.zeros((rows, width), F32)
    grad_k = jnp.zeros((rows, width), F32)
    grad_v = jnp.zeros((rows, width), F32)
    for head in range(width // HEAD_DIM):
        here = head_of == head
        scaled_here = jnp.where(here, scaled, 0.0).astype(LOW)
        scores = jnp.where(key_valid, nt(keys, scaled_here), -1e30)
        expo = jnp.exp(scores - jnp.max(scores, 0, keepdims=True))
        probs = expo * (1.0 / jnp.sum(expo, 0, keepdims=True))
        grad_here = jnp.where(here, grad_att_full, 0.0).astype(LOW)
        grad_probs = nt(values, grad_here)
        grad_v = grad_v + nn(probs.astype(LOW), grad_here)
        inner = jnp.sum(probs * grad_probs, 0, keepdims=True)
        grad_scores = (probs * (grad_probs - inner)).astype(LOW)
        grad_k = grad_k + nn(grad_scores, scaled_here)
        grad_q = grad_q + tn(grad_scores, jnp.where(here, scaled_keys, 0.0).astype(LOW))
    low_q, low_k, low_v = grad_q.astype(LOW), grad_k.astype(LOW), grad_v.astype(LOW)
    gq_o[...] = low_q
    gk_o[...] = low_k
    gv_o[...] = low_v
    x = tokens[...]
    weight = jnp.concatenate(
        [tn(x, low_q), tn(x, low_k), tn(x, low_v), tn(grad_rows, att_i[...])], 1
    )
    spread(blocks, weight)
    sums[...] = vectors[...]
    last = VECTOR_ROWS - 1
    sums[last : last + 1, :width] = jnp.sum(low_q.astype(F32), 0, keepdims=True)
    sums[last : last + 1, 2 * width : 3 * width] = jnp.sum(low_v.astype(F32), 0, keepdims=True)
    vector_sums = sums[...]
    block = blocks.shape[1]
    pair = split_pair(vector_sums)
    count = keep_o.shape[0]
    for index in range(count):
        send_o[index, :block] = blocks[info[2 + index + count]].astype(LOW)
        send_o[index, block:] = pair
    for index in range(count):
        keep_o[index, :block] = blocks[info[2 + index]]
        keep_o[index, block : block + VECTOR_ROWS] = vector_sums
        keep_o[index, block + VECTOR_ROWS :] = jnp.zeros_like(vector_sums)


def token_back(info, gq, gk, gv, w_qkv, send_o, keep_o):
    half = send_o.shape[0]

    def rows_from(start):
        picked = pl.ds(pl.multiple_of(start, half), half)
        return (
            nt(gq[picked, :], w_qkv[0]) + nt(gk[picked, :], w_qkv[1]) + nt(gv[picked, :], w_qkv[2])
        )

    send_o[...] = rows_from((1 - info[0]) * half).astype(LOW)
    keep_o[...] = rows_from(info[0] * half)


def merge_weights(info, keep, received, send_o, keep_o):
    count = keep_o.shape[0]
    for index in range(count):
        send_o[index] = (keep[count + index] + received[count + index].astype(F32)).astype(LOW)
    for index in range(count):
        keep_o[index] = keep[index] + received[index].astype(F32)


def merge_last_weights(info, keep, received, down_o, up_o):
    down_o[...] = (keep[0, 0] + received[0, 0].astype(F32)).T
    up_o[...] = keep[0, 1] + received[0, 1].astype(F32)


def merged_vectors(keep, received, index, block):
    high = received[index, block : block + VECTOR_ROWS].astype(F32)
    low = received[index, block + VECTOR_ROWS :].astype(F32)
    return keep[index, block : block + VECTOR_ROWS] + high + low


def merge_attn(info, keep, received, send_o, keep_o):
    count = keep_o.shape[0]
    block = keep_o.shape[1] - PAIR_ROWS
    for index in range(count):
        at = count + index
        send_o[index, :block] = (keep[at, :block] + received[at, :block].astype(F32)).astype(LOW)
        send_o[index, block:] = split_pair(merged_vectors(keep, received, at, block))
    for index in range(count):
        keep_o[index, :block] = keep[index, :block] + received[index, :block].astype(F32)
        vectors = merged_vectors(keep, received, index, block)
        keep_o[index, block : block + VECTOR_ROWS] = vectors
        keep_o[index, block + VECTOR_ROWS :] = jnp.zeros_like(vectors)


def merge_last_attn(info, keep, received, qkv_o, out_o, vectors_o):
    block, width = qkv_o.shape[1], qkv_o.shape[2]
    total = keep[0, :block] + received[0, :block].astype(F32)
    for part in range(3):
        qkv_o[part] = total[:, part * width : (part + 1) * width]
    out_o[...] = total[:, 3 * width :].T
    vectors_o[...] = merged_vectors(keep, received, 0, block)


CORE_PAIRS = [(i, i ^ 1) for i in range(4)]
CHIP_PAIRS = [(i, i ^ 2) for i in range(4)]


def to_core(block):
    return lax.ppermute(block, "tensor", CORE_PAIRS)


def to_chip(block):
    return lax.ppermute(block, "tensor", CHIP_PAIRS)


def dp_orders(dp_size):
    bits = list(range(dp_size.bit_length() - 1))
    swapped = bits[:2][::-1] + bits[2:]
    return (bits, swapped)


def to_dp(block, step, dp_size, tensor_size):
    orders = dp_orders(dp_size)
    pairs = []
    for d in range(dp_size):
        for t in range(tensor_size):
            partner = d ^ (1 << orders[t % CORES][step])
            pairs.append((d * tensor_size + t, partner * tensor_size + t))
    return lax.ppermute(block, ("dp", "tensor"), pairs)


def block_order(dp_size, core):
    tables = []
    for order in dp_orders(dp_size):
        table = []
        for index in range(dp_size):
            pattern = 0
            for step, bit in enumerate(order):
                if (index >> (len(order) - 1 - step)) & 1:
                    pattern |= 1 << bit
            table.append(pattern)
        tables.append(table)
    relative = jnp.asarray(tables, jnp.int32)[core]
    return relative ^ lax.axis_index("dp").astype(jnp.int32)


def in_order(own, other, core):
    return jnp.where(
        core == 0, jnp.concatenate([own, other], 0), jnp.concatenate([other, own], 0)
    )


def on_device(
    tokens,
    w_qkv,
    bias_qv,
    w_out,
    bias_out,
    gain_one,
    shift_one,
    w_up,
    bias_up,
    w_down,
    bias_down,
    gain_two,
    shift_two,
    cotangent,
    lengths,
):
    rows, model = tokens.shape
    half = rows // 2
    width = w_qkv.shape[2]
    units = w_up.shape[1]
    dp_size = lax.axis_size("dp")
    tensor_size = lax.axis_size("tensor")
    steps = dp_size.bit_length() - 1
    block = model // dp_size
    core = (lax.axis_index("tensor") % CORES).astype(jnp.int32)
    info = jnp.stack([core, lengths[0].astype(jnp.int32)])
    order = block_order(dp_size, core)
    row = lambda vector: vector.reshape(1, -1)

    up_other, down_other = to_core(w_up), to_core(w_down)
    bias_up_other = to_core(row(bias_up))

    heads_shape = (rows, width)
    query, keys, values, attended, attn_send, attn_keep = call(
        attn_forward,
        [(heads_shape, LOW)] * 4 + [((half, model), LOW), ((half, model), F32)],
        info, tokens, w_qkv, bias_qv, w_out,
        flops=2 * rows * (4 * model + 2 * rows) * width,
    )
    attn_own = (attn_keep + to_core(attn_send).astype(F32)).astype(LOW)
    attn_received = to_chip(attn_own)

    fwd_own, act_own, slope_own, slope_other, normed_one, inverse_one, mlp_own = call(
        mlp_forward,
        [
            ((half, model + units), LOW), ((half, units), LOW), ((half, units), F32),
            ((half, units), F32), ((half, model), F32), ((half, 1), F32), ((half, model), LOW),
        ],
        info, tokens, attn_own, attn_received, row(bias_out), row(gain_one), row(shift_one),
        w_up, up_other, row(bias_up), bias_up_other, w_down, down_other,
        flops=8 * half * model * units,
    )
    mlp_received = to_chip(mlp_own)
    fwd_other = to_core(fwd_own)

    out_half, resid_two, bwd_own, pre_own, back_own, sums_two = call(
        mlp_backward,
        [
            ((half, model), LOW), ((half, model), F32), ((half, model + units), LOW),
            ((half, units), LOW), ((half, model), LOW), ((2, model), F32),
        ],
        info, cotangent, mlp_own, mlp_received, normed_one, row(gain_one), row(shift_one),
        row(bias_down), row(gain_two), row(shift_two), slope_own, slope_other,
        w_up, up_other, w_down, down_other,
        flops=8 * half * model * units,
    )
    back_received = to_chip(back_own)
    bwd_other = to_core(bwd_own)
    output_low = in_order(out_half, to_core(out_half), core)

    count = dp_size // 2
    mlp_send, mlp_keep, sums_mlp = call(
        mlp_weights,
        [
            ((count, 2, block, units), LOW), ((count, 2, block, units), F32), ((2, units), F32),
        ],
        order, fwd_own, fwd_other, act_own, bwd_own, bwd_other, pre_own,
        scratch=[pltpu.VMEM((dp_size, block, units), F32)] * 2,
        flops=4 * rows * model * units,
    )
    mlp_got = to_dp(mlp_send, 0, dp_size, tensor_size)

    resid_one, grad_attn, sums_one = call(
        norm_one_back,
        [((half, model), F32), ((half, model), LOW), ((3, model), F32)],
        info, resid_two, back_own, back_received, normed_one, inverse_one, row(gain_one),
    )
    grad_attn_other = to_core(grad_attn)
    half_sums = jnp.concatenate([sums_two, sums_one], 0)
    half_sums = half_sums + to_core(half_sums)
    vectors = jnp.concatenate(
        [half_sums, sums_mlp, jnp.zeros((VECTOR_ROWS - 7, model), F32)], 0
    )

    grad_q, grad_k, grad_v, attn_w_send, attn_w_keep = call(
        attn_backward,
        [(heads_shape, LOW)] * 3
        + [
            ((count, block + PAIR_ROWS, model), LOW),
            ((count, block + PAIR_ROWS, model), F32),
        ],
        jnp.concatenate([info, order]),
        grad_attn, grad_attn_other, w_out, query, keys, values, attended, tokens, vectors,
        scratch=[
            pltpu.VMEM((rows, model), LOW),
            pltpu.VMEM((dp_size, block, model), F32),
            pltpu.VMEM((VECTOR_ROWS, model), F32),
        ],
        flops=2 * rows * (5 * model + 5 * rows) * width,
    )
    attn_got = to_dp(attn_w_send, 0, dp_size, tensor_size)
    token_send, token_keep = call(
        token_back,
        [((half, model), LOW), ((half, model), F32)],
        info, grad_q, grad_k, grad_v, w_qkv,
        flops=6 * rows * model * width,
    )
    token_own = (token_keep + to_core(token_send).astype(F32)).astype(LOW)
    token_received = to_chip(token_own)

    for step in range(1, steps):
        kept = dp_size >> (step + 1)
        mlp_send, mlp_keep = call(
            merge_weights,
            [((kept, 2, block, units), LOW), ((kept, 2, block, units), F32)],
            info, mlp_keep, mlp_got,
        )
        mlp_got = to_dp(mlp_send, step, dp_size, tensor_size)
    sum_w_down, sum_w_up = call(
        merge_last_weights, [((units, block), F32), ((block, units), F32)], info, mlp_keep, mlp_got
    )
    for step in range(1, steps):
        kept = dp_size >> (step + 1)
        attn_w_send, attn_w_keep = call(
            merge_attn,
            [((kept, block + PAIR_ROWS, model), LOW), ((kept, block + PAIR_ROWS, model), F32)],
            info, attn_w_keep, attn_got,
        )
        attn_got = to_dp(attn_w_send, step, dp_size, tensor_size)

    token_half = (
        resid_one + (token_own.astype(F32) + token_received.astype(F32))
    ).astype(LOW)
    token_total = in_order(token_half, to_core(token_half), core)

    sum_w_qkv, sum_w_out, sum_vectors = call(
        merge_last_attn,
        [((3, block, width), F32), ((width, block), F32), ((VECTOR_ROWS, model), F32)],
        info, attn_w_keep, attn_got,
    )
    me = lax.axis_index("dp")
    mine = lax.dynamic_slice_in_dim(sum_vectors[:7], me * block, block, 1)
    small = width // dp_size
    pair = sum_vectors[7, : 4 * width].reshape(2, 2 * width)[:, :width]
    sum_bias_qv = lax.dynamic_slice_in_dim(pair, me * small, small, 1)
    return (
        output_low,
        token_total,
        sum_w_qkv,
        sum_bias_qv,
        sum_w_out,
        mine[4],
        mine[2],
        mine[3],
        sum_w_up,
        mine[6],
        sum_w_down,
        mine[5],
        mine[0],
        mine[1],
    )


def solution(mesh):
    placed = (
        P("dp", None),
        P(None, None, "tensor"),
        P(None, "tensor"),
        P("tensor", None),
        P(),
        P(),
        P(),
        P(None, "tensor"),
        P("tensor"),
        P("tensor", None),
        P(),
        P(),
        P(),
        P("dp", None),
        P("dp"),
    )
    return jax.shard_map(
        on_device,
        mesh=mesh,
        in_specs=placed,
        out_specs=(
            P("dp", None),
            P("dp", None),
            P(None, "dp", "tensor"),
            P(None, ("tensor", "dp")),
            P("tensor", "dp"),
            P("dp"),
            P("dp"),
            P("dp"),
            P("dp", "tensor"),
            P(("tensor", "dp")),
            P("tensor", "dp"),
            P("dp"),
            P("dp"),
            P("dp"),
        ),
        check_vma=False,
    )
```

```python
from functools import partial

import jax
import jax.numpy as jnp
import numpy as np
from jax import lax
from jax.experimental import pallas as pl
from jax.experimental.pallas import tpu as pltpu
from jax.sharding import PartitionSpec as P

HEAD_DIM = 64
NORM_EPSILON = 1e-05
CORES = 2
CHUNKS = 1
F32 = jnp.float32
LOW = jnp.bfloat16
MIB = 1 << 20
COST_FLOPS = 0
COST_BYTES = 0

VECTOR_ROWS = 8
PAIR_ROWS = 2 * VECTOR_ROWS


def nn(left, right):
    return lax.dot_general(left, right, (((1,), (0,)), ((), ())), preferred_element_type=F32)


def nt(left, right):
    return lax.dot_general(left, right, (((1,), (1,)), ((), ())), preferred_element_type=F32)


def tn(left, right):
    return lax.dot_general(left, right, (((0,), (0,)), ((), ())), preferred_element_type=F32)


def normalize(resid):
    center = resid - jnp.mean(resid, -1, keepdims=True)
    inverse = lax.rsqrt(jnp.mean(center * center, -1, keepdims=True) + NORM_EPSILON)
    return center * inverse, inverse


def norm_back(grad_norm, normed, inverse):
    mean_grad = jnp.mean(grad_norm, -1, keepdims=True)
    mean_proj = jnp.mean(grad_norm * normed, -1, keepdims=True)
    return inverse * (grad_norm - mean_grad - normed * mean_proj)


class State:
    def __init__(self):
        self.arrays = {}

    def drop(self, *names):
        for name in names:
            del self.arrays[name]

    def call(self, kernel, outs, *inputs, mib=16, scratch=(), loose=False):
        names = list(self.arrays)
        direct = [item for item in inputs if not isinstance(item, str)]
        read = {item for item in inputs if isinstance(item, str)}
        vmem = pl.BlockSpec(memory_space=pltpu.VMEM)
        anywhere = pl.BlockSpec(memory_space=pl.ANY)
        scalar = pl.BlockSpec(memory_space=pltpu.SMEM)
        held_shapes = [
            jax.ShapeDtypeStruct(self.arrays[name].shape, self.arrays[name].dtype) for name in names
        ]
        out_shapes = [jax.ShapeDtypeStruct(out[0], out[1]) for out in outs]

        def body(*refs):
            refs = list(refs)
            arrays, refs = refs[: len(direct)], refs[len(direct) :]
            held, refs = dict(zip(names, refs)), refs[len(names) :]
            results, refs = refs[: len(outs)], refs[len(outs) :]
            rest = refs[len(names) :]
            ins = [held[item] if isinstance(item, str) else arrays.pop(0) for item in inputs]
            kernel(*ins, *results, *rest)

        results = pl.pallas_call(
            body,
            name=getattr(kernel, "__name__", None) or kernel.func.__name__,
            out_shape=tuple(out_shapes + held_shapes),
            in_specs=[
                anywhere if loose else scalar if array.dtype == jnp.int32 else vmem
                for array in direct
            ]
            + [vmem if name in read else anywhere for name in names],
            out_specs=tuple([vmem] * len(outs) + [anywhere] * len(names)),
            input_output_aliases={
                len(direct) + index: len(outs) + index for index in range(len(names))
            },
            scratch_shapes=list(scratch),
            compiler_params=pltpu.CompilerParams(vmem_limit_bytes=mib * MIB),
            cost_estimate=pl.CostEstimate(flops=COST_FLOPS, bytes_accessed=COST_BYTES, transcendentals=0),
        )(*direct, *self.arrays.values())
        for name, array in zip(names, results[len(outs) :]):
            self.arrays[name] = array
        returned = []
        for out, array in zip(outs, results):
            if len(out) == 3:
                self.arrays[out[2]] = array
            else:
                returned.append(array)
        return returned


def my_core():
    return lax.rem(lax.axis_index("tensor"), CORES)


BIAS_OUT, GAIN_ONE, SHIFT_ONE, BIAS_UP, BIAS_DOWN, GAIN_TWO, SHIFT_TWO = range(7)


def row(packed, index):
    return packed[index : index + 1, :]


def attn_forward(lengths, tokens, w_qkv, bias_qv, w_out, saved_o, send_o, keep_o):
    core, length = my_core(), lengths[0]
    rows, width = saved_o.shape[1:]
    half = rows // 2
    x = tokens[...]
    query = (nt(x, w_qkv[0]) + bias_qv[0:1, :]).astype(LOW)
    keys = nt(x, w_qkv[1]).astype(LOW)
    values = (nt(x, w_qkv[2]) + bias_qv[1:2, :]).astype(LOW)
    saved_o[0] = query
    saved_o[1] = keys
    saved_o[2] = values
    head_of = lax.broadcasted_iota(jnp.int32, (rows, width), 1) // HEAD_DIM
    key_valid = lax.broadcasted_iota(jnp.int32, (rows, rows), 1) < length
    scaled = query.astype(F32) * HEAD_DIM ** -0.5
    value_full = values.astype(F32)
    total = jnp.zeros((rows, width), F32)
    for head in range(width // HEAD_DIM):
        here = head_of == head
        scores = nt(jnp.where(here, scaled, 0.0).astype(LOW), keys)
        scores = jnp.where(key_valid, scores, -1e30)
        expo = jnp.exp(scores - jnp.max(scores, -1, keepdims=True))
        probs = (expo * (1.0 / jnp.sum(expo, -1, keepdims=True))).astype(LOW)
        total = total + nn(probs, jnp.where(here, value_full, 0.0).astype(LOW))
    saved_o[3] = total.astype(LOW)
    other_start = pl.multiple_of((1 - core) * half, half)
    own_start = pl.multiple_of(core * half, half)
    send_o[...] = nn(saved_o[3, pl.ds(other_start, half), :], w_out[...]).astype(LOW)
    keep_o[...] = nn(saved_o[3, pl.ds(own_start, half), :], w_out[...])


def add_chunks(kept, received, *outs):
    rows = outs[0].shape[0]
    count = len(outs) // 2
    for index in range(count):
        picked = slice(index * rows, (index + 1) * rows)
        total = (kept[picked, :] + received[picked, :].astype(F32)).astype(LOW)
        outs[index][...] = total
        outs[count + index][...] = total


def hold(*refs):
    sems = refs[-1]
    count = (len(refs) - 1) // 2
    copies = [
        pltpu.make_async_copy(refs[index], refs[count + index], sems.at[index])
        for index in range(count)
    ]
    for copy in copies:
        copy.start()
    for copy in copies:
        copy.wait()


def add_rows(kept, received, out):
    out[...] = (kept[...] + received[...].astype(F32)).astype(LOW)


def final_rows(*refs):
    resids, (own, received, out) = refs[:-3], refs[-3:]
    rows = resids[0].shape[0]
    for index, resid in enumerate(resids):
        picked = slice(index * rows, (index + 1) * rows)
        out[picked, :] = (
            resid[...] + (own[picked, :].astype(F32) + received[picked, :].astype(F32))
        ).astype(LOW)


def place_rows(*refs):
    out = refs[-1]
    pieces = refs[:-1]
    count = len(pieces) // 2
    rows = pieces[0].shape[0]
    half = count * rows
    core = my_core()
    for index in range(count):
        own_start = pl.multiple_of(core * half + index * rows, rows)
        other_start = pl.multiple_of((1 - core) * half + index * rows, rows)
        out[pl.ds(own_start, rows), :] = pieces[index][...]
        out[pl.ds(other_start, rows), :] = pieces[count + index][...]


def mlp_forward(
    index, received, tokens, own, packed, packed_other, up_own, up_other, down_own, down_other,
    part_o, pass_o, kept_o, hidden_o, act_o, slopes_o, normed_o, inverse_o,
):
    rows, width = part_o.shape
    units = up_own.shape[1]
    start = pl.multiple_of((my_core() * CHUNKS + index) * rows, rows)
    resid = tokens[pl.ds(start, rows), :].astype(F32) + row(packed, BIAS_OUT)
    resid = resid + (own[...].astype(F32) + received[...].astype(F32))
    normed, inverse = normalize(resid)
    normed_o[...] = normed
    inverse_o[...] = inverse
    hidden_low = (normed * row(packed, GAIN_ONE) + row(packed, SHIFT_ONE)).astype(LOW)
    pass_o[:, :width] = hidden_low
    hidden_o[...] = hidden_low

    def units_of(up, vectors, side):
        pre = nn(hidden_low, up[...]) + row(vectors, BIAS_UP)
        cdf = 0.5 * (1.0 + lax.erf(pre * 0.7071067811865476))
        slopes_o[side] = cdf + pre * (jnp.exp(-0.5 * pre * pre) * 0.3989422804014327)
        return (pre * cdf).astype(LOW)

    act_own = units_of(up_own, packed, 0)
    act_o[...] = act_own
    act_other = units_of(up_other, packed_other, 1)
    pass_o[:, width : width + units] = act_other
    part = (nn(act_own, down_own[...]) + nn(act_other, down_other[...])).astype(LOW)
    part_o[...] = part
    kept_o[...] = part


def mlp_backward(
    index, lengths, received, normed_one, own, packed, cotangent, down_own, down_other, slopes,
    up_own, up_other,
    part_o, pass_o, kept_o, grad_o, pre_o, resid_o, out_o, sums_o,
):
    rows, width = part_o.shape
    units = up_own.shape[1]
    length = lengths[0]
    start = pl.multiple_of((my_core() * CHUNKS + index) * rows, rows)
    hidden = normed_one[...] * row(packed, GAIN_ONE) + row(packed, SHIFT_ONE)
    branch = own[...].astype(F32) + received[...].astype(F32) + row(packed, BIAS_DOWN)
    normed, inverse = normalize(hidden + branch)
    valid = lax.broadcasted_iota(jnp.int32, (rows, width), 0) + start < length
    out = jnp.where(valid, normed * row(packed, GAIN_TWO) + row(packed, SHIFT_TWO), 0.0)
    out_o[...] = out.astype(LOW)
    grad_out = jnp.where(valid, cotangent[pl.ds(start, rows), :].astype(F32), 0.0)
    sums_o[0:1, :] = jnp.sum(grad_out * normed, 0, keepdims=True)
    sums_o[1:2, :] = jnp.sum(grad_out, 0, keepdims=True)
    grad_resid = norm_back(grad_out * row(packed, GAIN_TWO), normed, inverse)
    resid_o[...] = grad_resid
    grad_mlp = grad_resid.astype(LOW)
    pass_o[:, :width] = grad_mlp
    grad_o[...] = grad_mlp
    pre_own = (nt(grad_mlp, down_own[...]) * slopes[0]).astype(LOW)
    pre_o[...] = pre_own
    pre_other = (nt(grad_mlp, down_other[...]) * slopes[1]).astype(LOW)
    pass_o[:, width : width + units] = pre_other
    part = (nt(pre_own, up_own[...]) + nt(pre_other, up_other[...])).astype(LOW)
    part_o[...] = part
    kept_o[...] = part


def spread(blocks, grad):
    block = blocks.shape[1]
    for index in range(blocks.shape[0]):
        blocks[index] = grad[index * block : (index + 1) * block, :]


def block_of(dp_size, slot):
    patterns = []
    for order in dp_orders(dp_size):
        pattern = 0
        for step, bit in enumerate(order):
            if (slot >> (len(order) - 1 - step)) & 1:
                pattern |= 1 << bit
        patterns.append(pattern)
    return jnp.where(my_core() == 0, patterns[0], patterns[1]) ^ lax.axis_index("dp")


def weight_grad(take, *refs):
    pieces, (send_o, keep_o, sum_o, left, right, blocks) = refs[:-6], refs[-6:]
    model = left.shape[1]
    rows = pieces[0].shape[0]
    half = len(pieces) // 2
    for target, sources, columns in (
        (left, pieces[:half], take[:half]), (right, pieces[half:], take[half:])
    ):
        for index, (source, column) in enumerate(zip(sources, columns)):
            picked = slice(column * model, (column + 1) * model)
            target[index * rows : (index + 1) * rows, :] = source[:, picked]
    spread(blocks, tn(left[...], right[...]))
    summed = left if sum_o.shape[0] == 1 else right
    sum_o[0:1, :] = jnp.sum(summed[...].astype(F32), 0, keepdims=True)
    count = keep_o.shape[0]
    for index in range(count):
        send_o[index] = blocks[block_of(2 * count, index + count)].astype(LOW)
    for index in range(count):
        keep_o[index] = blocks[block_of(2 * count, index)]


def norm_one_back(
    received, own, resid_two, normed, inverse, packed, sums_two, sums_before,
    low_o, sums_o, resid_o,
):
    grad_hidden = resid_two[...] + (own[...].astype(F32) + received[...].astype(F32))
    xhat = normed[...]
    grad_resid = norm_back(grad_hidden * row(packed, GAIN_ONE), xhat, inverse[...])
    resid_o[...] = grad_resid
    low = grad_resid.astype(LOW)
    low_o[...] = low
    sums_o[...] = sums_before[...]
    sums_o[0:2, :] += sums_two[...]
    sums_o[2:3, :] += jnp.sum(grad_hidden * xhat, 0, keepdims=True)
    sums_o[3:4, :] += jnp.sum(grad_hidden, 0, keepdims=True)
    sums_o[4:5, :] += jnp.sum(low.astype(F32), 0, keepdims=True)


def split_pair(vectors):
    high = vectors.astype(LOW)
    return jnp.concatenate([high.astype(F32), vectors - high.astype(F32)], 0).astype(LOW)


def attn_backward(
    lengths, *refs,
):
    pieces, refs = refs[: 2 * CHUNKS], refs[2 * CHUNKS :]
    sums_own, sums_other, w_out, saved, tokens, sum_down, sum_up = refs[:7]
    send_o, keep_o, gq_o, gk_o, gv_o, grad_attn, blocks, sums = refs[7:]
    length = lengths[0]
    rows, width = saved.shape[1:]
    place_rows(*pieces, grad_attn)
    grad_rows = grad_attn[...]
    grad_att = nt(grad_rows, w_out[...]).astype(LOW)
    scale = HEAD_DIM ** -0.5
    head_of = lax.broadcasted_iota(jnp.int32, (rows, width), 1) // HEAD_DIM
    key_valid = lax.broadcasted_iota(jnp.int32, (rows, rows), 0) < length
    query, keys, values = saved[0], saved[1], saved[2]
    scaled = query.astype(F32) * scale
    scaled_keys = keys.astype(F32) * scale
    grad_att_full = grad_att.astype(F32)
    grad_q = jnp.zeros((rows, width), F32)
    grad_k = jnp.zeros((rows, width), F32)
    grad_v = jnp.zeros((rows, width), F32)
    for head in range(width // HEAD_DIM):
        here = head_of == head
        scaled_here = jnp.where(here, scaled, 0.0).astype(LOW)
        scores = jnp.where(key_valid, nt(keys, scaled_here), -1e30)
        expo = jnp.exp(scores - jnp.max(scores, 0, keepdims=True))
        probs = expo * (1.0 / jnp.sum(expo, 0, keepdims=True))
        grad_here = jnp.where(here, grad_att_full, 0.0).astype(LOW)
        grad_probs = nt(values, grad_here)
        grad_v = grad_v + nn(probs.astype(LOW), grad_here)
        inner = jnp.sum(probs * grad_probs, 0, keepdims=True)
        grad_scores = (probs * (grad_probs - inner)).astype(LOW)
        grad_k = grad_k + nn(grad_scores, scaled_here)
        grad_q = grad_q + tn(grad_scores, jnp.where(here, scaled_keys, 0.0).astype(LOW))
    low_q, low_k, low_v = grad_q.astype(LOW), grad_k.astype(LOW), grad_v.astype(LOW)
    gq_o[...] = low_q
    gk_o[...] = low_k
    gv_o[...] = low_v
    x = tokens[...]
    weight = jnp.concatenate(
        [tn(x, low_q), tn(x, low_k), tn(x, low_v), tn(grad_rows, saved[3])], 1
    )
    spread(blocks, weight)
    sums[...] = sums_own[...] + sums_other[...]
    sums[5:6, :] = sum_down[0:1, :]
    sums[6:7, :] = sum_up[0:1, :]
    last = VECTOR_ROWS - 1
    sums[last : last + 1, :width] = jnp.sum(low_q.astype(F32), 0, keepdims=True)
    sums[last : last + 1, 2 * width : 3 * width] = jnp.sum(low_v.astype(F32), 0, keepdims=True)
    vector_sums = sums[...]
    block = blocks.shape[1]
    pair = split_pair(vector_sums)
    count = keep_o.shape[0]
    for index in range(count):
        send_o[index, :block] = blocks[block_of(2 * count, index + count)].astype(LOW)
        send_o[index, block:] = pair
    for index in range(count):
        keep_o[index, :block] = blocks[block_of(2 * count, index)]
        keep_o[index, block : block + VECTOR_ROWS] = vector_sums
        keep_o[index, block + VECTOR_ROWS :] = jnp.zeros_like(vector_sums)


def token_back(gq, gk, gv, w_qkv, send_o, keep_o):
    half = send_o.shape[0]
    core = my_core()

    def rows_from(start):
        picked = pl.ds(pl.multiple_of(start, half), half)
        return (
            nn(gq[picked, :], w_qkv[0]) + nn(gk[picked, :], w_qkv[1]) + nn(gv[picked, :], w_qkv[2])
        )

    send_o[...] = rows_from((1 - core) * half).astype(LOW)
    keep_o[...] = rows_from(core * half)


def merge_weights(keep, received, send_o, keep_o):
    count = keep_o.shape[0]
    for index in range(count):
        send_o[index] = (keep[count + index] + received[count + index].astype(F32)).astype(LOW)
    for index in range(count):
        keep_o[index] = keep[index] + received[index].astype(F32)


def merge_last_weights(keep, received, out):
    out[...] = keep[0] + received[0].astype(F32)


def merged_vectors(keep, received, index, block):
    high = received[index, block : block + VECTOR_ROWS].astype(F32)
    low = received[index, block + VECTOR_ROWS :].astype(F32)
    return keep[index, block : block + VECTOR_ROWS] + high + low


def merge_attn(keep, received, send_o, keep_o):
    count = keep_o.shape[0]
    block = keep_o.shape[1] - PAIR_ROWS
    for index in range(count):
        at = count + index
        send_o[index, :block] = (keep[at, :block] + received[at, :block].astype(F32)).astype(LOW)
        send_o[index, block:] = split_pair(merged_vectors(keep, received, at, block))
    for index in range(count):
        keep_o[index, :block] = keep[index, :block] + received[index, :block].astype(F32)
        vectors = merged_vectors(keep, received, index, block)
        keep_o[index, block : block + VECTOR_ROWS] = vectors
        keep_o[index, block + VECTOR_ROWS :] = jnp.zeros_like(vectors)


def merge_last_attn(keep, received, qkv_o, out_o, vectors_o, pair_o):
    block, width = qkv_o.shape[1], qkv_o.shape[2]
    total = keep[0, :block] + received[0, :block].astype(F32)
    for part in range(3):
        qkv_o[part] = total[:, part * width : (part + 1) * width]
    out_o[...] = total[:, 3 * width :].T
    vectors = merged_vectors(keep, received, 0, block)
    model = vectors.shape[1]
    me = lax.axis_index("dp")
    vectors_o[...] = pltpu.roll(vectors, lax.rem(model - me * block, model), 1)[:, :block]
    small = pair_o.shape[1]
    turned = pltpu.roll(vectors, lax.rem(model - me * small, model), 1)
    last = VECTOR_ROWS - 1
    pair_o[0:1, :] = turned[last : last + 1, :small]
    pair_o[1:2, :] = turned[last : last + 1, 2 * width : 2 * width + small]


CORE_PAIRS = [(i, i ^ 1) for i in range(4)]
CHIP_PAIRS = [(i, i ^ 2) for i in range(4)]


def to_core(block):
    return lax.ppermute(block, "tensor", CORE_PAIRS)


def to_chip(block):
    return lax.ppermute(block, "tensor", CHIP_PAIRS)


def dp_orders(dp_size):
    bits = list(range(dp_size.bit_length() - 1))
    swapped = bits[:2][::-1] + bits[2:]
    return (bits, swapped)


def to_dp(block, step, dp_size, tensor_size):
    orders = dp_orders(dp_size)
    pairs = []
    for d in range(dp_size):
        for t in range(tensor_size):
            partner = d ^ (1 << orders[t % CORES][step])
            pairs.append((d * tensor_size + t, partner * tensor_size + t))
    return lax.ppermute(block, ("dp", "tensor"), pairs)


def on_device(
    tokens,
    w_qkv,
    bias_qv,
    w_out,
    bias_out,
    gain_one,
    shift_one,
    w_up,
    bias_up,
    w_down,
    bias_down,
    gain_two,
    shift_two,
    cotangent,
    lengths,
):
    rows, model = tokens.shape
    half = rows // 2
    chunk = half // CHUNKS
    width = w_qkv.shape[2]
    units = w_up.shape[1]
    dp_size = lax.axis_size("dp")
    tensor_size = lax.axis_size("tensor")
    steps = dp_size.bit_length() - 1
    block = model // dp_size
    count = dp_size // 2
    chunks = range(CHUNKS)
    packed = jnp.stack(
        [bias_out, gain_one, shift_one, bias_up, bias_down, gain_two, shift_two, shift_two]
    )
    w_turned = w_qkv.transpose(0, 2, 1)
    up_other, down_other = to_core(w_up), to_core(w_down)
    packed_other = to_core(packed)

    state = State()
    attn_send, attn_keep = state.call(
        attn_forward,
        [((4, rows, width), LOW, "saved"), ((half, model), LOW), ((half, model), F32)],
        lengths, tokens, w_turned, bias_qv, w_out,
        mib=20,
    )
    attn_parts = state.call(
        add_chunks,
        [((chunk, model), LOW)] * CHUNKS + [((chunk, model), LOW, f"attn{c}") for c in chunks],
        attn_keep, to_core(attn_send),
    )
    received = [to_chip(part) for part in attn_parts]
    held = {
        "tokens": tokens, "w_out": w_out, "w_qkv": w_turned, "cotangent": cotangent,
        "up_own": w_up, "up_other": up_other, "down_own": w_down, "down_other": down_other,
        "packed": packed, "packed_other": packed_other,
    }
    state.call(
        hold,
        [(array.shape, array.dtype, name) for name, array in held.items()],
        *held.values(),
        scratch=[pltpu.SemaphoreType.DMA((len(held),))], loose=True,
    )

    passed, fwd_other = [], []
    for c in chunks:
        part, fwd = state.call(
            partial(mlp_forward, c),
            [
                ((chunk, model), LOW), ((chunk, model + units), LOW),
                ((chunk, model), LOW, f"mlp{c}"), ((chunk, model), LOW, f"hid{c}"),
                ((chunk, units), LOW, f"act{c}"), ((2, chunk, units), F32, f"slopes{c}"),
                ((chunk, model), F32, f"normed{c}"), ((chunk, 1), F32, f"inverse{c}"),
            ],
            received[c], "tokens", f"attn{c}", "packed", "packed_other",
            "up_own", "up_other", "down_own", "down_other",
        )
        state.drop(f"attn{c}")
        passed.append(to_chip(part))
        fwd_other.append(to_core(fwd))
    received = passed

    passed, bwd_other, out_half = [], [], []
    for c in chunks:
        part, bwd, out_c = state.call(
            partial(mlp_backward, c),
            [
                ((chunk, model), LOW), ((chunk, model + units), LOW),
                ((chunk, model), LOW, f"back{c}"), ((chunk, model), LOW, f"grad{c}"),
                ((chunk, units), LOW, f"pre{c}"), ((chunk, model), F32, f"resid{c}"),
                ((chunk, model), LOW), ((2, model), F32, f"sums{c}"),
            ],
            lengths, received[c], f"normed{c}", f"mlp{c}", "packed", "cotangent",
            "down_own", "down_other", f"slopes{c}", "up_own", "up_other",
        )
        state.drop(f"mlp{c}", f"slopes{c}")
        passed.append(to_chip(part))
        bwd_other.append(to_core(bwd))
        out_half.append(out_c)
    state.drop("cotangent", "up_own", "up_other", "down_own", "down_other")
    received = passed
    out_other = [to_core(part) for part in out_half]

    scratch = [pltpu.VMEM((rows, model), LOW)] * 2 + [pltpu.VMEM((dp_size, block, units), F32)]
    grad_shape = (count, block, units)
    pairs = [0, 0] * CHUNKS

    def both(own, other):
        return [piece for c in chunks for piece in (f"{own}{c}", other[c])]

    (down_send,) = state.call(
        partial(weight_grad, pairs + [0, 1] * CHUNKS),
        [(grad_shape, LOW), (grad_shape, F32, "down_keep"), ((1, model), F32, "sum_down")],
        *both("grad", bwd_other),
        *[piece for c in chunks for piece in (f"act{c}", fwd_other[c])],
        scratch=scratch, mib=20,
    )
    down_got = to_dp(down_send, 0, dp_size, tensor_size)
    (up_send,) = state.call(
        partial(weight_grad, pairs + [0, 1] * CHUNKS),
        [(grad_shape, LOW), (grad_shape, F32, "up_keep"), ((2, units), F32, "sum_up")],
        *both("hid", fwd_other),
        *[piece for c in chunks for piece in (f"pre{c}", bwd_other[c])],
        scratch=scratch, mib=20,
    )
    up_got = to_dp(up_send, 0, dp_size, tensor_size)
    for c in chunks:
        state.drop(f"hid{c}", f"act{c}", f"grad{c}", f"pre{c}")
    for c in chunks:
        state.arrays[f"out_half{c}"] = out_half[c]
        state.arrays[f"out_other{c}"] = out_other[c]

    sums = jnp.zeros((VECTOR_ROWS, model), F32)
    grad_attn, grad_attn_other = [], []
    for c in chunks:
        low, sums = state.call(
            norm_one_back,
            [((chunk, model), LOW), ((VECTOR_ROWS, model), F32), ((chunk, model), F32, f"last{c}")],
            received[c], f"back{c}", f"resid{c}", f"normed{c}", f"inverse{c}", "packed", f"sums{c}",
            sums,
        )
        state.drop(f"back{c}", f"resid{c}", f"normed{c}", f"inverse{c}", f"sums{c}")
        grad_attn.append(low)
        grad_attn_other.append(to_core(low))
    sums_other = to_core(sums)

    def merge(name, got, step):
        kept = dp_size >> (step + 1)
        shape = state.arrays[name].shape[1:]
        kernel = merge_attn if name == "attn_keep" else merge_weights
        (send,) = state.call(
            kernel, [((kept,) + shape, LOW), ((kept,) + shape, F32, "next")], name, got
        )
        state.drop(name)
        state.arrays[name] = state.arrays.pop("next")
        return to_dp(send, step, dp_size, tensor_size)

    if steps > 1:
        down_got = merge("down_keep", down_got, 1)

    attn_w_send, grad_q, grad_k, grad_v = state.call(
        attn_backward,
        [
            ((count, block + PAIR_ROWS, model), LOW),
            ((count, block + PAIR_ROWS, model), F32, "attn_keep"),
        ]
        + [((rows, width), LOW)] * 3,
        lengths, *grad_attn, *grad_attn_other, sums, sums_other,
        "w_out", "saved", "tokens", "sum_down", "sum_up",
        scratch=[
            pltpu.VMEM((rows, model), LOW),
            pltpu.VMEM((dp_size, block, model), F32),
            pltpu.VMEM((VECTOR_ROWS, model), F32),
        ],
        mib=24,
    )
    state.drop("saved", "sum_down", "sum_up", "w_out", "tokens", "packed", "packed_other")
    attn_got = to_dp(attn_w_send, 0, dp_size, tensor_size)
    if steps > 1:
        up_got = merge("up_keep", up_got, 1)
    token_send, token_keep = state.call(
        token_back,
        [((half, model), LOW), ((half, model), F32)],
        grad_q, grad_k, grad_v, "w_qkv",
    )
    state.drop("w_qkv")
    (token_own,) = state.call(add_rows, [((half, model), LOW)], token_keep, to_core(token_send))
    token_received = to_chip(token_own)
    for step in range(2, steps):
        down_got = merge("down_keep", down_got, step)
    if steps > 1:
        attn_got = merge("attn_keep", attn_got, 1)
    for step in range(2, steps):
        up_got = merge("up_keep", up_got, step)
    (token_half,) = state.call(
        final_rows, [((half, model), LOW)], *[f"last{c}" for c in chunks],
        token_own, token_received,
    )
    state.drop(*[f"last{c}" for c in chunks])
    for step in range(2, steps):
        attn_got = merge("attn_keep", attn_got, step)
    (output_low,) = state.call(
        place_rows, [((rows, model), LOW)],
        *[f"out_half{c}" for c in chunks], *[f"out_other{c}" for c in chunks],
    )
    state.drop(*[f"out_half{c}" for c in chunks], *[f"out_other{c}" for c in chunks])
    (token_total,) = state.call(
        place_rows, [((rows, model), LOW)], token_half, to_core(token_half),
    )
    (sum_w_down,) = state.call(merge_last_weights, [((block, units), F32)], "down_keep", down_got)
    state.drop("down_keep")
    (sum_w_up,) = state.call(merge_last_weights, [((block, units), F32)], "up_keep", up_got)
    state.drop("up_keep")
    sum_w_qkv, sum_w_out, mine, sum_bias_qv = state.call(
        merge_last_attn,
        [
            ((3, block, width), F32), ((width, block), F32), ((VECTOR_ROWS, block), F32),
            ((2, width // dp_size), F32),
        ],
        "attn_keep", attn_got,
    )
    return (
        output_low,
        token_total,
        sum_w_qkv,
        sum_bias_qv,
        sum_w_out,
        mine[4],
        mine[2],
        mine[3],
        sum_w_up,
        mine[6],
        sum_w_down.T,
        mine[5],
        mine[0],
        mine[1],
    )


def solution(mesh):
    placed = (
        P("dp", None),
        P(None, None, "tensor"),
        P(None, "tensor"),
        P("tensor", None),
        P(),
        P(),
        P(),
        P(None, "tensor"),
        P("tensor"),
        P("tensor", None),
        P(),
        P(),
        P(),
        P("dp", None),
        P("dp"),
    )
    return jax.shard_map(
        on_device,
        mesh=mesh,
        in_specs=placed,
        out_specs=(
            P("dp", None),
            P("dp", None),
            P(None, "dp", "tensor"),
            P(None, ("tensor", "dp")),
            P("tensor", "dp"),
            P("dp"),
            P("dp"),
            P("dp"),
            P("dp", "tensor"),
            P(("tensor", "dp")),
            P("tensor", "dp"),
            P("dp"),
            P("dp"),
            P("dp"),
        ),
        check_vma=False,
    )
```

```python
from functools import partial

import jax
import jax.numpy as jnp
import numpy as np
from jax import lax
from jax.experimental import pallas as pl
from jax.experimental.pallas import tpu as pltpu
from jax.sharding import PartitionSpec as P

HEAD_DIM = 64
NORM_EPSILON = 1e-05
CORES = 2
CHUNKS = 2
DOWN_PARTS = 2
UP_PARTS = 1
PIECES = 2
F32 = jnp.float32
LOW = jnp.bfloat16
MIB = 1 << 20
COST_FLOPS = 0
COST_BYTES = 0

VECTOR_ROWS = 8
PAIR_ROWS = 2 * VECTOR_ROWS


def nn(left, right):
    return lax.dot_general(left, right, (((1,), (0,)), ((), ())), preferred_element_type=F32)


def nt(left, right):
    return lax.dot_general(left, right, (((1,), (1,)), ((), ())), preferred_element_type=F32)


def tn(left, right):
    return lax.dot_general(left, right, (((0,), (0,)), ((), ())), preferred_element_type=F32)


def normalize(resid):
    center = resid - jnp.mean(resid, -1, keepdims=True)
    inverse = lax.rsqrt(jnp.mean(center * center, -1, keepdims=True) + NORM_EPSILON)
    return center * inverse, inverse


def norm_back(grad_norm, normed, inverse):
    mean_grad = jnp.mean(grad_norm, -1, keepdims=True)
    mean_proj = jnp.mean(grad_norm * normed, -1, keepdims=True)
    return inverse * (grad_norm - mean_grad - normed * mean_proj)


(
    H_ACT,
    H_ACT_PASS,
    H_ATTN,
    H_ATTN_KEEP,
    H_BACK,
    H_COTANGENT,
    H_DOWN_KEEP,
    H_DOWN_OTHER,
    H_DOWN_OWN,
    H_FWD_OTHER,
    H_GRAD,
    H_HID,
    H_INVERSE,
    H_LAST,
    H_MLP,
    H_NEXT,
    H_NORMED,
    H_OUT_HALF,
    H_OUT_OTHER,
    H_PACKED,
    H_PACKED_OTHER,
    H_PRE,
    H_PRE_PASS,
    H_RESID,
    H_SAVED,
    H_SLOPES,
    H_SUM_DOWN,
    H_SUM_UP,
    H_SUMS,
    H_TOKENS,
    H_UP_KEEP,
    H_UP_OTHER,
    H_UP_OWN,
    H_W_OUT,
    H_W_QKV,
) = range(35)


class State:
    def __init__(self):
        self.arrays = {}

    def drop(self, *names):
        for name in names:
            del self.arrays[name]

    def call(self, kernel, outs, *inputs, mib=16, scratch=(), loose=False):
        names = list(self.arrays)
        direct = [item for item in inputs if not isinstance(item, tuple)]
        read = {item for item in inputs if isinstance(item, tuple)}
        vmem = pl.BlockSpec(memory_space=pltpu.VMEM)
        anywhere = pl.BlockSpec(memory_space=pl.ANY)
        scalar = pl.BlockSpec(memory_space=pltpu.SMEM)
        held_shapes = [
            jax.ShapeDtypeStruct(self.arrays[name].shape, self.arrays[name].dtype) for name in names
        ]
        out_shapes = [jax.ShapeDtypeStruct(out[0], out[1]) for out in outs]

        def body(*refs):
            refs = list(refs)
            arrays, refs = refs[: len(direct)], refs[len(direct) :]
            held, refs = dict(zip(names, refs)), refs[len(names) :]
            results, refs = refs[: len(outs)], refs[len(outs) :]
            rest = refs[len(names) :]
            ins = [held[item] if isinstance(item, tuple) else arrays.pop(0) for item in inputs]
            kernel(*ins, *results, *rest)

        results = pl.pallas_call(
            body,
            name=getattr(kernel, "func", kernel).__name__,
            out_shape=tuple(out_shapes + held_shapes),
            in_specs=[
                anywhere if loose else scalar if array.dtype == jnp.int32 else vmem
                for array in direct
            ]
            + [vmem if name in read else anywhere for name in names],
            out_specs=tuple([vmem] * len(outs) + [anywhere] * len(names)),
            input_output_aliases={
                len(direct) + index: len(outs) + index for index in range(len(names))
            },
            scratch_shapes=list(scratch),
            compiler_params=pltpu.CompilerParams(vmem_limit_bytes=mib * MIB),
            cost_estimate=pl.CostEstimate(flops=COST_FLOPS, bytes_accessed=COST_BYTES, transcendentals=0),
        )(*direct, *self.arrays.values())
        for name, array in zip(names, results[len(outs) :]):
            self.arrays[name] = array
        returned = []
        for out, array in zip(outs, results):
            if len(out) == 3:
                self.arrays[out[2]] = array
            else:
                returned.append(array)
        return returned


def my_core():
    return lax.rem(lax.axis_index("tensor"), CORES)


BIAS_OUT, GAIN_ONE, SHIFT_ONE, BIAS_UP, BIAS_DOWN, GAIN_TWO, SHIFT_TWO = range(7)


def row(packed, index):
    return packed[index : index + 1, :]


def attn_forward(lengths, tokens, w_qkv, bias_qv, w_out, saved_o, send_o, keep_o):
    core, length = my_core(), lengths[0]
    rows, width = saved_o.shape[1:]
    half = rows // 2
    x = tokens[...]
    query = (nt(x, w_qkv[0]) + bias_qv[0:1, :]).astype(LOW)
    keys = nt(x, w_qkv[1]).astype(LOW)
    values = (nt(x, w_qkv[2]) + bias_qv[1:2, :]).astype(LOW)
    saved_o[0] = query
    saved_o[1] = keys
    saved_o[2] = values
    head_of = lax.broadcasted_iota(jnp.int32, (rows, width), 1) // HEAD_DIM
    key_valid = lax.broadcasted_iota(jnp.int32, (rows, rows), 1) < length
    scaled = query.astype(F32) * HEAD_DIM ** -0.5
    value_full = values.astype(F32)
    total = jnp.zeros((rows, width), F32)
    for head in range(width // HEAD_DIM):
        here = head_of == head
        scores = nt(jnp.where(here, scaled, 0.0).astype(LOW), keys)
        scores = jnp.where(key_valid, scores, -1e30)
        expo = jnp.exp(scores - jnp.max(scores, -1, keepdims=True))
        probs = (expo * (1.0 / jnp.sum(expo, -1, keepdims=True))).astype(LOW)
        total = total + nn(probs, jnp.where(here, value_full, 0.0).astype(LOW))
    saved_o[3] = total.astype(LOW)
    other_start = pl.multiple_of((1 - core) * half, half)
    own_start = pl.multiple_of(core * half, half)
    send_o[...] = nn(saved_o[3, pl.ds(other_start, half), :], w_out[...]).astype(LOW)
    keep_o[...] = nn(saved_o[3, pl.ds(own_start, half), :], w_out[...])


def add_chunks(kept, received, *outs):
    rows = outs[0].shape[0]
    count = len(outs) // 2
    for index in range(count):
        picked = slice(index * rows, (index + 1) * rows)
        total = (kept[picked, :] + received[picked, :].astype(F32)).astype(LOW)
        outs[index][...] = total
        outs[count + index][...] = total


def hold(*refs):
    sems = refs[-1]
    count = (len(refs) - 1) // 2
    copies = [
        pltpu.make_async_copy(refs[index], refs[count + index], sems.at[index])
        for index in range(count)
    ]
    for copy in copies:
        copy.start()
    for copy in copies:
        copy.wait()


def add_rows(kept, *refs):
    received, out = refs[:-1], refs[-1]
    rows = received[0].shape[0]
    for index, part in enumerate(received):
        picked = slice(index * rows, (index + 1) * rows)
        out[picked, :] = (kept[picked, :] + part[...].astype(F32)).astype(LOW)


def final_rows(*refs):
    resids, (own, received, out) = refs[:-3], refs[-3:]
    rows = resids[0].shape[0]
    for index, resid in enumerate(resids):
        picked = slice(index * rows, (index + 1) * rows)
        out[picked, :] = (
            resid[...] + (own[picked, :].astype(F32) + received[picked, :].astype(F32))
        ).astype(LOW)


def place_rows(*refs):
    out = refs[-1]
    pieces = refs[:-1]
    count = len(pieces) // 2
    rows = pieces[0].shape[0]
    half = count * rows
    core = my_core()
    for index in range(count):
        own_start = pl.multiple_of(core * half + index * rows, rows)
        other_start = pl.multiple_of((1 - core) * half + index * rows, rows)
        out[pl.ds(own_start, rows), :] = pieces[index][...]
        out[pl.ds(other_start, rows), :] = pieces[count + index][...]


def mlp_forward(
    index, received, tokens, own, packed, packed_other, up_own, up_other, down_own, down_other, *refs
):
    part_o, hidden_pass_o, act_pass_o, kept_o, hidden_o, act_o, slopes_o, normed_o, inverse_o = refs
    rows, width = part_o.shape
    start = pl.multiple_of((my_core() * CHUNKS + index) * rows, rows)
    resid = tokens[pl.ds(start, rows), :].astype(F32) + row(packed, BIAS_OUT)
    resid = resid + (own[...].astype(F32) + received[...].astype(F32))
    normed, inverse = normalize(resid)
    normed_o[...] = normed
    inverse_o[...] = inverse
    hidden_low = (normed * row(packed, GAIN_ONE) + row(packed, SHIFT_ONE)).astype(LOW)
    hidden_o[...] = hidden_low
    hidden_pass_o[...] = hidden_low

    def units_of(up, vectors, side):
        pre = nn(hidden_low, up[...]) + row(vectors, BIAS_UP)
        cdf = 0.5 * (1.0 + lax.erf(pre * 0.7071067811865476))
        slopes_o[side] = cdf + pre * (jnp.exp(-0.5 * pre * pre) * 0.3989422804014327)
        return (pre * cdf).astype(LOW)

    act_own = units_of(up_own, packed, 0)
    act_o[...] = act_own
    act_other = units_of(up_other, packed_other, 1)
    act_pass_o[...] = act_other
    part = (nn(act_own, down_own[...]) + nn(act_other, down_other[...])).astype(LOW)
    part_o[...] = part
    kept_o[...] = part


def mlp_backward(
    index, lengths, received, normed_one, own, packed, cotangent, down_own, down_other, slopes,
    up_own, up_other, *refs
):
    before, refs = refs[: 4 * index], refs[4 * index :]
    kept_o, grad_o, pre_o, pre_pass_o, out_o, resid_o, sums_o = refs[:7]
    rows, width = kept_o.shape
    length = lengths[0]
    start = pl.multiple_of((my_core() * CHUNKS + index) * rows, rows)
    hidden = normed_one[...] * row(packed, GAIN_ONE) + row(packed, SHIFT_ONE)
    branch = own[...].astype(F32) + received[...].astype(F32) + row(packed, BIAS_DOWN)
    normed, inverse = normalize(hidden + branch)
    valid = lax.broadcasted_iota(jnp.int32, (rows, width), 0) + start < length
    out = jnp.where(valid, normed * row(packed, GAIN_TWO) + row(packed, SHIFT_TWO), 0.0).astype(LOW)
    out_o[...] = out
    grad_out = jnp.where(valid, cotangent[pl.ds(start, rows), :].astype(F32), 0.0)
    sums_o[0:1, :] = jnp.sum(grad_out * normed, 0, keepdims=True)
    sums_o[1:2, :] = jnp.sum(grad_out, 0, keepdims=True)
    grad_resid = norm_back(grad_out * row(packed, GAIN_TWO), normed, inverse)
    resid_o[...] = grad_resid
    grad_mlp = grad_resid.astype(LOW)
    grad_o[...] = grad_mlp
    pre_own = (nt(grad_mlp, down_own[...]) * slopes[0]).astype(LOW)
    pre_o[...] = pre_own
    pre_other = (nt(grad_mlp, down_other[...]) * slopes[1]).astype(LOW)
    pre_pass_o[...] = pre_other
    part = (nt(pre_own, up_own[...]) + nt(pre_other, up_other[...])).astype(LOW)
    kept_o[...] = part
    if len(refs) > 7:
        sends = refs[7:]
        for send, last in zip(sends, (part, grad_mlp, pre_other, out)):
            send[index * rows :, :] = last
        for piece in range(index):
            for send, early in zip(sends, before[4 * piece : 4 * piece + 4]):
                send[piece * rows : (piece + 1) * rows, :] = early[...]


def spread(blocks, grad):
    block = blocks.shape[1]
    for index in range(blocks.shape[0]):
        blocks[index] = grad[index * block : (index + 1) * block, :]


def block_of(dp_size, slot):
    patterns = []
    for order in dp_orders(dp_size):
        pattern = 0
        for step, bit in enumerate(order):
            if (slot >> (len(order) - 1 - step)) & 1:
                pattern |= 1 << bit
        patterns.append(pattern)
    return jnp.where(my_core() == 0, patterns[0], patterns[1]) ^ lax.axis_index("dp")


def weight_grad(left_count, right_count, *refs):
    left_pieces, refs = refs[:left_count], refs[left_count:]
    right_pieces, refs = refs[:right_count], refs[right_count:]
    *sends, keep_o, sum_o, left, right, blocks = refs
    for target, sources in ((left, left_pieces), (right, right_pieces)):
        at = 0
        for source in sources:
            rows = source.shape[0]
            target[at : at + rows, :] = source[...]
            at += rows
    spread(blocks, tn(left[...], right[...]))
    summed = left if sum_o.shape[0] == 1 else right
    sum_o[0:1, :] = jnp.sum(summed[...].astype(F32), 0, keepdims=True)
    count = keep_o.shape[0]
    each = sends[0].shape[0]
    for index in range(count):
        sent = blocks[block_of(2 * count, index + count)].astype(LOW)
        sends[index // each][index % each] = sent
    for index in range(count):
        keep_o[index] = blocks[block_of(2 * count, index)]


def norm_one_back(received, packed, *refs):
    pieces, (low_o, sums_o, resid_o) = refs[:-3], refs[-3:]
    rows = pieces[0].shape[0]
    sums_o[...] = jnp.zeros(sums_o.shape, F32)
    for index in range(CHUNKS):
        own, resid_two, normed, inverse, sums_two = pieces[5 * index : 5 * index + 5]
        picked = slice(index * rows, (index + 1) * rows)
        grad_hidden = resid_two[...] + (own[...].astype(F32) + received[picked, :].astype(F32))
        xhat = normed[...]
        grad_resid = norm_back(grad_hidden * row(packed, GAIN_ONE), xhat, inverse[...])
        resid_o[picked, :] = grad_resid
        low = grad_resid.astype(LOW)
        low_o[picked, :] = low
        sums_o[0:2, :] += sums_two[...]
        sums_o[2:3, :] += jnp.sum(grad_hidden * xhat, 0, keepdims=True)
        sums_o[3:4, :] += jnp.sum(grad_hidden, 0, keepdims=True)
        sums_o[4:5, :] += jnp.sum(low.astype(F32), 0, keepdims=True)


def split_pair(vectors):
    high = vectors.astype(LOW)
    return jnp.concatenate([high.astype(F32), vectors - high.astype(F32)], 0).astype(LOW)


def attn_backward(
    lengths, *refs,
):
    pieces, refs = refs[:2], refs[2:]
    sums_own, sums_other, w_out, saved, tokens, sum_down, sum_up = refs[:7]
    send_o, keep_o, gq_o, gk_o, gv_o, grad_attn, blocks, sums = refs[7:]
    length = lengths[0]
    rows, width = saved.shape[1:]
    place_rows(*pieces, grad_attn)
    grad_rows = grad_attn[...]
    grad_att = nt(grad_rows, w_out[...]).astype(LOW)
    scale = HEAD_DIM ** -0.5
    head_of = lax.broadcasted_iota(jnp.int32, (rows, width), 1) // HEAD_DIM
    key_valid = lax.broadcasted_iota(jnp.int32, (rows, rows), 0) < length
    query, keys, values = saved[0], saved[1], saved[2]
    scaled = query.astype(F32) * scale
    scaled_keys = keys.astype(F32) * scale
    grad_att_full = grad_att.astype(F32)
    grad_q = jnp.zeros((rows, width), F32)
    grad_k = jnp.zeros((rows, width), F32)
    grad_v = jnp.zeros((rows, width), F32)
    for head in range(width // HEAD_DIM):
        here = head_of == head
        scaled_here = jnp.where(here, scaled, 0.0).astype(LOW)
        scores = jnp.where(key_valid, nt(keys, scaled_here), -1e30)
        expo = jnp.exp(scores - jnp.max(scores, 0, keepdims=True))
        probs = expo * (1.0 / jnp.sum(expo, 0, keepdims=True))
        grad_here = jnp.where(here, grad_att_full, 0.0).astype(LOW)
        grad_probs = nt(values, grad_here)
        grad_v = grad_v + nn(probs.astype(LOW), grad_here)
        inner = jnp.sum(probs * grad_probs, 0, keepdims=True)
        grad_scores = (probs * (grad_probs - inner)).astype(LOW)
        grad_k = grad_k + nn(grad_scores, scaled_here)
        grad_q = grad_q + tn(grad_scores, jnp.where(here, scaled_keys, 0.0).astype(LOW))
    low_q, low_k, low_v = grad_q.astype(LOW), grad_k.astype(LOW), grad_v.astype(LOW)
    gq_o[...] = low_q
    gk_o[...] = low_k
    gv_o[...] = low_v
    x = tokens[...]
    weight = jnp.concatenate(
        [tn(x, low_q), tn(x, low_k), tn(x, low_v), tn(grad_rows, saved[3])], 1
    )
    spread(blocks, weight)
    sums[...] = sums_own[...] + sums_other[...]
    sums[5:6, :] = sum_down[0:1, :]
    sums[6:7, :] = sum_up[0:1, :]
    last = VECTOR_ROWS - 1
    sums[last : last + 1, :width] = jnp.sum(low_q.astype(F32), 0, keepdims=True)
    sums[last : last + 1, 2 * width : 3 * width] = jnp.sum(low_v.astype(F32), 0, keepdims=True)
    vector_sums = sums[...]
    block = blocks.shape[1]
    pair = split_pair(vector_sums)
    count = keep_o.shape[0]
    for index in range(count):
        send_o[index, :block] = blocks[block_of(2 * count, index + count)].astype(LOW)
        send_o[index, block:] = pair
    for index in range(count):
        keep_o[index, :block] = blocks[block_of(2 * count, index)]
        keep_o[index, block : block + VECTOR_ROWS] = vector_sums
        keep_o[index, block + VECTOR_ROWS :] = jnp.zeros_like(vector_sums)


def token_back(gq, gk, gv, w_qkv, *outs):
    sends, keep_o = outs[:-1], outs[-1]
    half, rows = keep_o.shape[0], sends[0].shape[0]
    core = my_core()

    def rows_from(start):
        picked = pl.ds(pl.multiple_of(start, half), half)
        return (
            nn(gq[picked, :], w_qkv[0]) + nn(gk[picked, :], w_qkv[1]) + nn(gv[picked, :], w_qkv[2])
        )

    other = rows_from((1 - core) * half).astype(LOW)
    for index, send_o in enumerate(sends):
        send_o[...] = other[index * rows : (index + 1) * rows, :]
    keep_o[...] = rows_from(core * half)


def merge_weights(keep, *refs):
    parts, (send_o, keep_o) = refs[:-2], refs[-2:]
    count = keep_o.shape[0]
    each = parts[0].shape[0]

    def total(index):
        return keep[index] + parts[index // each][index % each].astype(F32)

    for index in range(count):
        send_o[index] = total(count + index).astype(LOW)
    for index in range(count):
        keep_o[index] = total(index)


def merge_last_weights(keep, received, out):
    out[...] = keep[0] + received[0].astype(F32)


def merged_vectors(keep, received, index, at, block):
    high = received[at, block : block + VECTOR_ROWS].astype(F32)
    low = received[at, block + VECTOR_ROWS :].astype(F32)
    return keep[index, block : block + VECTOR_ROWS] + high + low


def merge_attn(part_count, keep, *refs):
    parts, (*sends, keep_o) = refs[:part_count], refs[part_count:]
    count = keep_o.shape[0]
    block = keep_o.shape[1] - PAIR_ROWS
    each = parts[0].shape[0]

    def weights_at(index):
        part = parts[index // each]
        return keep[index, :block] + part[index % each, :block].astype(F32)

    def vectors_at(index):
        return merged_vectors(keep, parts[index // each], index, index % each, block)

    for index in range(count):
        sent = weights_at(count + index).astype(LOW)
        if len(sends) == 1:
            sends[0][index, :block] = sent
            sends[0][index, block:] = split_pair(vectors_at(count + index))
        else:
            first = sends[0].shape[1]
            sends[0][index] = sent[:first]
            sends[1][index, : block - first] = sent[first:]
            sends[1][index, block - first :] = split_pair(vectors_at(count + index))
    for index in range(count):
        keep_o[index, :block] = weights_at(index)
        vectors = vectors_at(index)
        keep_o[index, block : block + VECTOR_ROWS] = vectors
        keep_o[index, block + VECTOR_ROWS :] = jnp.zeros_like(vectors)


def merge_last_attn(keep, first, second, qkv_o, out_o, vectors_o, pair_o):
    block, width = qkv_o.shape[1], qkv_o.shape[2]
    rows = first.shape[1]
    received = jnp.concatenate([first[0].astype(F32), second[0, : block - rows].astype(F32)], 0)
    total = keep[0, :block] + received
    for part in range(3):
        qkv_o[part] = total[:, part * width : (part + 1) * width]
    out_o[...] = total[:, 3 * width :].T
    high = second[0, block - rows : block - rows + VECTOR_ROWS].astype(F32)
    low = second[0, block - rows + VECTOR_ROWS :].astype(F32)
    vectors = keep[0, block : block + VECTOR_ROWS] + high + low
    model = vectors.shape[1]
    me = lax.axis_index("dp")
    vectors_o[...] = pltpu.roll(vectors, lax.rem(model - me * block, model), 1)[:, :block]
    small = pair_o.shape[1]
    turned = pltpu.roll(vectors, lax.rem(model - me * small, model), 1)
    last = VECTOR_ROWS - 1
    pair_o[0:1, :] = turned[last : last + 1, :small]
    pair_o[1:2, :] = turned[last : last + 1, 2 * width : 2 * width + small]


def run_parts(plan, *refs):
    refs = list(refs)
    ins, outs = refs[: sum(part[1] for part in plan)], refs[sum(part[1] for part in plan) :]
    for kernel, taken, given in plan:
        kernel(*ins[:taken], *outs[:given])
        ins, outs = ins[taken:], outs[given:]


CORE_PAIRS = [(i, i ^ 1) for i in range(4)]
CHIP_PAIRS = [(i, i ^ 2) for i in range(4)]


def to_core(block):
    return lax.ppermute(block, "tensor", CORE_PAIRS)


def to_chip(block):
    return lax.ppermute(block, "tensor", CHIP_PAIRS)


def dp_orders(dp_size):
    bits = list(range(dp_size.bit_length() - 1))
    swapped = bits[:2][::-1] + bits[2:]
    return (bits, swapped)


def to_dp(block, step, dp_size, tensor_size):
    orders = dp_orders(dp_size)
    pairs = []
    for d in range(dp_size):
        for t in range(tensor_size):
            partner = d ^ (1 << orders[t % CORES][step])
            pairs.append((d * tensor_size + t, partner * tensor_size + t))
    return lax.ppermute(block, ("dp", "tensor"), pairs)


def on_device(
    tokens,
    w_qkv,
    bias_qv,
    w_out,
    bias_out,
    gain_one,
    shift_one,
    w_up,
    bias_up,
    w_down,
    bias_down,
    gain_two,
    shift_two,
    cotangent,
    lengths,
):
    rows, model = tokens.shape
    half = rows // 2
    chunk = half // CHUNKS
    width = w_qkv.shape[2]
    units = w_up.shape[1]
    dp_size = lax.axis_size("dp")
    tensor_size = lax.axis_size("tensor")
    steps = dp_size.bit_length() - 1
    block = model // dp_size
    count = dp_size // 2
    chunks = range(CHUNKS)
    packed = jnp.stack(
        [bias_out, gain_one, shift_one, bias_up, bias_down, gain_two, shift_two, shift_two]
    )
    w_turned = w_qkv.transpose(0, 2, 1)
    up_other, down_other = to_core(w_up), to_core(w_down)
    packed_other = to_core(packed)

    state = State()
    attn_send, attn_keep = state.call(
        attn_forward,
        [((4, rows, width), LOW, (H_SAVED,)), ((half, model), LOW), ((half, model), F32)],
        lengths, tokens, w_turned, bias_qv, w_out,
        mib=20,
    )
    attn_parts = state.call(
        add_chunks,
        [((chunk, model), LOW)] * CHUNKS + [((chunk, model), LOW, (H_ATTN, c)) for c in chunks],
        attn_keep, to_core(attn_send),
    )
    received = [to_chip(part) for part in attn_parts]
    held = {
        (H_TOKENS,): tokens, (H_W_OUT,): w_out, (H_W_QKV,): w_turned, (H_COTANGENT,): cotangent,
        (H_UP_OWN,): w_up, (H_UP_OTHER,): up_other, (H_DOWN_OWN,): w_down, (H_DOWN_OTHER,): down_other,
        (H_PACKED,): packed, (H_PACKED_OTHER,): packed_other,
    }
    state.call(
        hold,
        [(array.shape, array.dtype, name) for name, array in held.items()],
        *held.values(),
        scratch=[pltpu.SemaphoreType.DMA((len(held),))], loose=True,
    )

    last = CHUNKS - 1
    passed, hidden_other, act_other = [], [], []
    for c in chunks:
        part, hidden_pass, act_pass = state.call(
            partial(mlp_forward, c),
            [((chunk, model), LOW)] * 2
            + [
                ((chunk, units), LOW), ((chunk, model), LOW, (H_MLP, c)),
                ((chunk, model), LOW, (H_HID, c)), ((chunk, units), LOW, (H_ACT, c)),
                ((2, chunk, units), F32, (H_SLOPES, c)),
                ((chunk, model), F32, (H_NORMED, c)), ((chunk, 1), F32, (H_INVERSE, c)),
            ],
            received[c], (H_TOKENS,), (H_ATTN, c), (H_PACKED,), (H_PACKED_OTHER,),
            (H_UP_OWN,), (H_UP_OTHER,), (H_DOWN_OWN,), (H_DOWN_OTHER,),
        )
        state.drop((H_ATTN, c))
        passed.append(to_chip(part))
        hidden_other.append(to_core(hidden_pass))
        act_other.append(to_core(act_pass))
    received = passed

    for c in chunks:
        sends = state.call(
            partial(mlp_backward, c),
            [
                ((chunk, model), LOW, (H_BACK, c)), ((chunk, model), LOW, (H_GRAD, c)),
                ((chunk, units), LOW, (H_PRE, c)), ((chunk, units), LOW, (H_PRE_PASS, c)),
                ((chunk, model), LOW, (H_OUT_HALF, c)), ((chunk, model), F32, (H_RESID, c)),
                ((2, model), F32, (H_SUMS, c)),
            ]
            + [((half, model), LOW)] * (4 * (c == last)),
            lengths, received[c], (H_NORMED, c), (H_MLP, c), (H_PACKED,), (H_COTANGENT,),
            (H_DOWN_OWN,), (H_DOWN_OTHER,), (H_SLOPES, c), (H_UP_OWN,), (H_UP_OTHER,),
            *[
                (name, early)
                for early in range(c)
                for name in (H_BACK, H_GRAD, H_PRE_PASS, H_OUT_HALF)
            ],
        )
        state.drop((H_MLP, c), (H_SLOPES, c))
    for c in chunks:
        state.drop((H_PRE_PASS, c), (H_OUT_HALF, c))
    state.drop((H_COTANGENT,), (H_UP_OWN,), (H_UP_OTHER,), (H_DOWN_OWN,), (H_DOWN_OTHER,))
    back_part, grad_pass, pre_pass, out_half = sends
    received = to_chip(back_part)
    grad_other, pre_other = to_core(grad_pass), to_core(pre_pass)
    out_other = to_core(out_half)

    scratch = [pltpu.VMEM((rows, model), LOW)] * 2 + [pltpu.VMEM((dp_size, block, units), F32)]
    grad_shape = (count, block, units)

    def weight_parts(parts, keep, sum_shape, sum_name, left, right):
        sent = state.call(
            partial(weight_grad, len(left), len(right)),
            [((count // parts, block, units), LOW)] * parts
            + [(grad_shape, F32, (keep,)), (sum_shape, F32, (sum_name,))],
            *left, *right,
            scratch=scratch, mib=20,
        )
        return [to_dp(part, 0, dp_size, tensor_size) for part in sent]

    def held_chunks(name):
        return [(name, c) for c in chunks]

    down_got = weight_parts(
        DOWN_PARTS, H_DOWN_KEEP, (1, model), H_SUM_DOWN,
        held_chunks(H_GRAD) + [grad_other], held_chunks(H_ACT) + act_other,
    )
    up_got = weight_parts(
        UP_PARTS, H_UP_KEEP, (2, units), H_SUM_UP,
        held_chunks(H_HID) + hidden_other, held_chunks(H_PRE) + [pre_other],
    )
    for c in chunks:
        state.drop((H_HID, c), (H_ACT, c), (H_GRAD, c), (H_PRE, c))
    state.arrays[(H_OUT_HALF,)] = out_half
    state.arrays[(H_OUT_OTHER,)] = out_other

    grad_attn, sums = state.call(
        norm_one_back,
        [((half, model), LOW), ((VECTOR_ROWS, model), F32), ((half, model), F32, (H_LAST,))],
        received, (H_PACKED,),
        *[
            (name, c) for c in chunks for name in (H_BACK, H_RESID, H_NORMED, H_INVERSE, H_SUMS)
        ],
    )
    for c in chunks:
        state.drop((H_BACK, c), (H_RESID, c), (H_NORMED, c), (H_INVERSE, c), (H_SUMS, c))
    grad_attn_other = to_core(grad_attn)
    sums_other = to_core(sums)

    running = {(H_DOWN_KEEP,): (down_got, 1), (H_UP_KEEP,): (up_got, 1)}
    finished = {}

    def advance(*names):
        plan, outs, inputs, ends = [], [], [], []
        for name in names:
            got, step = running[name]
            attn = name == (H_ATTN_KEEP,)
            shape = state.arrays[name].shape[1:]
            inputs += [name, *got]
            if step < steps:
                kept = (dp_size >> (step + 1),) + shape
                sends = [(kept, LOW)]
                if attn and step == steps - 1:
                    sends = [
                        (kept[:1] + (rows_of,) + kept[2:], LOW)
                        for rows_of in (block // 2, block - block // 2 + PAIR_ROWS)
                    ]
                kernel = partial(merge_attn, len(got)) if attn else merge_weights
                given = len(sends) + 1
                outs += sends + [(kept, F32, (H_NEXT, name))]
            elif attn:
                kernel, given = merge_last_attn, 4
                outs += [
                    ((3, block, width), F32), ((width, block), F32),
                    ((VECTOR_ROWS, block), F32), ((2, width // dp_size), F32),
                ]
            else:
                kernel, given = merge_last_weights, 1
                outs += [(shape, F32)]
            plan.append((kernel, 1 + len(got), given))
        results = state.call(partial(run_parts, tuple(plan)), outs, *inputs)
        for name in names:
            got, step = running.pop(name)
            state.drop(name)
            if step < steps:
                state.arrays[name] = state.arrays.pop((H_NEXT, name))
                parts = 2 if name == (H_ATTN_KEEP,) and step == steps - 1 else 1
                sent, results = results[:parts], results[parts:]
                running[name] = (
                    [to_dp(part, step, dp_size, tensor_size) for part in sent], step + 1
                )
            elif name == (H_ATTN_KEEP,):
                finished[name], results = results[:4], results[4:]
            else:
                finished[name] = results.pop(0)

    advance((H_DOWN_KEEP,))

    attn_w_send, grad_q, grad_k, grad_v = state.call(
        attn_backward,
        [
            ((count, block + PAIR_ROWS, model), LOW),
            ((count, block + PAIR_ROWS, model), F32, (H_ATTN_KEEP,)),
        ]
        + [((rows, width), LOW)] * 3,
        lengths, grad_attn, grad_attn_other, sums, sums_other,
        (H_W_OUT,), (H_SAVED,), (H_TOKENS,), (H_SUM_DOWN,), (H_SUM_UP,),
        scratch=[
            pltpu.VMEM((rows, model), LOW),
            pltpu.VMEM((dp_size, block, model), F32),
            pltpu.VMEM((VECTOR_ROWS, model), F32),
        ],
        mib=24,
    )
    state.drop((H_SAVED,), (H_SUM_DOWN,), (H_SUM_UP,), (H_W_OUT,), (H_TOKENS,))
    state.drop((H_PACKED,), (H_PACKED_OTHER,))
    running_attn = ([to_dp(attn_w_send, 0, dp_size, tensor_size)], 1)
    advance((H_UP_KEEP,), (H_DOWN_KEEP,))
    *token_parts, token_keep = state.call(
        token_back,
        [((half // PIECES, model), LOW)] * PIECES + [((half, model), F32)],
        grad_q, grad_k, grad_v, (H_W_QKV,),
    )
    state.drop((H_W_QKV,))
    token_other = [to_core(part) for part in token_parts]
    (token_own,) = state.call(add_rows, [((half, model), LOW)], token_keep, *token_other)
    token_received = to_chip(token_own)
    running[(H_ATTN_KEEP,)] = running_attn
    others = [(H_DOWN_KEEP,), (H_UP_KEEP,)]
    while running[(H_ATTN_KEEP,)][1] < steps:
        if running[(H_ATTN_KEEP,)][1] == steps - 1:
            (token_half,) = state.call(
                final_rows, [((half, model), LOW)], (H_LAST,), token_own, token_received
            )
            state.drop((H_LAST,))
        advance((H_ATTN_KEEP,))
        left = [name for name in others if name in running]
        if left != [(H_UP_KEEP,)]:
            advance(*left)
    (output_low,) = state.call(
        place_rows, [((rows, model), LOW)], (H_OUT_HALF,), (H_OUT_OTHER,)
    )
    state.drop((H_OUT_HALF,), (H_OUT_OTHER,))
    (token_total,) = state.call(
        place_rows, [((rows, model), LOW)], token_half, to_core(token_half),
    )
    advance(*[name for name in others if name in running], (H_ATTN_KEEP,))
    sum_w_down, sum_w_up = finished[(H_DOWN_KEEP,)], finished[(H_UP_KEEP,)]
    sum_w_qkv, sum_w_out, mine, sum_bias_qv = finished[(H_ATTN_KEEP,)]
    return (
        output_low,
        token_total,
        sum_w_qkv,
        sum_bias_qv,
        sum_w_out,
        mine[4],
        mine[2],
        mine[3],
        sum_w_up,
        mine[6],
        sum_w_down.T,
        mine[5],
        mine[0],
        mine[1],
    )


def solution(mesh):
    placed = (
        P("dp", None),
        P(None, None, "tensor"),
        P(None, "tensor"),
        P("tensor", None),
        P(),
        P(),
        P(),
        P(None, "tensor"),
        P("tensor"),
        P("tensor", None),
        P(),
        P(),
        P(),
        P("dp", None),
        P("dp"),
    )
    return jax.shard_map(
        on_device,
        mesh=mesh,
        in_specs=placed,
        out_specs=(
            P("dp", None),
            P("dp", None),
            P(None, "dp", "tensor"),
            P(None, ("tensor", "dp")),
            P("tensor", "dp"),
            P("dp"),
            P("dp"),
            P("dp"),
            P("dp", "tensor"),
            P(("tensor", "dp")),
            P("tensor", "dp"),
            P("dp"),
            P("dp"),
            P("dp"),
        ),
        check_vma=False,
    )
```

```python
from functools import partial

import jax
import jax.numpy as jnp
import numpy as np
from jax import lax
from jax.experimental import pallas as pl
from jax.experimental.pallas import tpu as pltpu
from jax.sharding import PartitionSpec as P

HEAD_DIM = 64
NORM_EPSILON = 1e-05
CORES = 2
CHUNKS = 2
DOWN_PARTS = 2
UP_PARTS = 1
PIECES = 4
F32 = jnp.float32
LOW = jnp.bfloat16
MIB = 1 << 20
COST_FLOPS = 0
COST_BYTES = 0

VECTOR_ROWS = 8
PAIR_ROWS = 2 * VECTOR_ROWS
EXTRA_ROWS = VECTOR_ROWS


def nn(left, right):
    return lax.dot_general(left, right, (((1,), (0,)), ((), ())), preferred_element_type=F32)


def nt(left, right):
    return lax.dot_general(left, right, (((1,), (1,)), ((), ())), preferred_element_type=F32)


def tn(left, right):
    return lax.dot_general(left, right, (((0,), (0,)), ((), ())), preferred_element_type=F32)


def normalize(resid):
    center = resid - jnp.mean(resid, -1, keepdims=True)
    inverse = lax.rsqrt(jnp.mean(center * center, -1, keepdims=True) + NORM_EPSILON)
    return center * inverse, inverse


def norm_back(grad_norm, normed, inverse):
    mean_grad = jnp.mean(grad_norm, -1, keepdims=True)
    mean_proj = jnp.mean(grad_norm * normed, -1, keepdims=True)
    return inverse * (grad_norm - mean_grad - normed * mean_proj)


(
    H_ACT,
    H_ACT_PASS,
    H_ATTN,
    H_ATTN_KEEP,
    H_BACK,
    H_COTANGENT,
    H_DOWN_KEEP,
    H_DOWN_OTHER,
    H_DOWN_OWN,
    H_FWD_OTHER,
    H_GRAD,
    H_HID,
    H_INVERSE,
    H_LAST,
    H_MLP,
    H_NEXT,
    H_NORMED,
    H_OUT_HALF,
    H_OUT_OTHER,
    H_PACKED,
    H_PACKED_OTHER,
    H_PRE,
    H_PRE_PASS,
    H_RESID,
    H_SAVED,
    H_SLOPES,
    H_SUM_DOWN,
    H_SUM_UP,
    H_SUMS,
    H_TOKENS,
    H_UP_KEEP,
    H_UP_OTHER,
    H_UP_OWN,
    H_W_OUT,
    H_W_QKV,
) = range(35)


class State:
    def __init__(self):
        self.arrays = {}

    def drop(self, *names):
        for name in names:
            del self.arrays[name]

    def call(self, kernel, outs, *inputs, mib=16, scratch=(), loose=()):
        names = list(self.arrays)
        direct = [item for item in inputs if not isinstance(item, tuple)]
        read = {item for item in inputs if isinstance(item, tuple)}
        vmem = pl.BlockSpec(memory_space=pltpu.VMEM)
        anywhere = pl.BlockSpec(memory_space=pl.ANY)
        scalar = pl.BlockSpec(memory_space=pltpu.SMEM)
        held_shapes = [
            jax.ShapeDtypeStruct(self.arrays[name].shape, self.arrays[name].dtype) for name in names
        ]
        out_shapes = [jax.ShapeDtypeStruct(out[0], out[1]) for out in outs]

        def body(*refs):
            refs = list(refs)
            arrays, refs = refs[: len(direct)], refs[len(direct) :]
            held, refs = dict(zip(names, refs)), refs[len(names) :]
            results, refs = refs[: len(outs)], refs[len(outs) :]
            rest = refs[len(names) :]
            ins = [held[item] if isinstance(item, tuple) else arrays.pop(0) for item in inputs]
            kernel(*ins, *results, *rest)

        results = pl.pallas_call(
            body,
            name=getattr(kernel, "func", kernel).__name__,
            out_shape=tuple(out_shapes + held_shapes),
            in_specs=[
                anywhere if index in loose else scalar if array.dtype == jnp.int32 else vmem
                for index, array in enumerate(direct)
            ]
            + [vmem if name in read else anywhere for name in names],
            out_specs=tuple([vmem] * len(outs) + [anywhere] * len(names)),
            input_output_aliases={
                len(direct) + index: len(outs) + index for index in range(len(names))
            },
            scratch_shapes=list(scratch),
            compiler_params=pltpu.CompilerParams(vmem_limit_bytes=mib * MIB),
            cost_estimate=pl.CostEstimate(flops=COST_FLOPS, bytes_accessed=COST_BYTES, transcendentals=0),
        )(*direct, *self.arrays.values())
        for name, array in zip(names, results[len(outs) :]):
            self.arrays[name] = array
        returned = []
        for out, array in zip(outs, results):
            if len(out) == 3:
                self.arrays[out[2]] = array
            else:
                returned.append(array)
        return returned


def my_core():
    return lax.rem(lax.axis_index("tensor"), CORES)


BIAS_OUT, GAIN_ONE, SHIFT_ONE, BIAS_UP, BIAS_DOWN, GAIN_TWO, SHIFT_TWO = range(7)


def row(packed, index):
    return packed[index : index + 1, :]


def attn_forward(lengths, tokens, w_qkv, bias_qv, w_out, saved_o, send_o, keep_o):
    core, length = my_core(), lengths[0]
    rows, width = saved_o.shape[1:]
    half = rows // 2
    x = tokens[...]
    query = (nt(x, w_qkv[0]) + bias_qv[0:1, :]).astype(LOW)
    keys = nt(x, w_qkv[1]).astype(LOW)
    values = (nt(x, w_qkv[2]) + bias_qv[1:2, :]).astype(LOW)
    saved_o[0] = query
    saved_o[1] = keys
    saved_o[2] = values
    head_of = lax.broadcasted_iota(jnp.int32, (rows, width), 1) // HEAD_DIM
    key_valid = lax.broadcasted_iota(jnp.int32, (rows, rows), 1) < length
    scaled = query.astype(F32) * HEAD_DIM ** -0.5
    value_full = values.astype(F32)
    total = jnp.zeros((rows, width), F32)
    for head in range(width // HEAD_DIM):
        here = head_of == head
        scores = nt(jnp.where(here, scaled, 0.0).astype(LOW), keys)
        scores = jnp.where(key_valid, scores, -1e30)
        expo = jnp.exp(scores - jnp.max(scores, -1, keepdims=True))
        probs = (expo * (1.0 / jnp.sum(expo, -1, keepdims=True))).astype(LOW)
        total = total + nn(probs, jnp.where(here, value_full, 0.0).astype(LOW))
    saved_o[3] = total.astype(LOW)
    other_start = pl.multiple_of((1 - core) * half, half)
    own_start = pl.multiple_of(core * half, half)
    send_o[...] = nn(saved_o[3, pl.ds(other_start, half), :], w_out[...]).astype(LOW)
    keep_o[...] = nn(saved_o[3, pl.ds(own_start, half), :], w_out[...])


def add_chunks(kept, received, *outs):
    rows = outs[0].shape[0]
    count = len(outs) // 2
    for index in range(count):
        picked = slice(index * rows, (index + 1) * rows)
        total = (kept[picked, :] + received[picked, :].astype(F32)).astype(LOW)
        outs[index][...] = total
        outs[count + index][...] = total


def hold(*refs):
    sems = refs[-1]
    count = (len(refs) - 1) // 2
    copies = [
        pltpu.make_async_copy(refs[index], refs[count + index], sems.at[index])
        for index in range(count)
    ]
    for copy in copies:
        copy.start()
    for copy in copies:
        copy.wait()


def add_rows(kept, *refs):
    received, out = refs[:-1], refs[-1]
    rows = received[0].shape[0]
    for index, part in enumerate(received):
        picked = slice(index * rows, (index + 1) * rows)
        out[picked, :] = (kept[picked, :] + part[...].astype(F32)).astype(LOW)


def final_rows(*refs):
    resids, (own, received, out) = refs[:-3], refs[-3:]
    rows = resids[0].shape[0]
    for index, resid in enumerate(resids):
        picked = slice(index * rows, (index + 1) * rows)
        out[picked, :] = (
            resid[...] + (own[picked, :].astype(F32) + received[picked, :].astype(F32))
        ).astype(LOW)


def place_rows(*refs):
    out = refs[-1]
    pieces = refs[:-1]
    count = len(pieces) // 2
    rows = pieces[0].shape[0]
    half = count * rows
    core = my_core()
    for index in range(count):
        own_start = pl.multiple_of(core * half + index * rows, rows)
        other_start = pl.multiple_of((1 - core) * half + index * rows, rows)
        out[pl.ds(own_start, rows), :] = pieces[index][...]
        out[pl.ds(other_start, rows), :] = pieces[count + index][...]


def mlp_forward(
    index, received, tokens, own, packed, packed_other, up_own, up_other, down_own, down_other, *refs
):
    part_o, hidden_pass_o, act_pass_o, kept_o, hidden_o, act_o, slopes_o, normed_o, inverse_o = refs
    rows, width = part_o.shape
    start = pl.multiple_of((my_core() * CHUNKS + index) * rows, rows)
    resid = tokens[pl.ds(start, rows), :].astype(F32) + row(packed, BIAS_OUT)
    resid = resid + (own[...].astype(F32) + received[...].astype(F32))
    normed, inverse = normalize(resid)
    normed_o[...] = normed
    inverse_o[...] = inverse
    hidden_low = (normed * row(packed, GAIN_ONE) + row(packed, SHIFT_ONE)).astype(LOW)
    hidden_o[...] = hidden_low
    hidden_pass_o[...] = hidden_low

    def units_of(up, vectors, side):
        pre = nn(hidden_low, up[...]) + row(vectors, BIAS_UP)
        cdf = 0.5 * (1.0 + lax.erf(pre * 0.7071067811865476))
        slopes_o[side] = cdf + pre * (jnp.exp(-0.5 * pre * pre) * 0.3989422804014327)
        return (pre * cdf).astype(LOW)

    act_own = units_of(up_own, packed, 0)
    act_o[...] = act_own
    act_other = units_of(up_other, packed_other, 1)
    act_pass_o[...] = act_other
    part = (nn(act_own, down_own[...]) + nn(act_other, down_other[...])).astype(LOW)
    part_o[...] = part
    kept_o[...] = part


def mlp_backward(
    index, lengths, received, normed_one, own, packed, cotangent, down_own, down_other, slopes,
    up_own, up_other, *refs
):
    before, refs = refs[: 4 * index], refs[4 * index :]
    kept_o, grad_o, pre_o, pre_pass_o, out_o, resid_o, sums_o = refs[:7]
    rows, width = kept_o.shape
    length = lengths[0]
    start = pl.multiple_of((my_core() * CHUNKS + index) * rows, rows)
    hidden = normed_one[...] * row(packed, GAIN_ONE) + row(packed, SHIFT_ONE)
    branch = own[...].astype(F32) + received[...].astype(F32) + row(packed, BIAS_DOWN)
    normed, inverse = normalize(hidden + branch)
    valid = lax.broadcasted_iota(jnp.int32, (rows, width), 0) + start < length
    out = jnp.where(valid, normed * row(packed, GAIN_TWO) + row(packed, SHIFT_TWO), 0.0).astype(LOW)
    out_o[...] = out
    grad_out = jnp.where(valid, cotangent[pl.ds(start, rows), :].astype(F32), 0.0)
    sums_o[0:1, :] = jnp.sum(grad_out * normed, 0, keepdims=True)
    sums_o[1:2, :] = jnp.sum(grad_out, 0, keepdims=True)
    grad_resid = norm_back(grad_out * row(packed, GAIN_TWO), normed, inverse)
    resid_o[...] = grad_resid
    grad_mlp = grad_resid.astype(LOW)
    grad_o[...] = grad_mlp
    pre_own = (nt(grad_mlp, down_own[...]) * slopes[0]).astype(LOW)
    pre_o[...] = pre_own
    pre_other = (nt(grad_mlp, down_other[...]) * slopes[1]).astype(LOW)
    pre_pass_o[...] = pre_other
    part = (nt(pre_own, up_own[...]) + nt(pre_other, up_other[...])).astype(LOW)
    kept_o[...] = part
    if len(refs) > 7:
        sends = refs[7:]
        for send, last in zip(sends, (part, grad_mlp, pre_other, out)):
            send[index * rows :, :] = last
        for piece in range(index):
            for send, early in zip(sends, before[4 * piece : 4 * piece + 4]):
                send[piece * rows : (piece + 1) * rows, :] = early[...]


def spread(blocks, grad):
    block = blocks.shape[1]
    for index in range(blocks.shape[0]):
        blocks[index] = grad[index * block : (index + 1) * block, :]


def block_of(dp_size, slot):
    patterns = []
    for order in dp_orders(dp_size):
        pattern = 0
        for step, bit in enumerate(order):
            if (slot >> (len(order) - 1 - step)) & 1:
                pattern |= 1 << bit
        patterns.append(pattern)
    return jnp.where(my_core() == 0, patterns[0], patterns[1]) ^ lax.axis_index("dp")


def weight_grad(left_count, right_count, *refs):
    left_pieces, refs = refs[:left_count], refs[left_count:]
    right_pieces, refs = refs[:right_count], refs[right_count:]
    *sends, keep_o, sum_o, left, right, blocks = refs
    for target, sources in ((left, left_pieces), (right, right_pieces)):
        at = 0
        for source in sources:
            rows = source.shape[0]
            target[at : at + rows, :] = source[...]
            at += rows
    spread(blocks, tn(left[...], right[...]))
    summed = left if sum_o.shape[0] == 1 else right
    sum_o[0:1, :] = jnp.sum(summed[...].astype(F32), 0, keepdims=True)
    count = keep_o.shape[0]
    each = sends[0].shape[0]
    for index in range(count):
        sent = blocks[block_of(2 * count, index + count)].astype(LOW)
        sends[index // each][index % each] = sent
    for index in range(count):
        keep_o[index] = blocks[block_of(2 * count, index)]


def norm_one_back(received, packed, *refs):
    pieces, (low_o, sums_o, resid_o) = refs[:-3], refs[-3:]
    rows = pieces[0].shape[0]
    half = CHUNKS * rows
    sums_o[...] = jnp.zeros(sums_o.shape, F32)
    for index in range(CHUNKS):
        own, resid_two, normed, inverse, sums_two = pieces[5 * index : 5 * index + 5]
        picked = slice(index * rows, (index + 1) * rows)
        grad_hidden = resid_two[...] + (own[...].astype(F32) + received[picked, :].astype(F32))
        xhat = normed[...]
        grad_resid = norm_back(grad_hidden * row(packed, GAIN_ONE), xhat, inverse[...])
        resid_o[picked, :] = grad_resid
        low = grad_resid.astype(LOW)
        low_o[picked, :] = low
        sums_o[0:2, :] += sums_two[...]
        sums_o[2:3, :] += jnp.sum(grad_hidden * xhat, 0, keepdims=True)
        sums_o[3:4, :] += jnp.sum(grad_hidden, 0, keepdims=True)
        sums_o[4:5, :] += jnp.sum(low.astype(F32), 0, keepdims=True)
    low_o[half:, :] = split_pair(sums_o[...])


def split_pair(vectors):
    high = vectors.astype(LOW)
    return jnp.concatenate([high.astype(F32), vectors - high.astype(F32)], 0).astype(LOW)


def attn_backward(
    lengths, *refs,
):
    pieces, refs = refs[:2], refs[2:]
    sums_own, w_out, saved, tokens, sum_down, sum_up = refs[:6]
    send_o, keep_o, gq_o, gk_o, gv_o, grad_attn, blocks, sums = refs[6:]
    length = lengths[0]
    rows, width = saved.shape[1:]
    half = rows // 2
    place_rows(*[piece.at[pl.ds(0, half)] for piece in pieces], grad_attn)
    grad_rows = grad_attn[...]
    grad_att = nt(grad_rows, w_out[...]).astype(LOW)
    scale = HEAD_DIM ** -0.5
    head_of = lax.broadcasted_iota(jnp.int32, (rows, width), 1) // HEAD_DIM
    key_valid = lax.broadcasted_iota(jnp.int32, (rows, rows), 0) < length
    query, keys, values = saved[0], saved[1], saved[2]
    scaled = query.astype(F32) * scale
    scaled_keys = keys.astype(F32) * scale
    grad_att_full = grad_att.astype(F32)
    grad_q = jnp.zeros((rows, width), F32)
    grad_k = jnp.zeros((rows, width), F32)
    grad_v = jnp.zeros((rows, width), F32)
    for head in range(width // HEAD_DIM):
        here = head_of == head
        scaled_here = jnp.where(here, scaled, 0.0).astype(LOW)
        scores = jnp.where(key_valid, nt(keys, scaled_here), -1e30)
        expo = jnp.exp(scores - jnp.max(scores, 0, keepdims=True))
        probs = expo * (1.0 / jnp.sum(expo, 0, keepdims=True))
        grad_here = jnp.where(here, grad_att_full, 0.0).astype(LOW)
        grad_probs = nt(values, grad_here)
        grad_v = grad_v + nn(probs.astype(LOW), grad_here)
        inner = jnp.sum(probs * grad_probs, 0, keepdims=True)
        grad_scores = (probs * (grad_probs - inner)).astype(LOW)
        grad_k = grad_k + nn(grad_scores, scaled_here)
        grad_q = grad_q + tn(grad_scores, jnp.where(here, scaled_keys, 0.0).astype(LOW))
    low_q, low_k, low_v = grad_q.astype(LOW), grad_k.astype(LOW), grad_v.astype(LOW)
    gq_o[...] = low_q
    gk_o[...] = low_k
    gv_o[...] = low_v
    x = tokens[...]
    weight = jnp.concatenate(
        [tn(x, low_q), tn(x, low_k), tn(x, low_v), tn(grad_rows, saved[3])], 1
    )
    spread(blocks, weight)
    others = pieces[1][half:, :].astype(F32)
    sums[...] = sums_own[...] + others[:VECTOR_ROWS] + others[VECTOR_ROWS:]
    sums[5:6, :] = sum_down[0:1, :]
    sums[6:7, :] = sum_up[0:1, :]
    last = VECTOR_ROWS - 1
    sums[last : last + 1, :width] = jnp.sum(low_q.astype(F32), 0, keepdims=True)
    sums[last : last + 1, 2 * width : 3 * width] = jnp.sum(low_v.astype(F32), 0, keepdims=True)
    vector_sums = sums[...]
    block = blocks.shape[1]
    pair = vector_sums.astype(LOW)
    count = keep_o.shape[0]
    for index in range(count):
        send_o[index, :block] = blocks[block_of(2 * count, index + count)].astype(LOW)
        send_o[index, block:] = pair
    for index in range(count):
        keep_o[index, :block] = blocks[block_of(2 * count, index)]
        keep_o[index, block:] = vector_sums


def token_back(gq, gk, gv, w_qkv, *outs):
    sends, keep_o = outs[:-1], outs[-1]
    half, rows = keep_o.shape[0], sends[0].shape[0]
    core = my_core()

    def rows_from(start):
        picked = pl.ds(pl.multiple_of(start, half), half)
        return (
            nn(gq[picked, :], w_qkv[0]) + nn(gk[picked, :], w_qkv[1]) + nn(gv[picked, :], w_qkv[2])
        )

    other = rows_from((1 - core) * half).astype(LOW)
    for index, send_o in enumerate(sends):
        send_o[...] = other[index * rows : (index + 1) * rows, :]
    keep_o[...] = rows_from(core * half)


def merge_weights(keep, *refs):
    parts, (send_o, keep_o) = refs[:-2], refs[-2:]
    count = keep_o.shape[0]
    each = parts[0].shape[0]

    def total(index):
        return keep[index] + parts[index // each][index % each].astype(F32)

    for index in range(count):
        send_o[index] = total(count + index).astype(LOW)
    for index in range(count):
        keep_o[index] = total(index)


def merge_last_weights(keep, received, out):
    out[...] = keep[0] + received[0].astype(F32)


def merged_vectors(keep, received, index, at, block):
    return keep[index, block:] + received[at, block:].astype(F32)


def merge_attn(part_count, keep, *refs):
    parts, (*sends, keep_o) = refs[:part_count], refs[part_count:]
    count = keep_o.shape[0]
    block = keep_o.shape[1] - EXTRA_ROWS
    each = parts[0].shape[0]

    def weights_at(index):
        part = parts[index // each]
        return keep[index, :block] + part[index % each, :block].astype(F32)

    def vectors_at(index):
        return merged_vectors(keep, parts[index // each], index, index % each, block)

    for index in range(count):
        sent = weights_at(count + index).astype(LOW)
        if len(sends) == 1:
            sends[0][index, :block] = sent
            sends[0][index, block:] = vectors_at(count + index).astype(LOW)
        else:
            first = sends[0].shape[1]
            sends[0][index] = sent[:first]
            sends[1][index, : block - first] = sent[first:]
            sends[1][index, block - first :] = vectors_at(count + index).astype(LOW)
    for index in range(count):
        keep_o[index, :block] = weights_at(index)
        keep_o[index, block:] = vectors_at(index)


def merge_last_attn(keep, first, second, qkv_o, out_o, pair_o, *vectors_o):
    block, width = qkv_o.shape[1], qkv_o.shape[2]
    rows = first.shape[1]
    received = jnp.concatenate([first[0].astype(F32), second[0, : block - rows].astype(F32)], 0)
    total = keep[0, :block] + received
    for part in range(3):
        qkv_o[part] = total[:, part * width : (part + 1) * width]
    out_o[...] = total[:, 3 * width :].T
    vectors = keep[0, block:] + second[0, block - rows :].astype(F32)
    model = vectors.shape[1]
    me = lax.axis_index("dp")
    mine = pltpu.roll(vectors, lax.rem(model - me * block, model), 1)
    for index, vector_o in enumerate(vectors_o):
        vector_o[...] = mine[index, :block]
    small = pair_o.shape[1]
    turned = pltpu.roll(vectors, lax.rem(model - me * small, model), 1)
    last = VECTOR_ROWS - 1
    pair_o[0:1, :] = turned[last : last + 1, :small]
    pair_o[1:2, :] = turned[last : last + 1, 2 * width : 2 * width + small]


def run_parts(plan, *refs):
    refs = list(refs)
    ins, outs = refs[: sum(part[1] for part in plan)], refs[sum(part[1] for part in plan) :]
    for kernel, taken, given in plan:
        kernel(*ins[:taken], *outs[:given])
        ins, outs = ins[taken:], outs[given:]


CORE_PAIRS = [(i, i ^ 1) for i in range(4)]
CHIP_PAIRS = [(i, i ^ 2) for i in range(4)]


def to_core(block):
    return lax.ppermute(block, "tensor", CORE_PAIRS)


def to_chip(block):
    return lax.ppermute(block, "tensor", CHIP_PAIRS)


def dp_orders(dp_size):
    bits = list(range(dp_size.bit_length() - 1))
    swapped = bits[:2][::-1] + bits[2:]
    return (bits, swapped)


def to_dp(block, step, dp_size, tensor_size):
    orders = dp_orders(dp_size)
    pairs = []
    for d in range(dp_size):
        for t in range(tensor_size):
            partner = d ^ (1 << orders[t % CORES][step])
            pairs.append((d * tensor_size + t, partner * tensor_size + t))
    return lax.ppermute(block, ("dp", "tensor"), pairs)


def on_device(
    tokens,
    w_qkv,
    bias_qv,
    w_out,
    bias_out,
    gain_one,
    shift_one,
    w_up,
    bias_up,
    w_down,
    bias_down,
    gain_two,
    shift_two,
    cotangent,
    lengths,
):
    rows, model = tokens.shape
    half = rows // 2
    chunk = half // CHUNKS
    width = w_qkv.shape[2]
    units = w_up.shape[1]
    dp_size = lax.axis_size("dp")
    tensor_size = lax.axis_size("tensor")
    steps = dp_size.bit_length() - 1
    block = model // dp_size
    count = dp_size // 2
    chunks = range(CHUNKS)
    packed = jnp.stack(
        [bias_out, gain_one, shift_one, bias_up, bias_down, gain_two, shift_two, shift_two]
    )
    w_turned = w_qkv.transpose(0, 2, 1)
    up_other, down_other = to_core(w_up), to_core(w_down)
    packed_other = to_core(packed)

    state = State()
    attn_send, attn_keep = state.call(
        attn_forward,
        [((4, rows, width), LOW, (H_SAVED,)), ((half, model), LOW), ((half, model), F32)],
        lengths, tokens, w_turned, bias_qv, w_out,
        mib=20,
    )
    attn_parts = state.call(
        add_chunks,
        [((chunk, model), LOW)] * CHUNKS + [((chunk, model), LOW, (H_ATTN, c)) for c in chunks],
        attn_keep, to_core(attn_send),
    )
    received = [to_chip(part) for part in attn_parts]
    held = {
        (H_TOKENS,): tokens, (H_W_OUT,): w_out, (H_W_QKV,): w_turned, (H_COTANGENT,): cotangent,
        (H_UP_OWN,): w_up, (H_UP_OTHER,): up_other, (H_DOWN_OWN,): w_down, (H_DOWN_OTHER,): down_other,
        (H_PACKED,): packed, (H_PACKED_OTHER,): packed_other,
    }
    state.call(
        hold,
        [(array.shape, array.dtype, name) for name, array in held.items()],
        *held.values(),
        scratch=[pltpu.SemaphoreType.DMA((len(held),))], loose=range(len(held)),
    )

    last = CHUNKS - 1
    passed, hidden_other, act_other = [], [], []
    for c in chunks:
        part, hidden_pass, act_pass = state.call(
            partial(mlp_forward, c),
            [((chunk, model), LOW)] * 2
            + [
                ((chunk, units), LOW), ((chunk, model), LOW, (H_MLP, c)),
                ((chunk, model), LOW, (H_HID, c)), ((chunk, units), LOW, (H_ACT, c)),
                ((2, chunk, units), F32, (H_SLOPES, c)),
                ((chunk, model), F32, (H_NORMED, c)), ((chunk, 1), F32, (H_INVERSE, c)),
            ],
            received[c], (H_TOKENS,), (H_ATTN, c), (H_PACKED,), (H_PACKED_OTHER,),
            (H_UP_OWN,), (H_UP_OTHER,), (H_DOWN_OWN,), (H_DOWN_OTHER,),
        )
        state.drop((H_ATTN, c))
        passed.append(to_chip(part))
        hidden_other.append(to_core(hidden_pass))
        act_other.append(to_core(act_pass))
    received = passed

    for c in chunks:
        sends = state.call(
            partial(mlp_backward, c),
            [
                ((chunk, model), LOW, (H_BACK, c)), ((chunk, model), LOW, (H_GRAD, c)),
                ((chunk, units), LOW, (H_PRE, c)), ((chunk, units), LOW, (H_PRE_PASS, c)),
                ((chunk, model), LOW, (H_OUT_HALF, c)), ((chunk, model), F32, (H_RESID, c)),
                ((2, model), F32, (H_SUMS, c)),
            ]
            + [((half, model), LOW)] * (4 * (c == last)),
            lengths, received[c], (H_NORMED, c), (H_MLP, c), (H_PACKED,), (H_COTANGENT,),
            (H_DOWN_OWN,), (H_DOWN_OTHER,), (H_SLOPES, c), (H_UP_OWN,), (H_UP_OTHER,),
            *[
                (name, early)
                for early in range(c)
                for name in (H_BACK, H_GRAD, H_PRE_PASS, H_OUT_HALF)
            ],
        )
        state.drop((H_MLP, c), (H_SLOPES, c))
    for c in chunks:
        state.drop((H_PRE_PASS, c), (H_OUT_HALF, c))
    state.drop((H_COTANGENT,), (H_UP_OWN,), (H_UP_OTHER,), (H_DOWN_OWN,), (H_DOWN_OTHER,))
    back_part, grad_pass, pre_pass, out_half = sends
    received = to_chip(back_part)
    grad_other, pre_other = to_core(grad_pass), to_core(pre_pass)
    out_other = to_core(out_half)

    scratch = [pltpu.VMEM((rows, model), LOW)] * 2 + [pltpu.VMEM((dp_size, block, units), F32)]
    grad_shape = (count, block, units)

    def weight_parts(parts, keep, sum_shape, sum_name, left, right):
        sent = state.call(
            partial(weight_grad, len(left), len(right)),
            [((count // parts, block, units), LOW)] * parts
            + [(grad_shape, F32, (keep,)), (sum_shape, F32, (sum_name,))],
            *left, *right,
            scratch=scratch, mib=20,
        )
        return [to_dp(part, 0, dp_size, tensor_size) for part in sent]

    def held_chunks(name):
        return [(name, c) for c in chunks]

    down_got = weight_parts(
        DOWN_PARTS, H_DOWN_KEEP, (1, model), H_SUM_DOWN,
        held_chunks(H_GRAD) + [grad_other], held_chunks(H_ACT) + act_other,
    )
    up_got = weight_parts(
        UP_PARTS, H_UP_KEEP, (2, units), H_SUM_UP,
        held_chunks(H_HID) + hidden_other, held_chunks(H_PRE) + [pre_other],
    )
    for c in chunks:
        state.drop((H_HID, c), (H_ACT, c), (H_GRAD, c), (H_PRE, c))
    state.arrays[(H_OUT_HALF,)] = out_half
    state.arrays[(H_OUT_OTHER,)] = out_other

    grad_attn, sums = state.call(
        norm_one_back,
        [
            ((half + PAIR_ROWS, model), LOW), ((VECTOR_ROWS, model), F32),
            ((half, model), F32, (H_LAST,)),
        ],
        received, (H_PACKED,),
        *[
            (name, c) for c in chunks for name in (H_BACK, H_RESID, H_NORMED, H_INVERSE, H_SUMS)
        ],
    )
    for c in chunks:
        state.drop((H_BACK, c), (H_RESID, c), (H_NORMED, c), (H_INVERSE, c), (H_SUMS, c))
    grad_attn_other = to_core(grad_attn)

    running = {(H_DOWN_KEEP,): (down_got, 1), (H_UP_KEEP,): (up_got, 1)}
    finished = {}

    def advance(*names):
        plan, outs, inputs, ends = [], [], [], []
        for name in names:
            got, step = running[name]
            attn = name == (H_ATTN_KEEP,)
            shape = state.arrays[name].shape[1:]
            inputs += [name, *got]
            if step < steps:
                kept = (dp_size >> (step + 1),) + shape
                sends = [(kept, LOW)]
                if attn and step == steps - 1:
                    sends = [
                        (kept[:1] + (rows_of,) + kept[2:], LOW)
                        for rows_of in (block // 2, block - block // 2 + EXTRA_ROWS)
                    ]
                kernel = partial(merge_attn, len(got)) if attn else merge_weights
                given = len(sends) + 1
                outs += sends + [(kept, F32, (H_NEXT, name))]
            elif attn:
                kernel, given = merge_last_attn, 3 + VECTOR_ROWS - 1
                outs += [
                    ((3, block, width), F32), ((width, block), F32), ((2, width // dp_size), F32),
                ]
                outs += [((block,), F32)] * (VECTOR_ROWS - 1)
            else:
                kernel, given = merge_last_weights, 1
                outs += [(shape, F32)]
            plan.append((kernel, 1 + len(got), given))
        results = state.call(partial(run_parts, tuple(plan)), outs, *inputs)
        for name in names:
            got, step = running.pop(name)
            state.drop(name)
            if step < steps:
                state.arrays[name] = state.arrays.pop((H_NEXT, name))
                parts = 2 if name == (H_ATTN_KEEP,) and step == steps - 1 else 1
                sent, results = results[:parts], results[parts:]
                running[name] = (
                    [to_dp(part, step, dp_size, tensor_size) for part in sent], step + 1
                )
            elif name == (H_ATTN_KEEP,):
                given = 3 + VECTOR_ROWS - 1
                finished[name], results = results[:given], results[given:]
            else:
                finished[name] = results.pop(0)

    advance((H_DOWN_KEEP,))

    attn_w_send, grad_q, grad_k, grad_v = state.call(
        attn_backward,
        [
            ((count, block + EXTRA_ROWS, model), LOW),
            ((count, block + EXTRA_ROWS, model), F32, (H_ATTN_KEEP,)),
        ]
        + [((rows, width), LOW)] * 3,
        lengths, grad_attn, grad_attn_other, sums,
        (H_W_OUT,), (H_SAVED,), (H_TOKENS,), (H_SUM_DOWN,), (H_SUM_UP,),
        scratch=[
            pltpu.VMEM((rows, model), LOW),
            pltpu.VMEM((dp_size, block, model), F32),
            pltpu.VMEM((VECTOR_ROWS, model), F32),
        ],
        mib=24,
    )
    state.drop((H_SAVED,), (H_SUM_DOWN,), (H_SUM_UP,), (H_W_OUT,), (H_TOKENS,))
    state.drop((H_PACKED,), (H_PACKED_OTHER,))
    running_attn = ([to_dp(attn_w_send, 0, dp_size, tensor_size)], 1)
    *token_parts, token_keep = state.call(
        token_back,
        [((half // PIECES, model), LOW)] * PIECES + [((half, model), F32)],
        grad_q, grad_k, grad_v, (H_W_QKV,),
    )
    state.drop((H_W_QKV,))
    token_other = [to_core(part) for part in token_parts]
    advance((H_UP_KEEP,), (H_DOWN_KEEP,))
    (token_own,) = state.call(add_rows, [((half, model), LOW)], token_keep, *token_other)
    token_received = to_chip(token_own)
    running[(H_ATTN_KEEP,)] = running_attn
    others = [(H_DOWN_KEEP,), (H_UP_KEEP,)]
    while running[(H_ATTN_KEEP,)][1] < steps:
        if running[(H_ATTN_KEEP,)][1] == steps - 1:
            (token_half,) = state.call(
                final_rows, [((half, model), LOW)], (H_LAST,), token_own, token_received
            )
            state.drop((H_LAST,))
        advance((H_ATTN_KEEP,))
        left = [name for name in others if name in running]
        if left != [(H_UP_KEEP,)]:
            advance(*left)
    (output_low,) = state.call(
        place_rows, [((rows, model), LOW)], (H_OUT_HALF,), (H_OUT_OTHER,)
    )
    state.drop((H_OUT_HALF,), (H_OUT_OTHER,))
    (token_total,) = state.call(
        place_rows, [((rows, model), LOW)], token_half, to_core(token_half),
    )
    advance(*[name for name in others if name in running], (H_ATTN_KEEP,))
    sum_w_down, sum_w_up = finished[(H_DOWN_KEEP,)], finished[(H_UP_KEEP,)]
    sum_w_qkv, sum_w_out, sum_bias_qv, *mine = finished[(H_ATTN_KEEP,)]
    return (
        output_low,
        token_total,
        sum_w_qkv,
        sum_bias_qv,
        sum_w_out,
        mine[4],
        mine[2],
        mine[3],
        sum_w_up,
        mine[6],
        sum_w_down.T,
        mine[5],
        mine[0],
        mine[1],
    )


def solution(mesh):
    placed = (
        P("dp", None),
        P(None, None, "tensor"),
        P(None, "tensor"),
        P("tensor", None),
        P(),
        P(),
        P(),
        P(None, "tensor"),
        P("tensor"),
        P("tensor", None),
        P(),
        P(),
        P(),
        P("dp", None),
        P("dp"),
    )
    return jax.shard_map(
        on_device,
        mesh=mesh,
        in_specs=placed,
        out_specs=(
            P("dp", None),
            P("dp", None),
            P(None, "dp", "tensor"),
            P(None, ("tensor", "dp")),
            P("tensor", "dp"),
            P("dp"),
            P("dp"),
            P("dp"),
            P("dp", "tensor"),
            P(("tensor", "dp")),
            P("tensor", "dp"),
            P("dp"),
            P("dp"),
            P("dp"),
        ),
        check_vma=False,
    )
```

```python
from functools import partial

import jax
import jax.numpy as jnp
import numpy as np
from jax import lax
from jax.experimental import pallas as pl
from jax.experimental.pallas import tpu as pltpu
from jax.sharding import PartitionSpec as P

HEAD_DIM = 64
NORM_EPSILON = 1e-05
CORES = 2
CHUNKS = 2
DOWN_PARTS = 2
UP_PARTS = 1
PIECES = 4
F32 = jnp.float32
LOW = jnp.bfloat16
MIB = 1 << 20
COST_FLOPS = 0
COST_BYTES = 0

VECTOR_ROWS = 8
PAIR_ROWS = 2 * VECTOR_ROWS
EXTRA_ROWS = VECTOR_ROWS


def nn(left, right):
    return lax.dot_general(left, right, (((1,), (0,)), ((), ())), preferred_element_type=F32)


def nt(left, right):
    return lax.dot_general(left, right, (((1,), (1,)), ((), ())), preferred_element_type=F32)


def tn(left, right):
    return lax.dot_general(left, right, (((0,), (0,)), ((), ())), preferred_element_type=F32)


def normalize(resid):
    center = resid - jnp.mean(resid, -1, keepdims=True)
    inverse = lax.rsqrt(jnp.mean(center * center, -1, keepdims=True) + NORM_EPSILON)
    return center * inverse, inverse


def norm_back(grad_norm, normed, inverse):
    mean_grad = jnp.mean(grad_norm, -1, keepdims=True)
    mean_proj = jnp.mean(grad_norm * normed, -1, keepdims=True)
    return inverse * (grad_norm - mean_grad - normed * mean_proj)


(
    H_ACT,
    H_ACT_PASS,
    H_ATTN,
    H_ATT_OWN,
    H_ATT_OTHER,
    H_ATTN_KEEP,
    H_BACK,
    H_COTANGENT,
    H_DOWN_KEEP,
    H_DOWN_OTHER,
    H_DOWN_OWN,
    H_FWD_OTHER,
    H_GRAD,
    H_HID,
    H_INVERSE,
    H_LAST,
    H_MLP,
    H_NEXT,
    H_NORMED,
    H_OUT_HALF,
    H_OUT_OTHER,
    H_PACKED,
    H_PACKED_OTHER,
    H_PRE,
    H_PRE_PASS,
    H_RESID,
    H_SAVED,
    H_SLOPES,
    H_SUM_DOWN,
    H_SUM_UP,
    H_SUMS,
    H_TOKENS,
    H_UP_KEEP,
    H_UP_OTHER,
    H_UP_OWN,
    H_W_OUT,
    H_W_QKV,
) = range(37)


class State:
    def __init__(self):
        self.arrays = {}

    def drop(self, *names):
        for name in names:
            del self.arrays[name]

    def call(self, kernel, outs, *inputs, mib=16, scratch=(), loose=()):
        names = list(self.arrays)
        direct = [item for item in inputs if not isinstance(item, tuple)]
        read = {item for item in inputs if isinstance(item, tuple)}
        vmem = pl.BlockSpec(memory_space=pltpu.VMEM)
        anywhere = pl.BlockSpec(memory_space=pl.ANY)
        scalar = pl.BlockSpec(memory_space=pltpu.SMEM)
        held_shapes = [
            jax.ShapeDtypeStruct(self.arrays[name].shape, self.arrays[name].dtype) for name in names
        ]
        out_shapes = [jax.ShapeDtypeStruct(out[0], out[1]) for out in outs]

        def body(*refs):
            refs = list(refs)
            arrays, refs = refs[: len(direct)], refs[len(direct) :]
            held, refs = dict(zip(names, refs)), refs[len(names) :]
            results, refs = refs[: len(outs)], refs[len(outs) :]
            rest = refs[len(names) :]
            ins = [held[item] if isinstance(item, tuple) else arrays.pop(0) for item in inputs]
            kernel(*ins, *results, *rest)

        results = pl.pallas_call(
            body,
            name=getattr(kernel, "func", kernel).__name__,
            out_shape=tuple(out_shapes + held_shapes),
            in_specs=[
                anywhere if index in loose else scalar if array.dtype == jnp.int32 else vmem
                for index, array in enumerate(direct)
            ]
            + [vmem if name in read else anywhere for name in names],
            out_specs=tuple([vmem] * len(outs) + [anywhere] * len(names)),
            input_output_aliases={
                len(direct) + index: len(outs) + index for index in range(len(names))
            },
            scratch_shapes=list(scratch),
            compiler_params=pltpu.CompilerParams(vmem_limit_bytes=mib * MIB),
            cost_estimate=pl.CostEstimate(flops=COST_FLOPS, bytes_accessed=COST_BYTES, transcendentals=0),
        )(*direct, *self.arrays.values())
        for name, array in zip(names, results[len(outs) :]):
            self.arrays[name] = array
        returned = []
        for out, array in zip(outs, results):
            if len(out) == 3:
                self.arrays[out[2]] = array
            else:
                returned.append(array)
        return returned


def my_core():
    return lax.rem(lax.axis_index("tensor"), CORES)


BIAS_OUT, GAIN_ONE, SHIFT_ONE, BIAS_UP, BIAS_DOWN, GAIN_TWO, SHIFT_TWO = range(7)


def row(packed, index):
    return packed[index : index + 1, :]


def attend(start, rows_here, length, query, keys, values, saved_o):
    rows, width = keys.shape
    head_of = lax.broadcasted_iota(jnp.int32, (rows, width), 1) // HEAD_DIM
    head_here = lax.broadcasted_iota(jnp.int32, (rows_here, width), 1) // HEAD_DIM
    key_valid = lax.broadcasted_iota(jnp.int32, (rows_here, rows), 1) < length
    scaled = query.astype(F32) * HEAD_DIM ** -0.5
    value_full = values.astype(F32)
    total = jnp.zeros((rows_here, width), F32)
    for head in range(width // HEAD_DIM):
        scores = nt(jnp.where(head_here == head, scaled, 0.0).astype(LOW), keys)
        scores = jnp.where(key_valid, scores, -1e30)
        expo = jnp.exp(scores - jnp.max(scores, -1, keepdims=True))
        probs = (expo * (1.0 / jnp.sum(expo, -1, keepdims=True))).astype(LOW)
        total = total + nn(probs, jnp.where(head_of == head, value_full, 0.0).astype(LOW))
    attended = total.astype(LOW)
    saved_o[...] = attended
    return attended


def attn_forward_other(lengths, tokens, w_qkv, bias_qv, w_out, saved_o, att_o, send_o):
    rows = saved_o.shape[1]
    half = rows // 2
    x = tokens[...]
    saved_o[0] = (nt(x, w_qkv[0]) + bias_qv[0:1, :]).astype(LOW)
    keys = nt(x, w_qkv[1]).astype(LOW)
    values = (nt(x, w_qkv[2]) + bias_qv[1:2, :]).astype(LOW)
    saved_o[1] = keys
    saved_o[2] = values
    start = pl.multiple_of((1 - my_core()) * half, half)
    query = saved_o[0, pl.ds(start, half), :]
    attended = attend(start, half, lengths[0], query, keys, values, att_o)
    send_o[...] = nn(attended, w_out[...]).astype(LOW)


def attn_forward_own(lengths, w_out, saved, att_o, keep_o):
    rows = saved.shape[1]
    half = rows // 2
    start = pl.multiple_of(my_core() * half, half)
    query = saved[0, pl.ds(start, half), :]
    attended = attend(start, half, lengths[0], query, saved[1], saved[2], att_o)
    keep_o[...] = nn(attended, w_out[...])


def add_chunks(kept, received, *outs):
    rows = outs[0].shape[0]
    count = len(outs) // 2
    for index in range(count):
        picked = slice(index * rows, (index + 1) * rows)
        total = (kept[picked, :] + received[picked, :].astype(F32)).astype(LOW)
        outs[index][...] = total
        outs[count + index][...] = total


def hold(*refs):
    sems = refs[-1]
    count = (len(refs) - 1) // 2
    copies = [
        pltpu.make_async_copy(refs[index], refs[count + index], sems.at[index])
        for index in range(count)
    ]
    for copy in copies:
        copy.start()
    for copy in copies:
        copy.wait()


def add_rows(kept, *refs):
    received, out = refs[:-1], refs[-1]
    rows = received[0].shape[0]
    for index, part in enumerate(received):
        picked = slice(index * rows, (index + 1) * rows)
        out[picked, :] = (kept[picked, :] + part[...].astype(F32)).astype(LOW)


def final_rows(*refs):
    resids, (own, received, out) = refs[:-3], refs[-3:]
    rows = resids[0].shape[0]
    for index, resid in enumerate(resids):
        picked = slice(index * rows, (index + 1) * rows)
        out[picked, :] = (
            resid[...] + (own[picked, :].astype(F32) + received[picked, :].astype(F32))
        ).astype(LOW)


def place_rows(*refs):
    out = refs[-1]
    pieces = refs[:-1]
    count = len(pieces) // 2
    rows = pieces[0].shape[0]
    half = count * rows
    core = my_core()
    for index in range(count):
        own_start = pl.multiple_of(core * half + index * rows, rows)
        other_start = pl.multiple_of((1 - core) * half + index * rows, rows)
        out[pl.ds(own_start, rows), :] = pieces[index][...]
        out[pl.ds(other_start, rows), :] = pieces[count + index][...]


def mlp_forward(
    index, received, tokens, own, packed, packed_other, up_own, up_other, down_own, down_other, *refs
):
    part_o, hidden_pass_o, act_pass_o, kept_o, hidden_o, act_o, slopes_o, normed_o, inverse_o = refs
    rows, width = part_o.shape
    start = pl.multiple_of((my_core() * CHUNKS + index) * rows, rows)
    resid = tokens[pl.ds(start, rows), :].astype(F32) + row(packed, BIAS_OUT)
    resid = resid + (own[...].astype(F32) + received[...].astype(F32))
    normed, inverse = normalize(resid)
    normed_o[...] = normed
    inverse_o[...] = inverse
    hidden_low = (normed * row(packed, GAIN_ONE) + row(packed, SHIFT_ONE)).astype(LOW)
    hidden_o[...] = hidden_low
    hidden_pass_o[...] = hidden_low

    def units_of(up, vectors, side):
        pre = nn(hidden_low, up[...]) + row(vectors, BIAS_UP)
        cdf = 0.5 * (1.0 + lax.erf(pre * 0.7071067811865476))
        slopes_o[side] = cdf + pre * (jnp.exp(-0.5 * pre * pre) * 0.3989422804014327)
        return (pre * cdf).astype(LOW)

    act_own = units_of(up_own, packed, 0)
    act_o[...] = act_own
    act_other = units_of(up_other, packed_other, 1)
    act_pass_o[...] = act_other
    part = (nn(act_own, down_own[...]) + nn(act_other, down_other[...])).astype(LOW)
    part_o[...] = part
    kept_o[...] = part


def mlp_backward(
    index, lengths, received, normed_one, own, packed, cotangent, down_own, down_other, slopes,
    up_own, up_other, *refs
):
    before, refs = refs[: 4 * index], refs[4 * index :]
    kept_o, grad_o, pre_o, pre_pass_o, out_o, resid_o, sums_o = refs[:7]
    rows, width = kept_o.shape
    length = lengths[0]
    start = pl.multiple_of((my_core() * CHUNKS + index) * rows, rows)
    hidden = normed_one[...] * row(packed, GAIN_ONE) + row(packed, SHIFT_ONE)
    branch = own[...].astype(F32) + received[...].astype(F32) + row(packed, BIAS_DOWN)
    normed, inverse = normalize(hidden + branch)
    valid = lax.broadcasted_iota(jnp.int32, (rows, width), 0) + start < length
    out = jnp.where(valid, normed * row(packed, GAIN_TWO) + row(packed, SHIFT_TWO), 0.0).astype(LOW)
    out_o[...] = out
    grad_out = jnp.where(valid, cotangent[pl.ds(start, rows), :].astype(F32), 0.0)
    sums_o[0:1, :] = jnp.sum(grad_out * normed, 0, keepdims=True)
    sums_o[1:2, :] = jnp.sum(grad_out, 0, keepdims=True)
    grad_resid = norm_back(grad_out * row(packed, GAIN_TWO), normed, inverse)
    resid_o[...] = grad_resid
    grad_mlp = grad_resid.astype(LOW)
    grad_o[...] = grad_mlp
    pre_own = (nt(grad_mlp, down_own[...]) * slopes[0]).astype(LOW)
    pre_o[...] = pre_own
    pre_other = (nt(grad_mlp, down_other[...]) * slopes[1]).astype(LOW)
    pre_pass_o[...] = pre_other
    part = (nt(pre_own, up_own[...]) + nt(pre_other, up_other[...])).astype(LOW)
    kept_o[...] = part
    if len(refs) > 7:
        sends = refs[7:]
        for send, last in zip(sends, (part, grad_mlp, pre_other, out)):
            send[index * rows :, :] = last
        for piece in range(index):
            for send, early in zip(sends, before[4 * piece : 4 * piece + 4]):
                send[piece * rows : (piece + 1) * rows, :] = early[...]


def spread(blocks, grad):
    block = blocks.shape[1]
    for index in range(blocks.shape[0]):
        blocks[index] = grad[index * block : (index + 1) * block, :]


def block_of(dp_size, slot):
    patterns = []
    for order in dp_orders(dp_size):
        pattern = 0
        for step, bit in enumerate(order):
            if (slot >> (len(order) - 1 - step)) & 1:
                pattern |= 1 << bit
        patterns.append(pattern)
    return jnp.where(my_core() == 0, patterns[0], patterns[1]) ^ lax.axis_index("dp")


def weight_grad(left_count, right_count, *refs):
    left_pieces, refs = refs[:left_count], refs[left_count:]
    right_pieces, refs = refs[:right_count], refs[right_count:]
    *sends, keep_o, sum_o, left, right, blocks = refs
    for target, sources in ((left, left_pieces), (right, right_pieces)):
        at = 0
        for source in sources:
            rows = source.shape[0]
            target[at : at + rows, :] = source[...]
            at += rows
    spread(blocks, tn(left[...], right[...]))
    summed = left if sum_o.shape[0] == 1 else right
    sum_o[0:1, :] = jnp.sum(summed[...].astype(F32), 0, keepdims=True)
    count = keep_o.shape[0]
    each = sends[0].shape[0]
    for index in range(count):
        sent = blocks[block_of(2 * count, index + count)].astype(LOW)
        sends[index // each][index % each] = sent
    for index in range(count):
        keep_o[index] = blocks[block_of(2 * count, index)]


def norm_one_back(received, packed, *refs):
    pieces, (low_o, sums_o, resid_o) = refs[:-3], refs[-3:]
    rows = pieces[0].shape[0]
    half = CHUNKS * rows
    sums_o[...] = jnp.zeros(sums_o.shape, F32)
    for index in range(CHUNKS):
        own, resid_two, normed, inverse, sums_two = pieces[5 * index : 5 * index + 5]
        picked = slice(index * rows, (index + 1) * rows)
        grad_hidden = resid_two[...] + (own[...].astype(F32) + received[picked, :].astype(F32))
        xhat = normed[...]
        grad_resid = norm_back(grad_hidden * row(packed, GAIN_ONE), xhat, inverse[...])
        resid_o[picked, :] = grad_resid
        low = grad_resid.astype(LOW)
        low_o[picked, :] = low
        sums_o[0:2, :] += sums_two[...]
        sums_o[2:3, :] += jnp.sum(grad_hidden * xhat, 0, keepdims=True)
        sums_o[3:4, :] += jnp.sum(grad_hidden, 0, keepdims=True)
        sums_o[4:5, :] += jnp.sum(low.astype(F32), 0, keepdims=True)
    low_o[half:, :] = split_pair(sums_o[...])


def split_pair(vectors):
    high = vectors.astype(LOW)
    return jnp.concatenate([high.astype(F32), vectors - high.astype(F32)], 0).astype(LOW)


def attn_backward(
    lengths, *refs,
):
    pieces, refs = refs[:2], refs[2:]
    sums_own, w_out, saved, att_own, att_other, tokens, sum_down, sum_up = refs[:8]
    send_o, keep_o, gq_o, gk_o, gv_o, grad_attn, attended, blocks, sums = refs[8:]
    length = lengths[0]
    rows, width = saved.shape[1:]
    half = rows // 2
    place_rows(*[piece.at[pl.ds(0, half)] for piece in pieces], grad_attn)
    place_rows(att_own, att_other, attended)
    grad_rows = grad_attn[...]
    grad_att = nt(grad_rows, w_out[...]).astype(LOW)
    scale = HEAD_DIM ** -0.5
    head_of = lax.broadcasted_iota(jnp.int32, (rows, width), 1) // HEAD_DIM
    key_valid = lax.broadcasted_iota(jnp.int32, (rows, rows), 0) < length
    query, keys, values = saved[0], saved[1], saved[2]
    scaled = query.astype(F32) * scale
    scaled_keys = keys.astype(F32) * scale
    grad_att_full = grad_att.astype(F32)
    grad_q = jnp.zeros((rows, width), F32)
    grad_k = jnp.zeros((rows, width), F32)
    grad_v = jnp.zeros((rows, width), F32)
    for head in range(width // HEAD_DIM):
        here = head_of == head
        scaled_here = jnp.where(here, scaled, 0.0).astype(LOW)
        scores = jnp.where(key_valid, nt(keys, scaled_here), -1e30)
        expo = jnp.exp(scores - jnp.max(scores, 0, keepdims=True))
        probs = expo * (1.0 / jnp.sum(expo, 0, keepdims=True))
        grad_here = jnp.where(here, grad_att_full, 0.0).astype(LOW)
        grad_probs = nt(values, grad_here)
        grad_v = grad_v + nn(probs.astype(LOW), grad_here)
        inner = jnp.sum(probs * grad_probs, 0, keepdims=True)
        grad_scores = (probs * (grad_probs - inner)).astype(LOW)
        grad_k = grad_k + nn(grad_scores, scaled_here)
        grad_q = grad_q + tn(grad_scores, jnp.where(here, scaled_keys, 0.0).astype(LOW))
    low_q, low_k, low_v = grad_q.astype(LOW), grad_k.astype(LOW), grad_v.astype(LOW)
    gq_o[...] = low_q
    gk_o[...] = low_k
    gv_o[...] = low_v
    x = tokens[...]
    weight = jnp.concatenate(
        [tn(x, low_q), tn(x, low_k), tn(x, low_v), tn(grad_rows, attended[...])], 1
    )
    spread(blocks, weight)
    others = pieces[1][half:, :].astype(F32)
    sums[...] = sums_own[...] + others[:VECTOR_ROWS] + others[VECTOR_ROWS:]
    sums[5:6, :] = sum_down[0:1, :]
    sums[6:7, :] = sum_up[0:1, :]
    last = VECTOR_ROWS - 1
    sums[last : last + 1, :width] = jnp.sum(low_q.astype(F32), 0, keepdims=True)
    sums[last : last + 1, 2 * width : 3 * width] = jnp.sum(low_v.astype(F32), 0, keepdims=True)
    vector_sums = sums[...]
    block = blocks.shape[1]
    pair = vector_sums.astype(LOW)
    count = keep_o.shape[0]
    for index in range(count):
        send_o[index, :block] = blocks[block_of(2 * count, index + count)].astype(LOW)
        send_o[index, block:] = pair
    for index in range(count):
        keep_o[index, :block] = blocks[block_of(2 * count, index)]
        keep_o[index, block:] = vector_sums


def token_back(gq, gk, gv, w_qkv, *outs):
    sends, keep_o = outs[:-1], outs[-1]
    half, rows = keep_o.shape[0], sends[0].shape[0]
    core = my_core()

    def rows_from(start):
        picked = pl.ds(pl.multiple_of(start, half), half)
        return (
            nn(gq[picked, :], w_qkv[0]) + nn(gk[picked, :], w_qkv[1]) + nn(gv[picked, :], w_qkv[2])
        )

    other = rows_from((1 - core) * half).astype(LOW)
    for index, send_o in enumerate(sends):
        send_o[...] = other[index * rows : (index + 1) * rows, :]
    keep_o[...] = rows_from(core * half)


def merge_weights(keep, *refs):
    parts, (send_o, keep_o) = refs[:-2], refs[-2:]
    count = keep_o.shape[0]
    each = parts[0].shape[0]

    def total(index):
        return keep[index] + parts[index // each][index % each].astype(F32)

    for index in range(count):
        send_o[index] = total(count + index).astype(LOW)
    for index in range(count):
        keep_o[index] = total(index)


def merge_last_weights(keep, received, out):
    out[...] = keep[0] + received[0].astype(F32)


def merged_vectors(keep, received, index, at, block):
    return keep[index, block:] + received[at, block:].astype(F32)


def merge_attn(part_count, keep, *refs):
    parts, (*sends, keep_o) = refs[:part_count], refs[part_count:]
    count = keep_o.shape[0]
    block = keep_o.shape[1] - EXTRA_ROWS
    each = parts[0].shape[0]

    def weights_at(index):
        part = parts[index // each]
        return keep[index, :block] + part[index % each, :block].astype(F32)

    def vectors_at(index):
        return merged_vectors(keep, parts[index // each], index, index % each, block)

    for index in range(count):
        sent = weights_at(count + index).astype(LOW)
        if len(sends) == 1:
            sends[0][index, :block] = sent
            sends[0][index, block:] = vectors_at(count + index).astype(LOW)
        else:
            first = sends[0].shape[1]
            sends[0][index] = sent[:first]
            sends[1][index, : block - first] = sent[first:]
            sends[1][index, block - first :] = vectors_at(count + index).astype(LOW)
    for index in range(count):
        keep_o[index, :block] = weights_at(index)
        keep_o[index, block:] = vectors_at(index)


def merge_last_attn(keep, first, second, qkv_o, out_o, pair_o, *vectors_o):
    block, width = qkv_o.shape[1], qkv_o.shape[2]
    rows = first.shape[1]
    received = jnp.concatenate([first[0].astype(F32), second[0, : block - rows].astype(F32)], 0)
    total = keep[0, :block] + received
    for part in range(3):
        qkv_o[part] = total[:, part * width : (part + 1) * width]
    out_o[...] = total[:, 3 * width :].T
    vectors = keep[0, block:] + second[0, block - rows :].astype(F32)
    model = vectors.shape[1]
    me = lax.axis_index("dp")
    mine = pltpu.roll(vectors, lax.rem(model - me * block, model), 1)
    for index, vector_o in enumerate(vectors_o):
        vector_o[...] = mine[index, :block]
    small = pair_o.shape[1]
    turned = pltpu.roll(vectors, lax.rem(model - me * small, model), 1)
    last = VECTOR_ROWS - 1
    pair_o[0:1, :] = turned[last : last + 1, :small]
    pair_o[1:2, :] = turned[last : last + 1, 2 * width : 2 * width + small]


def run_parts(plan, *refs):
    refs = list(refs)
    ins, outs = refs[: sum(part[1] for part in plan)], refs[sum(part[1] for part in plan) :]
    for kernel, taken, given in plan:
        kernel(*ins[:taken], *outs[:given])
        ins, outs = ins[taken:], outs[given:]


CORE_PAIRS = [(i, i ^ 1) for i in range(4)]
CHIP_PAIRS = [(i, i ^ 2) for i in range(4)]


def to_core(block):
    return lax.ppermute(block, "tensor", CORE_PAIRS)


def to_chip(block):
    return lax.ppermute(block, "tensor", CHIP_PAIRS)


def dp_orders(dp_size):
    bits = list(range(dp_size.bit_length() - 1))
    swapped = bits[:2][::-1] + bits[2:]
    return (bits, swapped)


def to_dp(block, step, dp_size, tensor_size):
    orders = dp_orders(dp_size)
    pairs = []
    for d in range(dp_size):
        for t in range(tensor_size):
            partner = d ^ (1 << orders[t % CORES][step])
            pairs.append((d * tensor_size + t, partner * tensor_size + t))
    return lax.ppermute(block, ("dp", "tensor"), pairs)


def on_device(
    tokens,
    w_qkv,
    bias_qv,
    w_out,
    bias_out,
    gain_one,
    shift_one,
    w_up,
    bias_up,
    w_down,
    bias_down,
    gain_two,
    shift_two,
    cotangent,
    lengths,
):
    rows, model = tokens.shape
    half = rows // 2
    chunk = half // CHUNKS
    width = w_qkv.shape[2]
    units = w_up.shape[1]
    dp_size = lax.axis_size("dp")
    tensor_size = lax.axis_size("tensor")
    steps = dp_size.bit_length() - 1
    block = model // dp_size
    count = dp_size // 2
    chunks = range(CHUNKS)
    packed = jnp.stack(
        [bias_out, gain_one, shift_one, bias_up, bias_down, gain_two, shift_two, shift_two]
    )
    w_turned = w_qkv.transpose(0, 2, 1)
    up_other, down_other = to_core(w_up), to_core(w_down)
    packed_other = to_core(packed)

    state = State()
    (attn_send,) = state.call(
        attn_forward_other,
        [
            ((3, rows, width), LOW, (H_SAVED,)), ((half, width), LOW, (H_ATT_OTHER,)),
            ((half, model), LOW),
        ],
        lengths, tokens, w_turned, bias_qv, w_out,
        mib=20,
    )
    (attn_keep,) = state.call(
        attn_forward_own,
        [((half, width), LOW, (H_ATT_OWN,)), ((half, model), F32)],
        lengths, w_out, (H_SAVED,),
        mib=20,
    )
    attn_parts = state.call(
        add_chunks,
        [((chunk, model), LOW)] * CHUNKS + [((chunk, model), LOW, (H_ATTN, c)) for c in chunks],
        attn_keep, to_core(attn_send),
    )
    received = [to_chip(part) for part in attn_parts]
    held = {
        (H_TOKENS,): tokens, (H_W_OUT,): w_out, (H_W_QKV,): w_turned,
        (H_UP_OWN,): w_up, (H_UP_OTHER,): up_other, (H_DOWN_OWN,): w_down, (H_DOWN_OTHER,): down_other,
        (H_PACKED,): packed, (H_PACKED_OTHER,): packed_other,
    }
    def hold_on(arrays):
        state.call(
            hold,
            [(array.shape, array.dtype, name) for name, array in arrays.items()],
            *arrays.values(),
            scratch=[pltpu.SemaphoreType.DMA((len(arrays),))], loose=range(len(arrays)),
        )

    hold_on(held)
    last = CHUNKS - 1
    passed, hidden_other, act_other = [], [], []
    for c in chunks:
        part, hidden_pass, act_pass = state.call(
            partial(mlp_forward, c),
            [((chunk, model), LOW)] * 2
            + [
                ((chunk, units), LOW), ((chunk, model), LOW, (H_MLP, c)),
                ((chunk, model), LOW, (H_HID, c)), ((chunk, units), LOW, (H_ACT, c)),
                ((2, chunk, units), F32, (H_SLOPES, c)),
                ((chunk, model), F32, (H_NORMED, c)), ((chunk, 1), F32, (H_INVERSE, c)),
            ],
            received[c], (H_TOKENS,), (H_ATTN, c), (H_PACKED,), (H_PACKED_OTHER,),
            (H_UP_OWN,), (H_UP_OTHER,), (H_DOWN_OWN,), (H_DOWN_OTHER,),
        )
        state.drop((H_ATTN, c))
        passed.append(to_chip(part))
        hidden_other.append(to_core(hidden_pass))
        act_other.append(to_core(act_pass))
    received = passed
    hold_on({(H_COTANGENT,): cotangent})

    for c in chunks:
        if c == last:
            for early in chunks:
                state.arrays[(H_FWD_OTHER, early)] = hidden_other[early]
                state.arrays[(H_ACT_PASS, early)] = act_other[early]
        sends = state.call(
            partial(mlp_backward, c),
            [
                ((chunk, model), LOW, (H_BACK, c)), ((chunk, model), LOW, (H_GRAD, c)),
                ((chunk, units), LOW, (H_PRE, c)), ((chunk, units), LOW, (H_PRE_PASS, c)),
                ((chunk, model), LOW, (H_OUT_HALF, c)), ((chunk, model), F32, (H_RESID, c)),
                ((2, model), F32, (H_SUMS, c)),
            ]
            + [((half, model), LOW)] * (4 * (c == last)),
            lengths, received[c], (H_NORMED, c), (H_MLP, c), (H_PACKED,), (H_COTANGENT,),
            (H_DOWN_OWN,), (H_DOWN_OTHER,), (H_SLOPES, c), (H_UP_OWN,), (H_UP_OTHER,),
            *[
                (name, early)
                for early in range(c)
                for name in (H_BACK, H_GRAD, H_PRE_PASS, H_OUT_HALF)
            ],
        )
        state.drop((H_MLP, c), (H_SLOPES, c))
    for c in chunks:
        state.drop((H_PRE_PASS, c), (H_OUT_HALF, c))
    state.drop((H_COTANGENT,), (H_UP_OWN,), (H_UP_OTHER,), (H_DOWN_OWN,), (H_DOWN_OTHER,))
    back_part, grad_pass, pre_pass, out_half = sends
    received = to_chip(back_part)
    grad_other, pre_other = to_core(grad_pass), to_core(pre_pass)
    out_other = to_core(out_half)

    scratch = [pltpu.VMEM((rows, model), LOW)] * 2 + [pltpu.VMEM((dp_size, block, units), F32)]
    grad_shape = (count, block, units)

    def weight_parts(parts, keep, sum_shape, sum_name, left, right):
        sent = state.call(
            partial(weight_grad, len(left), len(right)),
            [((count // parts, block, units), LOW)] * parts
            + [(grad_shape, F32, (keep,)), (sum_shape, F32, (sum_name,))],
            *left, *right,
            scratch=scratch, mib=20,
        )
        return [to_dp(part, 0, dp_size, tensor_size) for part in sent]

    def held_chunks(name):
        return [(name, c) for c in chunks]

    down_got = weight_parts(
        DOWN_PARTS, H_DOWN_KEEP, (1, model), H_SUM_DOWN,
        held_chunks(H_GRAD) + [grad_other], held_chunks(H_ACT) + held_chunks(H_ACT_PASS),
    )
    up_got = weight_parts(
        UP_PARTS, H_UP_KEEP, (2, units), H_SUM_UP,
        held_chunks(H_HID) + held_chunks(H_FWD_OTHER), held_chunks(H_PRE) + [pre_other],
    )
    for c in chunks:
        state.drop((H_HID, c), (H_ACT, c), (H_GRAD, c), (H_PRE, c))
        state.drop((H_FWD_OTHER, c), (H_ACT_PASS, c))
    state.arrays[(H_OUT_HALF,)] = out_half
    state.arrays[(H_OUT_OTHER,)] = out_other

    grad_attn, sums = state.call(
        norm_one_back,
        [
            ((half + PAIR_ROWS, model), LOW), ((VECTOR_ROWS, model), F32),
            ((half, model), F32, (H_LAST,)),
        ],
        received, (H_PACKED,),
        *[
            (name, c) for c in chunks for name in (H_BACK, H_RESID, H_NORMED, H_INVERSE, H_SUMS)
        ],
    )
    for c in chunks:
        state.drop((H_BACK, c), (H_RESID, c), (H_NORMED, c), (H_INVERSE, c), (H_SUMS, c))
    grad_attn_other = to_core(grad_attn)

    running = {(H_DOWN_KEEP,): (down_got, 1), (H_UP_KEEP,): (up_got, 1)}
    finished = {}

    def advance(*names):
        plan, outs, inputs, ends = [], [], [], []
        for name in names:
            got, step = running[name]
            attn = name == (H_ATTN_KEEP,)
            shape = state.arrays[name].shape[1:]
            inputs += [name, *got]
            if step < steps:
                kept = (dp_size >> (step + 1),) + shape
                sends = [(kept, LOW)]
                if attn and step == steps - 1:
                    sends = [
                        (kept[:1] + (rows_of,) + kept[2:], LOW)
                        for rows_of in (block // 2, block - block // 2 + EXTRA_ROWS)
                    ]
                kernel = partial(merge_attn, len(got)) if attn else merge_weights
                given = len(sends) + 1
                outs += sends + [(kept, F32, (H_NEXT, name))]
            elif attn:
                kernel, given = merge_last_attn, 3 + VECTOR_ROWS - 1
                outs += [
                    ((3, block, width), F32), ((width, block), F32), ((2, width // dp_size), F32),
                ]
                outs += [((block,), F32)] * (VECTOR_ROWS - 1)
            else:
                kernel, given = merge_last_weights, 1
                outs += [(shape, F32)]
            plan.append((kernel, 1 + len(got), given))
        results = state.call(partial(run_parts, tuple(plan)), outs, *inputs)
        for name in names:
            got, step = running.pop(name)
            state.drop(name)
            if step < steps:
                state.arrays[name] = state.arrays.pop((H_NEXT, name))
                parts = 2 if name == (H_ATTN_KEEP,) and step == steps - 1 else 1
                sent, results = results[:parts], results[parts:]
                running[name] = (
                    [to_dp(part, step, dp_size, tensor_size) for part in sent], step + 1
                )
            elif name == (H_ATTN_KEEP,):
                given = 3 + VECTOR_ROWS - 1
                finished[name], results = results[:given], results[given:]
            else:
                finished[name] = results.pop(0)

    advance((H_DOWN_KEEP,))

    attn_w_send, grad_q, grad_k, grad_v = state.call(
        attn_backward,
        [
            ((count, block + EXTRA_ROWS, model), LOW),
            ((count, block + EXTRA_ROWS, model), F32, (H_ATTN_KEEP,)),
        ]
        + [((rows, width), LOW)] * 3,
        lengths, grad_attn, grad_attn_other, sums,
        (H_W_OUT,), (H_SAVED,), (H_ATT_OWN,), (H_ATT_OTHER,), (H_TOKENS,), (H_SUM_DOWN,), (H_SUM_UP,),
        scratch=[
            pltpu.VMEM((rows, model), LOW),
            pltpu.VMEM((rows, width), LOW),
            pltpu.VMEM((dp_size, block, model), F32),
            pltpu.VMEM((VECTOR_ROWS, model), F32),
        ],
        mib=24,
    )
    state.drop((H_SAVED,), (H_ATT_OWN,), (H_ATT_OTHER,))
    state.drop((H_SUM_DOWN,), (H_SUM_UP,), (H_W_OUT,), (H_TOKENS,))
    state.drop((H_PACKED,), (H_PACKED_OTHER,))
    running_attn = ([to_dp(attn_w_send, 0, dp_size, tensor_size)], 1)
    *token_parts, token_keep = state.call(
        token_back,
        [((half // PIECES, model), LOW)] * PIECES + [((half, model), F32)],
        grad_q, grad_k, grad_v, (H_W_QKV,),
    )
    state.drop((H_W_QKV,))
    token_other = [to_core(part) for part in token_parts]
    advance((H_UP_KEEP,), (H_DOWN_KEEP,))
    (token_own,) = state.call(add_rows, [((half, model), LOW)], token_keep, *token_other)
    token_received = to_chip(token_own)
    running[(H_ATTN_KEEP,)] = running_attn
    others = [(H_DOWN_KEEP,), (H_UP_KEEP,)]
    while running[(H_ATTN_KEEP,)][1] < steps:
        if running[(H_ATTN_KEEP,)][1] == steps - 1:
            (token_half,) = state.call(
                final_rows, [((half, model), LOW)], (H_LAST,), token_own, token_received
            )
            state.drop((H_LAST,))
        advance((H_ATTN_KEEP,))
        left = [name for name in others if name in running]
        if left != [(H_UP_KEEP,)]:
            advance(*left)
    (output_low,) = state.call(
        place_rows, [((rows, model), LOW)], (H_OUT_HALF,), (H_OUT_OTHER,)
    )
    state.drop((H_OUT_HALF,), (H_OUT_OTHER,))
    (token_total,) = state.call(
        place_rows, [((rows, model), LOW)], token_half, to_core(token_half),
    )
    advance(*[name for name in others if name in running], (H_ATTN_KEEP,))
    sum_w_down, sum_w_up = finished[(H_DOWN_KEEP,)], finished[(H_UP_KEEP,)]
    sum_w_qkv, sum_w_out, sum_bias_qv, *mine = finished[(H_ATTN_KEEP,)]
    return (
        output_low,
        token_total,
        sum_w_qkv,
        sum_bias_qv,
        sum_w_out,
        mine[4],
        mine[2],
        mine[3],
        sum_w_up,
        mine[6],
        sum_w_down.T,
        mine[5],
        mine[0],
        mine[1],
    )


def solution(mesh):
    placed = (
        P("dp", None),
        P(None, None, "tensor"),
        P(None, "tensor"),
        P("tensor", None),
        P(),
        P(),
        P(),
        P(None, "tensor"),
        P("tensor"),
        P("tensor", None),
        P(),
        P(),
        P(),
        P("dp", None),
        P("dp"),
    )
    return jax.shard_map(
        on_device,
        mesh=mesh,
        in_specs=placed,
        out_specs=(
            P("dp", None),
            P("dp", None),
            P(None, "dp", "tensor"),
            P(None, ("tensor", "dp")),
            P("tensor", "dp"),
            P("dp"),
            P("dp"),
            P("dp"),
            P("dp", "tensor"),
            P(("tensor", "dp")),
            P("tensor", "dp"),
            P("dp"),
            P("dp"),
            P("dp"),
        ),
        check_vma=False,
    )
```

```python
from functools import partial

import jax
import jax.numpy as jnp
import numpy as np
from jax import lax
from jax.experimental import pallas as pl
from jax.experimental.pallas import tpu as pltpu
from jax.sharding import PartitionSpec as P

HEAD_DIM = 64
NORM_EPSILON = 1e-05
CORES = 2
CHUNKS = 2
DOWN_PARTS = 1
UP_PARTS = 1
PIECES = 4
F32 = jnp.float32
LOW = jnp.bfloat16
MIB = 1 << 20
COST_FLOPS = 0
COST_BYTES = 0

VECTOR_ROWS = 8
PAIR_ROWS = 2 * VECTOR_ROWS
EXTRA_ROWS = VECTOR_ROWS


def nn(left, right):
    return lax.dot_general(left, right, (((1,), (0,)), ((), ())), preferred_element_type=F32)


def nt(left, right):
    return lax.dot_general(left, right, (((1,), (1,)), ((), ())), preferred_element_type=F32)


def tn(left, right):
    return lax.dot_general(left, right, (((0,), (0,)), ((), ())), preferred_element_type=F32)


def normalize(resid):
    center = resid - jnp.mean(resid, -1, keepdims=True)
    inverse = lax.rsqrt(jnp.mean(center * center, -1, keepdims=True) + NORM_EPSILON)
    return center * inverse, inverse


def norm_back(grad_norm, normed, inverse):
    mean_grad = jnp.mean(grad_norm, -1, keepdims=True)
    mean_proj = jnp.mean(grad_norm * normed, -1, keepdims=True)
    return inverse * (grad_norm - mean_grad - normed * mean_proj)


(
    H_ACT,
    H_ACT_PASS,
    H_ATTN,
    H_ATT_OWN,
    H_ATT_OTHER,
    H_ATTN_KEEP,
    H_BACK,
    H_COTANGENT,
    H_DOWN_KEEP,
    H_DOWN_OTHER,
    H_DOWN_OWN,
    H_FWD_OTHER,
    H_GRAD,
    H_HID,
    H_INVERSE,
    H_LAST,
    H_MLP,
    H_NEXT,
    H_NORMED,
    H_OUT_HALF,
    H_OUT_OTHER,
    H_PACKED,
    H_PACKED_OTHER,
    H_PRE,
    H_PRE_PASS,
    H_RESID,
    H_SAVED,
    H_SLOPES,
    H_SUM_DOWN,
    H_SUM_UP,
    H_SUMS,
    H_TOKENS,
    H_UP_KEEP,
    H_UP_OTHER,
    H_UP_OWN,
    H_W_OUT,
    H_W_QKV,
) = range(37)


class State:
    def __init__(self):
        self.arrays = {}

    def drop(self, *names):
        for name in names:
            del self.arrays[name]

    def call(self, kernel, outs, *inputs, mib=16, scratch=(), loose=()):
        names = list(self.arrays)
        direct = [item for item in inputs if not isinstance(item, tuple)]
        read = {item for item in inputs if isinstance(item, tuple)}
        vmem = pl.BlockSpec(memory_space=pltpu.VMEM)
        anywhere = pl.BlockSpec(memory_space=pl.ANY)
        scalar = pl.BlockSpec(memory_space=pltpu.SMEM)
        held_shapes = [
            jax.ShapeDtypeStruct(self.arrays[name].shape, self.arrays[name].dtype) for name in names
        ]
        out_shapes = [jax.ShapeDtypeStruct(out[0], out[1]) for out in outs]

        def body(*refs):
            refs = list(refs)
            arrays, refs = refs[: len(direct)], refs[len(direct) :]
            held, refs = dict(zip(names, refs)), refs[len(names) :]
            results, refs = refs[: len(outs)], refs[len(outs) :]
            rest = refs[len(names) :]
            ins = [held[item] if isinstance(item, tuple) else arrays.pop(0) for item in inputs]
            kernel(*ins, *results, *rest)

        results = pl.pallas_call(
            body,
            name=getattr(kernel, "func", kernel).__name__,
            out_shape=tuple(out_shapes + held_shapes),
            in_specs=[
                anywhere if index in loose else scalar if array.dtype == jnp.int32 else vmem
                for index, array in enumerate(direct)
            ]
            + [vmem if name in read else anywhere for name in names],
            out_specs=tuple([vmem] * len(outs) + [anywhere] * len(names)),
            input_output_aliases={
                len(direct) + index: len(outs) + index for index in range(len(names))
            },
            scratch_shapes=list(scratch),
            compiler_params=pltpu.CompilerParams(vmem_limit_bytes=mib * MIB),
            cost_estimate=pl.CostEstimate(flops=COST_FLOPS, bytes_accessed=COST_BYTES, transcendentals=0),
        )(*direct, *self.arrays.values())
        for name, array in zip(names, results[len(outs) :]):
            self.arrays[name] = array
        returned = []
        for out, array in zip(outs, results):
            if len(out) == 3:
                self.arrays[out[2]] = array
            else:
                returned.append(array)
        return returned


def my_core():
    return lax.rem(lax.axis_index("tensor"), CORES)


BIAS_OUT, GAIN_ONE, SHIFT_ONE, BIAS_UP, BIAS_DOWN, GAIN_TWO, SHIFT_TWO = range(7)


def row(packed, index):
    return packed[index : index + 1, :]


def attend(start, rows_here, length, query, keys, values, saved_o):
    rows, width = keys.shape
    head_of = lax.broadcasted_iota(jnp.int32, (rows, width), 1) // HEAD_DIM
    head_here = lax.broadcasted_iota(jnp.int32, (rows_here, width), 1) // HEAD_DIM
    key_valid = lax.broadcasted_iota(jnp.int32, (rows_here, rows), 1) < length
    scaled = query.astype(F32) * HEAD_DIM ** -0.5
    value_full = values.astype(F32)
    total = jnp.zeros((rows_here, width), F32)
    for head in range(width // HEAD_DIM):
        scores = nt(jnp.where(head_here == head, scaled, 0.0).astype(LOW), keys)
        scores = jnp.where(key_valid, scores, -1e30)
        expo = jnp.exp(scores - jnp.max(scores, -1, keepdims=True))
        probs = (expo * (1.0 / jnp.sum(expo, -1, keepdims=True))).astype(LOW)
        total = total + nn(probs, jnp.where(head_of == head, value_full, 0.0).astype(LOW))
    attended = total.astype(LOW)
    saved_o[...] = attended
    return attended


def attn_forward_other(lengths, tokens, w_qkv, bias_qv, w_out, saved_o, att_o, send_o):
    rows = saved_o.shape[1]
    half = rows // 2
    x = tokens[...]
    saved_o[0] = (nt(x, w_qkv[0]) + bias_qv[0:1, :]).astype(LOW)
    keys = nt(x, w_qkv[1]).astype(LOW)
    values = (nt(x, w_qkv[2]) + bias_qv[1:2, :]).astype(LOW)
    saved_o[1] = keys
    saved_o[2] = values
    start = pl.multiple_of((1 - my_core()) * half, half)
    query = saved_o[0, pl.ds(start, half), :]
    attended = attend(start, half, lengths[0], query, keys, values, att_o)
    send_o[...] = nn(attended, w_out[...]).astype(LOW)


def attn_forward_own(lengths, w_out, saved, att_o, keep_o):
    rows = saved.shape[1]
    half = rows // 2
    start = pl.multiple_of(my_core() * half, half)
    query = saved[0, pl.ds(start, half), :]
    attended = attend(start, half, lengths[0], query, saved[1], saved[2], att_o)
    keep_o[...] = nn(attended, w_out[...])


def add_chunks(kept, received, *outs):
    *parts, whole = outs
    rows = parts[0].shape[0]
    for index, part in enumerate(parts):
        picked = slice(index * rows, (index + 1) * rows)
        total = (kept[picked, :] + received[picked, :].astype(F32)).astype(LOW)
        part[...] = total
        whole[picked, :] = total


def hold(*refs):
    sems = refs[-1]
    count = (len(refs) - 1) // 2
    copies = [
        pltpu.make_async_copy(refs[index], refs[count + index], sems.at[index])
        for index in range(count)
    ]
    for copy in copies:
        copy.start()
    for copy in copies:
        copy.wait()


def add_rows(kept, *refs):
    received, out = refs[:-1], refs[-1]
    rows = received[0].shape[0]
    for index, part in enumerate(received):
        picked = slice(index * rows, (index + 1) * rows)
        out[picked, :] = (kept[picked, :] + part[...].astype(F32)).astype(LOW)


def final_rows(*refs):
    resids, (own, received, out) = refs[:-3], refs[-3:]
    rows = resids[0].shape[0]
    for index, resid in enumerate(resids):
        picked = slice(index * rows, (index + 1) * rows)
        out[picked, :] = (
            resid[...] + (own[picked, :].astype(F32) + received[picked, :].astype(F32))
        ).astype(LOW)


def place_rows(*refs):
    out = refs[-1]
    pieces = refs[:-1]
    count = len(pieces) // 2
    rows = pieces[0].shape[0]
    half = count * rows
    core = my_core()
    for index in range(count):
        own_start = pl.multiple_of(core * half + index * rows, rows)
        other_start = pl.multiple_of((1 - core) * half + index * rows, rows)
        out[pl.ds(own_start, rows), :] = pieces[index][...]
        out[pl.ds(other_start, rows), :] = pieces[count + index][...]


def mlp_forward(
    index, received, tokens, own, packed, packed_other, up_own, up_other, down_own, down_other, *refs
):
    part_o, hidden_pass_o, act_pass_o, kept_o, hidden_o, act_o, slopes_o, normed_o, inverse_o = refs
    rows, width = part_o.shape
    start = pl.multiple_of((my_core() * CHUNKS + index) * rows, rows)
    resid = tokens[pl.ds(start, rows), :].astype(F32) + row(packed, BIAS_OUT)
    own_rows = own[index * rows : (index + 1) * rows, :].astype(F32)
    resid = resid + (own_rows + received[...].astype(F32))
    normed, inverse = normalize(resid)
    normed_o[...] = normed
    inverse_o[...] = inverse
    hidden_low = (normed * row(packed, GAIN_ONE) + row(packed, SHIFT_ONE)).astype(LOW)
    hidden_o[...] = hidden_low
    hidden_pass_o[...] = hidden_low

    def units_of(up, vectors, side):
        pre = nn(hidden_low, up[...]) + row(vectors, BIAS_UP)
        cdf = 0.5 * (1.0 + lax.erf(pre * 0.7071067811865476))
        slopes_o[side] = cdf + pre * (jnp.exp(-0.5 * pre * pre) * 0.3989422804014327)
        return (pre * cdf).astype(LOW)

    act_own = units_of(up_own, packed, 0)
    act_o[...] = act_own
    act_other = units_of(up_other, packed_other, 1)
    act_pass_o[...] = act_other
    part = (nn(act_own, down_own[...]) + nn(act_other, down_other[...])).astype(LOW)
    part_o[...] = part
    kept_o[...] = part


def mlp_backward(
    index, lengths, received, normed_one, own, packed, cotangent, down_own, down_other, slopes,
    up_own, up_other, *refs
):
    before, refs = refs[: 4 * index], refs[4 * index :]
    kept_o, grad_o, pre_o, pre_pass_o, out_o, resid_o, sums_o = refs[:7]
    rows, width = kept_o.shape
    length = lengths[0]
    start = pl.multiple_of((my_core() * CHUNKS + index) * rows, rows)
    hidden = normed_one[...] * row(packed, GAIN_ONE) + row(packed, SHIFT_ONE)
    branch = own[...].astype(F32) + received[...].astype(F32) + row(packed, BIAS_DOWN)
    normed, inverse = normalize(hidden + branch)
    valid = lax.broadcasted_iota(jnp.int32, (rows, width), 0) + start < length
    out = jnp.where(valid, normed * row(packed, GAIN_TWO) + row(packed, SHIFT_TWO), 0.0).astype(LOW)
    out_o[...] = out
    grad_out = jnp.where(valid, cotangent[pl.ds(start, rows), :].astype(F32), 0.0)
    sums_o[0:1, :] = jnp.sum(grad_out * normed, 0, keepdims=True)
    sums_o[1:2, :] = jnp.sum(grad_out, 0, keepdims=True)
    grad_resid = norm_back(grad_out * row(packed, GAIN_TWO), normed, inverse)
    resid_o[...] = grad_resid
    grad_mlp = grad_resid.astype(LOW)
    grad_o[...] = grad_mlp
    pre_own = (nt(grad_mlp, down_own[...]) * slopes[0]).astype(LOW)
    pre_o[...] = pre_own
    pre_other = (nt(grad_mlp, down_other[...]) * slopes[1]).astype(LOW)
    pre_pass_o[...] = pre_other
    part = (nt(pre_own, up_own[...]) + nt(pre_other, up_other[...])).astype(LOW)
    kept_o[...] = part
    if len(refs) > 7:
        sends = refs[7:]
        for send, last in zip(sends, (part, grad_mlp, pre_other, out)):
            send[index * rows :, :] = last
        for piece in range(index):
            for send, early in zip(sends, before[4 * piece : 4 * piece + 4]):
                send[piece * rows : (piece + 1) * rows, :] = early[...]


def spread(blocks, grad):
    block = blocks.shape[1]
    for index in range(blocks.shape[0]):
        blocks[index] = grad[index * block : (index + 1) * block, :]


def block_of(dp_size, slot):
    patterns = []
    for order in dp_orders(dp_size):
        pattern = 0
        for step, bit in enumerate(order):
            if (slot >> (len(order) - 1 - step)) & 1:
                pattern |= 1 << bit
        patterns.append(pattern)
    return jnp.where(my_core() == 0, patterns[0], patterns[1]) ^ lax.axis_index("dp")


def weight_grad(left_count, right_count, *refs):
    left_pieces, refs = refs[:left_count], refs[left_count:]
    right_pieces, refs = refs[:right_count], refs[right_count:]
    *sends, keep_o, sum_o, left, right, blocks = refs
    for target, sources in ((left, left_pieces), (right, right_pieces)):
        at = 0
        for source in sources:
            rows = source.shape[0]
            target[at : at + rows, :] = source[...]
            at += rows
    spread(blocks, tn(left[...], right[...]))
    summed = left if sum_o.shape[0] == 1 else right
    sum_o[0:1, :] = jnp.sum(summed[...].astype(F32), 0, keepdims=True)
    count = keep_o.shape[0]
    each = sends[0].shape[0]
    for index in range(count):
        sent = blocks[block_of(2 * count, index + count)].astype(LOW)
        sends[index // each][index % each] = sent
    for index in range(count):
        keep_o[index] = blocks[block_of(2 * count, index)]


def norm_one_back(received, packed, *refs):
    pieces, (low_o, sums_o, resid_o) = refs[:-3], refs[-3:]
    rows = pieces[0].shape[0]
    half = CHUNKS * rows
    sums_o[...] = jnp.zeros(sums_o.shape, F32)
    for index in range(CHUNKS):
        own, resid_two, normed, inverse, sums_two = pieces[5 * index : 5 * index + 5]
        picked = slice(index * rows, (index + 1) * rows)
        grad_hidden = resid_two[...] + (own[...].astype(F32) + received[picked, :].astype(F32))
        xhat = normed[...]
        grad_resid = norm_back(grad_hidden * row(packed, GAIN_ONE), xhat, inverse[...])
        resid_o[picked, :] = grad_resid
        low = grad_resid.astype(LOW)
        low_o[picked, :] = low
        sums_o[0:2, :] += sums_two[...]
        sums_o[2:3, :] += jnp.sum(grad_hidden * xhat, 0, keepdims=True)
        sums_o[3:4, :] += jnp.sum(grad_hidden, 0, keepdims=True)
        sums_o[4:5, :] += jnp.sum(low.astype(F32), 0, keepdims=True)
    low_o[half:, :] = split_pair(sums_o[...])


def split_pair(vectors):
    high = vectors.astype(LOW)
    return jnp.concatenate([high.astype(F32), vectors - high.astype(F32)], 0).astype(LOW)


def attn_backward(
    lengths, *refs,
):
    pieces, refs = refs[:2], refs[2:]
    sums_own, w_out, saved, att_own, att_other, tokens, sum_down, sum_up = refs[:8]
    send_o, keep_o, gq_o, gk_o, gv_o, grad_attn, attended, blocks, sums = refs[8:]
    length = lengths[0]
    rows, width = saved.shape[1:]
    half = rows // 2
    place_rows(*[piece.at[pl.ds(0, half)] for piece in pieces], grad_attn)
    place_rows(att_own, att_other, attended)
    grad_rows = grad_attn[...]
    grad_att = nt(grad_rows, w_out[...]).astype(LOW)
    scale = HEAD_DIM ** -0.5
    head_of = lax.broadcasted_iota(jnp.int32, (rows, width), 1) // HEAD_DIM
    key_valid = lax.broadcasted_iota(jnp.int32, (rows, rows), 0) < length
    query, keys, values = saved[0], saved[1], saved[2]
    scaled = query.astype(F32) * scale
    scaled_keys = keys.astype(F32) * scale
    grad_att_full = grad_att.astype(F32)
    grad_q = jnp.zeros((rows, width), F32)
    grad_k = jnp.zeros((rows, width), F32)
    grad_v = jnp.zeros((rows, width), F32)
    for head in range(width // HEAD_DIM):
        here = head_of == head
        scaled_here = jnp.where(here, scaled, 0.0).astype(LOW)
        scores = jnp.where(key_valid, nt(keys, scaled_here), -1e30)
        expo = jnp.exp(scores - jnp.max(scores, 0, keepdims=True))
        probs = expo * (1.0 / jnp.sum(expo, 0, keepdims=True))
        grad_here = jnp.where(here, grad_att_full, 0.0).astype(LOW)
        grad_probs = nt(values, grad_here)
        grad_v = grad_v + nn(probs.astype(LOW), grad_here)
        inner = jnp.sum(probs * grad_probs, 0, keepdims=True)
        grad_scores = (probs * (grad_probs - inner)).astype(LOW)
        grad_k = grad_k + nn(grad_scores, scaled_here)
        grad_q = grad_q + tn(grad_scores, jnp.where(here, scaled_keys, 0.0).astype(LOW))
    low_q, low_k, low_v = grad_q.astype(LOW), grad_k.astype(LOW), grad_v.astype(LOW)
    gq_o[...] = low_q
    gk_o[...] = low_k
    gv_o[...] = low_v
    x = tokens[...]
    weight = jnp.concatenate(
        [tn(x, low_q), tn(x, low_k), tn(x, low_v), tn(grad_rows, attended[...])], 1
    )
    spread(blocks, weight)
    others = pieces[1][half:, :].astype(F32)
    sums[...] = sums_own[...] + others[:VECTOR_ROWS] + others[VECTOR_ROWS:]
    sums[5:6, :] = sum_down[0:1, :]
    sums[6:7, :] = sum_up[0:1, :]
    last = VECTOR_ROWS - 1
    sums[last : last + 1, :width] = jnp.sum(low_q.astype(F32), 0, keepdims=True)
    sums[last : last + 1, 2 * width : 3 * width] = jnp.sum(low_v.astype(F32), 0, keepdims=True)
    vector_sums = sums[...]
    block = blocks.shape[1]
    pair = vector_sums.astype(LOW)
    count = keep_o.shape[0]
    for index in range(count):
        send_o[index, :block] = blocks[block_of(2 * count, index + count)].astype(LOW)
        send_o[index, block:] = pair
    for index in range(count):
        keep_o[index, :block] = blocks[block_of(2 * count, index)]
        keep_o[index, block:] = vector_sums


def token_back(gq, gk, gv, w_qkv, *outs):
    sends, keep_o = outs[:-1], outs[-1]
    half, rows = keep_o.shape[0], sends[0].shape[0]
    core = my_core()

    def rows_from(start):
        picked = pl.ds(pl.multiple_of(start, half), half)
        return (
            nn(gq[picked, :], w_qkv[0]) + nn(gk[picked, :], w_qkv[1]) + nn(gv[picked, :], w_qkv[2])
        )

    other = rows_from((1 - core) * half).astype(LOW)
    for index, send_o in enumerate(sends):
        send_o[...] = other[index * rows : (index + 1) * rows, :]
    keep_o[...] = rows_from(core * half)


def merge_weights(keep, *refs):
    parts, (send_o, keep_o) = refs[:-2], refs[-2:]
    count = keep_o.shape[0]
    each = parts[0].shape[0]

    def total(index):
        return keep[index] + parts[index // each][index % each].astype(F32)

    for index in range(count):
        send_o[index] = total(count + index).astype(LOW)
    for index in range(count):
        keep_o[index] = total(index)


def merge_last_weights(keep, received, out):
    out[...] = keep[0] + received[0].astype(F32)


def merged_vectors(keep, received, index, at, block):
    return keep[index, block:] + received[at, block:].astype(F32)


def merge_attn(part_count, keep, *refs):
    parts, (*sends, keep_o) = refs[:part_count], refs[part_count:]
    count = keep_o.shape[0]
    block = keep_o.shape[1] - EXTRA_ROWS
    each = parts[0].shape[0]

    def weights_at(index):
        part = parts[index // each]
        return keep[index, :block] + part[index % each, :block].astype(F32)

    def vectors_at(index):
        return merged_vectors(keep, parts[index // each], index, index % each, block)

    for index in range(count):
        sent = weights_at(count + index).astype(LOW)
        if len(sends) == 1:
            sends[0][index, :block] = sent
            sends[0][index, block:] = vectors_at(count + index).astype(LOW)
        else:
            first = sends[0].shape[1]
            sends[0][index] = sent[:first]
            sends[1][index, : block - first] = sent[first:]
            sends[1][index, block - first :] = vectors_at(count + index).astype(LOW)
    for index in range(count):
        keep_o[index, :block] = weights_at(index)
        keep_o[index, block:] = vectors_at(index)


def merge_last_attn(keep, first, second, qkv_o, out_o, pair_o, *vectors_o):
    block, width = qkv_o.shape[1], qkv_o.shape[2]
    rows = first.shape[1]
    received = jnp.concatenate([first[0].astype(F32), second[0, : block - rows].astype(F32)], 0)
    total = keep[0, :block] + received
    for part in range(3):
        qkv_o[part] = total[:, part * width : (part + 1) * width]
    out_o[...] = total[:, 3 * width :].T
    vectors = keep[0, block:] + second[0, block - rows :].astype(F32)
    model = vectors.shape[1]
    me = lax.axis_index("dp")
    mine = pltpu.roll(vectors, lax.rem(model - me * block, model), 1)
    for index, vector_o in enumerate(vectors_o):
        vector_o[...] = mine[index, :block]
    small = pair_o.shape[1]
    turned = pltpu.roll(vectors, lax.rem(model - me * small, model), 1)
    last = VECTOR_ROWS - 1
    pair_o[0:1, :] = turned[last : last + 1, :small]
    pair_o[1:2, :] = turned[last : last + 1, 2 * width : 2 * width + small]


def run_parts(plan, *refs):
    refs = list(refs)
    ins, outs = refs[: sum(part[1] for part in plan)], refs[sum(part[1] for part in plan) :]
    for kernel, taken, given in plan:
        kernel(*ins[:taken], *outs[:given])
        ins, outs = ins[taken:], outs[given:]


CORE_PAIRS = [(i, i ^ 1) for i in range(4)]
CHIP_PAIRS = [(i, i ^ 2) for i in range(4)]


def to_core(block):
    return lax.ppermute(block, "tensor", CORE_PAIRS)


def to_chip(block):
    return lax.ppermute(block, "tensor", CHIP_PAIRS)


def dp_orders(dp_size):
    bits = list(range(dp_size.bit_length() - 1))
    swapped = bits[:2][::-1] + bits[2:]
    return (bits, swapped)


def to_dp(block, step, dp_size, tensor_size):
    orders = dp_orders(dp_size)
    pairs = []
    for d in range(dp_size):
        for t in range(tensor_size):
            partner = d ^ (1 << orders[t % CORES][step])
            pairs.append((d * tensor_size + t, partner * tensor_size + t))
    return lax.ppermute(block, ("dp", "tensor"), pairs)


def on_device(
    tokens,
    w_qkv,
    bias_qv,
    w_out,
    bias_out,
    gain_one,
    shift_one,
    w_up,
    bias_up,
    w_down,
    bias_down,
    gain_two,
    shift_two,
    cotangent,
    lengths,
):
    rows, model = tokens.shape
    half = rows // 2
    chunk = half // CHUNKS
    width = w_qkv.shape[2]
    units = w_up.shape[1]
    dp_size = lax.axis_size("dp")
    tensor_size = lax.axis_size("tensor")
    steps = dp_size.bit_length() - 1
    block = model // dp_size
    count = dp_size // 2
    chunks = range(CHUNKS)
    packed = jnp.stack(
        [bias_out, gain_one, shift_one, bias_up, bias_down, gain_two, shift_two, shift_two]
    )
    w_turned = w_qkv.transpose(0, 2, 1)
    up_other, down_other = to_core(w_up), to_core(w_down)
    packed_other = to_core(packed)

    state = State()
    (attn_send,) = state.call(
        attn_forward_other,
        [
            ((3, rows, width), LOW, (H_SAVED,)), ((half, width), LOW, (H_ATT_OTHER,)),
            ((half, model), LOW),
        ],
        lengths, tokens, w_turned, bias_qv, w_out,
        mib=20,
    )
    (attn_keep,) = state.call(
        attn_forward_own,
        [((half, width), LOW, (H_ATT_OWN,)), ((half, model), F32)],
        lengths, w_out, (H_SAVED,),
        mib=20,
    )
    attn_parts = state.call(
        add_chunks,
        [((chunk, model), LOW)] * CHUNKS + [((half, model), LOW, (H_ATTN,))],
        attn_keep, to_core(attn_send),
    )
    received = [to_chip(part) for part in attn_parts]
    held = {
        (H_TOKENS,): tokens, (H_W_OUT,): w_out, (H_W_QKV,): w_turned,
        (H_UP_OWN,): w_up, (H_UP_OTHER,): up_other, (H_DOWN_OWN,): w_down, (H_DOWN_OTHER,): down_other,
        (H_PACKED,): packed, (H_PACKED_OTHER,): packed_other,
    }
    def hold_on(arrays):
        state.call(
            hold,
            [(array.shape, array.dtype, name) for name, array in arrays.items()],
            *arrays.values(),
            scratch=[pltpu.SemaphoreType.DMA((len(arrays),))], loose=range(len(arrays)),
        )

    hold_on(held)
    last = CHUNKS - 1
    passed, hidden_other, act_other = [], [], []
    for c in chunks:
        part, hidden_pass, act_pass = state.call(
            partial(mlp_forward, c),
            [((chunk, model), LOW)] * 2
            + [
                ((chunk, units), LOW), ((chunk, model), LOW, (H_MLP, c)),
                ((chunk, model), LOW, (H_HID, c)), ((chunk, units), LOW, (H_ACT, c)),
                ((2, chunk, units), F32, (H_SLOPES, c)),
                ((chunk, model), F32, (H_NORMED, c)), ((chunk, 1), F32, (H_INVERSE, c)),
            ],
            received[c], (H_TOKENS,), (H_ATTN,), (H_PACKED,), (H_PACKED_OTHER,),
            (H_UP_OWN,), (H_UP_OTHER,), (H_DOWN_OWN,), (H_DOWN_OTHER,),
        )
        passed.append(to_chip(part))
        hidden_other.append(to_core(hidden_pass))
        act_other.append(to_core(act_pass))
    state.drop((H_ATTN,))
    received = passed
    hold_on({(H_COTANGENT,): cotangent})

    for c in chunks:
        if c == last:
            for early in chunks:
                state.arrays[(H_FWD_OTHER, early)] = hidden_other[early]
                state.arrays[(H_ACT_PASS, early)] = act_other[early]
        sends = state.call(
            partial(mlp_backward, c),
            [
                ((chunk, model), LOW, (H_BACK, c)), ((chunk, model), LOW, (H_GRAD, c)),
                ((chunk, units), LOW, (H_PRE, c)), ((chunk, units), LOW, (H_PRE_PASS, c)),
                ((chunk, model), LOW, (H_OUT_HALF, c)), ((chunk, model), F32, (H_RESID, c)),
                ((2, model), F32, (H_SUMS, c)),
            ]
            + [((half, model), LOW)] * (4 * (c == last)),
            lengths, received[c], (H_NORMED, c), (H_MLP, c), (H_PACKED,), (H_COTANGENT,),
            (H_DOWN_OWN,), (H_DOWN_OTHER,), (H_SLOPES, c), (H_UP_OWN,), (H_UP_OTHER,),
            *[
                (name, early)
                for early in range(c)
                for name in (H_BACK, H_GRAD, H_PRE_PASS, H_OUT_HALF)
            ],
        )
        state.drop((H_MLP, c), (H_SLOPES, c))
    for c in chunks:
        state.drop((H_PRE_PASS, c), (H_OUT_HALF, c))
    state.drop((H_COTANGENT,), (H_UP_OWN,), (H_UP_OTHER,), (H_DOWN_OWN,), (H_DOWN_OTHER,))
    back_part, grad_pass, pre_pass, out_half = sends
    received = to_chip(back_part)
    grad_other, pre_other = to_core(grad_pass), to_core(pre_pass)
    out_other = to_core(out_half)

    scratch = [pltpu.VMEM((rows, model), LOW)] * 2 + [pltpu.VMEM((dp_size, block, units), F32)]
    grad_shape = (count, block, units)

    def weight_parts(parts, keep, sum_shape, sum_name, left, right):
        sent = state.call(
            partial(weight_grad, len(left), len(right)),
            [((count // parts, block, units), LOW)] * parts
            + [(grad_shape, F32, (keep,)), (sum_shape, F32, (sum_name,))],
            *left, *right,
            scratch=scratch, mib=20,
        )
        return [to_dp(part, 0, dp_size, tensor_size) for part in sent]

    def held_chunks(name):
        return [(name, c) for c in chunks]

    down_got = weight_parts(
        DOWN_PARTS, H_DOWN_KEEP, (1, model), H_SUM_DOWN,
        held_chunks(H_GRAD) + [grad_other], held_chunks(H_ACT) + held_chunks(H_ACT_PASS),
    )
    up_got = weight_parts(
        UP_PARTS, H_UP_KEEP, (2, units), H_SUM_UP,
        held_chunks(H_HID) + held_chunks(H_FWD_OTHER), held_chunks(H_PRE) + [pre_other],
    )
    for c in chunks:
        state.drop((H_HID, c), (H_ACT, c), (H_GRAD, c), (H_PRE, c))
        state.drop((H_FWD_OTHER, c), (H_ACT_PASS, c))
    state.arrays[(H_OUT_HALF,)] = out_half
    state.arrays[(H_OUT_OTHER,)] = out_other

    grad_attn, sums = state.call(
        norm_one_back,
        [
            ((half + PAIR_ROWS, model), LOW), ((VECTOR_ROWS, model), F32),
            ((half, model), F32, (H_LAST,)),
        ],
        received, (H_PACKED,),
        *[
            (name, c) for c in chunks for name in (H_BACK, H_RESID, H_NORMED, H_INVERSE, H_SUMS)
        ],
    )
    for c in chunks:
        state.drop((H_BACK, c), (H_RESID, c), (H_NORMED, c), (H_INVERSE, c), (H_SUMS, c))
    grad_attn_other = to_core(grad_attn)

    running = {(H_DOWN_KEEP,): (down_got, 1), (H_UP_KEEP,): (up_got, 1)}
    finished = {}

    def advance(*names):
        plan, outs, inputs, ends = [], [], [], []
        for name in names:
            got, step = running[name]
            attn = name == (H_ATTN_KEEP,)
            shape = state.arrays[name].shape[1:]
            inputs += [name, *got]
            if step < steps:
                kept = (dp_size >> (step + 1),) + shape
                sends = [(kept, LOW)]
                if attn and step == steps - 1:
                    sends = [
                        (kept[:1] + (rows_of,) + kept[2:], LOW)
                        for rows_of in (block // 2, block - block // 2 + EXTRA_ROWS)
                    ]
                kernel = partial(merge_attn, len(got)) if attn else merge_weights
                given = len(sends) + 1
                outs += sends + [(kept, F32, (H_NEXT, name))]
            elif attn:
                kernel, given = merge_last_attn, 3 + VECTOR_ROWS - 1
                outs += [
                    ((3, block, width), F32), ((width, block), F32), ((2, width // dp_size), F32),
                ]
                outs += [((block,), F32)] * (VECTOR_ROWS - 1)
            else:
                kernel, given = merge_last_weights, 1
                outs += [(shape, F32)]
            plan.append((kernel, 1 + len(got), given))
        results = state.call(partial(run_parts, tuple(plan)), outs, *inputs)
        for name in names:
            got, step = running.pop(name)
            state.drop(name)
            if step < steps:
                state.arrays[name] = state.arrays.pop((H_NEXT, name))
                parts = 2 if name == (H_ATTN_KEEP,) and step == steps - 1 else 1
                sent, results = results[:parts], results[parts:]
                running[name] = (
                    [to_dp(part, step, dp_size, tensor_size) for part in sent], step + 1
                )
            elif name == (H_ATTN_KEEP,):
                given = 3 + VECTOR_ROWS - 1
                finished[name], results = results[:given], results[given:]
            else:
                finished[name] = results.pop(0)

    advance((H_DOWN_KEEP,))

    attn_w_send, grad_q, grad_k, grad_v = state.call(
        attn_backward,
        [
            ((count, block + EXTRA_ROWS, model), LOW),
            ((count, block + EXTRA_ROWS, model), F32, (H_ATTN_KEEP,)),
        ]
        + [((rows, width), LOW)] * 3,
        lengths, grad_attn, grad_attn_other, sums,
        (H_W_OUT,), (H_SAVED,), (H_ATT_OWN,), (H_ATT_OTHER,), (H_TOKENS,), (H_SUM_DOWN,), (H_SUM_UP,),
        scratch=[
            pltpu.VMEM((rows, model), LOW),
            pltpu.VMEM((rows, width), LOW),
            pltpu.VMEM((dp_size, block, model), F32),
            pltpu.VMEM((VECTOR_ROWS, model), F32),
        ],
        mib=24,
    )
    state.drop((H_SAVED,), (H_ATT_OWN,), (H_ATT_OTHER,))
    state.drop((H_SUM_DOWN,), (H_SUM_UP,), (H_W_OUT,), (H_TOKENS,))
    state.drop((H_PACKED,), (H_PACKED_OTHER,))
    running_attn = ([to_dp(attn_w_send, 0, dp_size, tensor_size)], 1)
    *token_parts, token_keep = state.call(
        token_back,
        [((half // PIECES, model), LOW)] * PIECES + [((half, model), F32)],
        grad_q, grad_k, grad_v, (H_W_QKV,),
    )
    state.drop((H_W_QKV,))
    token_other = [to_core(part) for part in token_parts]
    advance((H_UP_KEEP,), (H_DOWN_KEEP,))
    (token_own,) = state.call(add_rows, [((half, model), LOW)], token_keep, *token_other)
    token_received = to_chip(token_own)
    running[(H_ATTN_KEEP,)] = running_attn
    others = [(H_DOWN_KEEP,), (H_UP_KEEP,)]
    while running[(H_ATTN_KEEP,)][1] < steps:
        if running[(H_ATTN_KEEP,)][1] == steps - 1:
            (token_half,) = state.call(
                final_rows, [((half, model), LOW)], (H_LAST,), token_own, token_received
            )
            state.drop((H_LAST,))
        advance((H_ATTN_KEEP,))
        left = [name for name in others if name in running]
        if left != [(H_UP_KEEP,)]:
            for name in reversed(left):
                advance(name)
    (output_low,) = state.call(
        place_rows, [((rows, model), LOW)], (H_OUT_HALF,), (H_OUT_OTHER,)
    )
    state.drop((H_OUT_HALF,), (H_OUT_OTHER,))
    (token_total,) = state.call(
        place_rows, [((rows, model), LOW)], token_half, to_core(token_half),
    )
    advance(*[name for name in others if name in running], (H_ATTN_KEEP,))
    sum_w_down, sum_w_up = finished[(H_DOWN_KEEP,)], finished[(H_UP_KEEP,)]
    sum_w_qkv, sum_w_out, sum_bias_qv, *mine = finished[(H_ATTN_KEEP,)]
    return (
        output_low,
        token_total,
        sum_w_qkv,
        sum_bias_qv,
        sum_w_out,
        mine[4],
        mine[2],
        mine[3],
        sum_w_up,
        mine[6],
        sum_w_down.T,
        mine[5],
        mine[0],
        mine[1],
    )


def solution(mesh):
    placed = (
        P("dp", None),
        P(None, None, "tensor"),
        P(None, "tensor"),
        P("tensor", None),
        P(),
        P(),
        P(),
        P(None, "tensor"),
        P("tensor"),
        P("tensor", None),
        P(),
        P(),
        P(),
        P("dp", None),
        P("dp"),
    )
    return jax.shard_map(
        on_device,
        mesh=mesh,
        in_specs=placed,
        out_specs=(
            P("dp", None),
            P("dp", None),
            P(None, "dp", "tensor"),
            P(None, ("tensor", "dp")),
            P("tensor", "dp"),
            P("dp"),
            P("dp"),
            P("dp"),
            P("dp", "tensor"),
            P(("tensor", "dp")),
            P("tensor", "dp"),
            P("dp"),
            P("dp"),
            P("dp"),
        ),
        check_vma=False,
    )
```

```python
from functools import partial

import jax
import jax.numpy as jnp
import numpy as np
from jax import lax
from jax.experimental import pallas as pl
from jax.experimental.pallas import tpu as pltpu
from jax.sharding import PartitionSpec as P

HEAD_DIM = 64
NORM_EPSILON = 1e-05
CORES = 2
CHUNKS = 2
DOWN_PARTS = 1
UP_PARTS = 1
PIECES = 4
F32 = jnp.float32
LOW = jnp.bfloat16
MIB = 1 << 20
COST_FLOPS = 0
COST_BYTES = 0

VECTOR_ROWS = 8
PAIR_ROWS = 2 * VECTOR_ROWS
EXTRA_ROWS = VECTOR_ROWS


def nn(left, right):
    return lax.dot_general(left, right, (((1,), (0,)), ((), ())), preferred_element_type=F32)


def nt(left, right):
    return lax.dot_general(left, right, (((1,), (1,)), ((), ())), preferred_element_type=F32)


def tn(left, right):
    return lax.dot_general(left, right, (((0,), (0,)), ((), ())), preferred_element_type=F32)


def normalize(resid):
    center = resid - jnp.mean(resid, -1, keepdims=True)
    inverse = lax.rsqrt(jnp.mean(center * center, -1, keepdims=True) + NORM_EPSILON)
    return center * inverse, inverse


def norm_back(grad_norm, normed, inverse):
    mean_grad = jnp.mean(grad_norm, -1, keepdims=True)
    mean_proj = jnp.mean(grad_norm * normed, -1, keepdims=True)
    return inverse * (grad_norm - mean_grad - normed * mean_proj)


(
    H_ACT,
    H_ACT_PASS,
    H_ATTN,
    H_ATT_OWN,
    H_ATT_OTHER,
    H_ATTN_KEEP,
    H_BACK,
    H_COTANGENT,
    H_DOWN_KEEP,
    H_DOWN_OTHER,
    H_DOWN_OWN,
    H_FWD_OTHER,
    H_GRAD,
    H_HID,
    H_INVERSE,
    H_LAST,
    H_MLP,
    H_NEXT,
    H_NORMED,
    H_OUT_HALF,
    H_OUT_OTHER,
    H_PACKED,
    H_PACKED_OTHER,
    H_PRE,
    H_PRE_PASS,
    H_RESID,
    H_SAVED,
    H_SLOPES,
    H_SUM_DOWN,
    H_SUM_UP,
    H_SUMS,
    H_TOKENS,
    H_UP_KEEP,
    H_UP_OTHER,
    H_UP_OWN,
    H_W_OUT,
    H_W_QKV,
) = range(37)


class State:
    def __init__(self):
        self.arrays = {}

    def drop(self, *names):
        for name in names:
            del self.arrays[name]

    def call(self, kernel, outs, *inputs, mib=16, scratch=(), loose=()):
        names = list(self.arrays)
        direct = [item for item in inputs if not isinstance(item, tuple)]
        read = {item for item in inputs if isinstance(item, tuple)}
        vmem = pl.BlockSpec(memory_space=pltpu.VMEM)
        anywhere = pl.BlockSpec(memory_space=pl.ANY)
        scalar = pl.BlockSpec(memory_space=pltpu.SMEM)
        held_shapes = [
            jax.ShapeDtypeStruct(self.arrays[name].shape, self.arrays[name].dtype) for name in names
        ]
        out_shapes = [jax.ShapeDtypeStruct(out[0], out[1]) for out in outs]

        def body(*refs):
            refs = list(refs)
            arrays, refs = refs[: len(direct)], refs[len(direct) :]
            held, refs = dict(zip(names, refs)), refs[len(names) :]
            results, refs = refs[: len(outs)], refs[len(outs) :]
            rest = refs[len(names) :]
            ins = [held[item] if isinstance(item, tuple) else arrays.pop(0) for item in inputs]
            kernel(*ins, *results, *rest)

        results = pl.pallas_call(
            body,
            name=getattr(kernel, "func", kernel).__name__,
            out_shape=tuple(out_shapes + held_shapes),
            in_specs=[
                anywhere if index in loose else scalar if array.dtype == jnp.int32 else vmem
                for index, array in enumerate(direct)
            ]
            + [vmem if name in read else anywhere for name in names],
            out_specs=tuple([vmem] * len(outs) + [anywhere] * len(names)),
            input_output_aliases={
                len(direct) + index: len(outs) + index for index in range(len(names))
            },
            scratch_shapes=list(scratch),
            compiler_params=pltpu.CompilerParams(vmem_limit_bytes=mib * MIB),
            cost_estimate=pl.CostEstimate(flops=COST_FLOPS, bytes_accessed=COST_BYTES, transcendentals=0),
        )(*direct, *self.arrays.values())
        for name, array in zip(names, results[len(outs) :]):
            self.arrays[name] = array
        returned = []
        for out, array in zip(outs, results):
            if len(out) == 3:
                self.arrays[out[2]] = array
            else:
                returned.append(array)
        return returned


def my_core():
    return lax.rem(lax.axis_index("tensor"), CORES)


BIAS_OUT, GAIN_ONE, SHIFT_ONE, BIAS_UP, BIAS_DOWN, GAIN_TWO, SHIFT_TWO = range(7)


def row(packed, index):
    return packed[index : index + 1, :]


def attend(start, rows_here, length, query, keys, values, saved_o):
    rows, width = keys.shape
    head_of = lax.broadcasted_iota(jnp.int32, (rows, width), 1) // HEAD_DIM
    head_here = lax.broadcasted_iota(jnp.int32, (rows_here, width), 1) // HEAD_DIM
    key_valid = lax.broadcasted_iota(jnp.int32, (rows_here, rows), 1) < length
    scaled = query.astype(F32) * HEAD_DIM ** -0.5
    value_full = values.astype(F32)
    total = jnp.zeros((rows_here, width), F32)
    for head in range(width // HEAD_DIM):
        scores = nt(jnp.where(head_here == head, scaled, 0.0).astype(LOW), keys)
        scores = jnp.where(key_valid, scores, -1e30)
        expo = jnp.exp(scores - jnp.max(scores, -1, keepdims=True))
        probs = (expo * (1.0 / jnp.sum(expo, -1, keepdims=True))).astype(LOW)
        total = total + nn(probs, jnp.where(head_of == head, value_full, 0.0).astype(LOW))
    attended = total.astype(LOW)
    saved_o[...] = attended
    return attended


def attn_forward_other(lengths, tokens, w_qkv, bias_qv, w_out, saved_o, att_o, send_o):
    rows = saved_o.shape[1]
    half = rows // 2
    x = tokens[...]
    saved_o[0] = (nt(x, w_qkv[0]) + bias_qv[0:1, :]).astype(LOW)
    keys = nt(x, w_qkv[1]).astype(LOW)
    values = (nt(x, w_qkv[2]) + bias_qv[1:2, :]).astype(LOW)
    saved_o[1] = keys
    saved_o[2] = values
    start = pl.multiple_of((1 - my_core()) * half, half)
    query = saved_o[0, pl.ds(start, half), :]
    attended = attend(start, half, lengths[0], query, keys, values, att_o)
    send_o[...] = nn(attended, w_out[...]).astype(LOW)


def attn_forward_own(lengths, w_out, saved, att_o, keep_o):
    rows = saved.shape[1]
    half = rows // 2
    start = pl.multiple_of(my_core() * half, half)
    query = saved[0, pl.ds(start, half), :]
    attended = attend(start, half, lengths[0], query, saved[1], saved[2], att_o)
    keep_o[...] = nn(attended, w_out[...])


def add_chunks(kept, received, *outs):
    *parts, whole = outs
    rows = parts[0].shape[0]
    for index, part in enumerate(parts):
        picked = slice(index * rows, (index + 1) * rows)
        total = (kept[picked, :] + received[picked, :].astype(F32)).astype(LOW)
        part[...] = total
        whole[picked, :] = total


def hold(*refs):
    sems = refs[-1]
    count = (len(refs) - 1) // 2
    copies = [
        pltpu.make_async_copy(refs[index], refs[count + index], sems.at[index])
        for index in range(count)
    ]
    for copy in copies:
        copy.start()
    for copy in copies:
        copy.wait()


def add_rows(kept, *refs):
    received, out = refs[:-1], refs[-1]
    rows = received[0].shape[0]
    for index, part in enumerate(received):
        picked = slice(index * rows, (index + 1) * rows)
        out[picked, :] = (kept[picked, :] + part[...].astype(F32)).astype(LOW)


def final_rows(resid, own, received, *outs):
    rows = outs[0].shape[0]
    for index, out in enumerate(outs):
        picked = slice(index * rows, (index + 1) * rows)
        out[...] = (
            resid[picked, :] + (own[picked, :].astype(F32) + received[picked, :].astype(F32))
        ).astype(LOW)


def place_rows(*refs):
    out = refs[-1]
    pieces = refs[:-1]
    count = len(pieces) // 2
    rows = pieces[0].shape[0]
    half = count * rows
    core = my_core()
    for index in range(count):
        own_start = pl.multiple_of(core * half + index * rows, rows)
        other_start = pl.multiple_of((1 - core) * half + index * rows, rows)
        out[pl.ds(own_start, rows), :] = pieces[index][...]
        out[pl.ds(other_start, rows), :] = pieces[count + index][...]


def mlp_forward(
    index, received, tokens, own, packed, packed_other, up_own, up_other, down_own, down_other, *refs
):
    part_o, hidden_pass_o, act_pass_o, kept_o, hidden_o, act_o, slopes_o, normed_o, inverse_o = refs
    rows, width = part_o.shape
    start = pl.multiple_of((my_core() * CHUNKS + index) * rows, rows)
    resid = tokens[pl.ds(start, rows), :].astype(F32) + row(packed, BIAS_OUT)
    own_rows = own[index * rows : (index + 1) * rows, :].astype(F32)
    resid = resid + (own_rows + received[...].astype(F32))
    normed, inverse = normalize(resid)
    normed_o[...] = normed
    inverse_o[...] = inverse
    hidden_low = (normed * row(packed, GAIN_ONE) + row(packed, SHIFT_ONE)).astype(LOW)
    hidden_o[...] = hidden_low
    hidden_pass_o[...] = hidden_low

    def units_of(up, vectors, side):
        pre = nn(hidden_low, up[...]) + row(vectors, BIAS_UP)
        cdf = 0.5 * (1.0 + lax.erf(pre * 0.7071067811865476))
        slopes_o[side] = cdf + pre * (jnp.exp(-0.5 * pre * pre) * 0.3989422804014327)
        return (pre * cdf).astype(LOW)

    act_own = units_of(up_own, packed, 0)
    act_o[...] = act_own
    act_other = units_of(up_other, packed_other, 1)
    act_pass_o[...] = act_other
    part = (nn(act_own, down_own[...]) + nn(act_other, down_other[...])).astype(LOW)
    part_o[...] = part
    kept_o[...] = part


def mlp_backward(
    index, lengths, received, normed_one, own, packed, cotangent, down_own, down_other, slopes,
    up_own, up_other, *refs
):
    before, refs = refs[: 4 * index], refs[4 * index :]
    kept_o, grad_o, pre_o, pre_pass_o, out_o, resid_o, sums_o = refs[:7]
    rows, width = kept_o.shape
    length = lengths[0]
    start = pl.multiple_of((my_core() * CHUNKS + index) * rows, rows)
    hidden = normed_one[...] * row(packed, GAIN_ONE) + row(packed, SHIFT_ONE)
    branch = own[...].astype(F32) + received[...].astype(F32) + row(packed, BIAS_DOWN)
    normed, inverse = normalize(hidden + branch)
    valid = lax.broadcasted_iota(jnp.int32, (rows, width), 0) + start < length
    out = jnp.where(valid, normed * row(packed, GAIN_TWO) + row(packed, SHIFT_TWO), 0.0).astype(LOW)
    out_o[...] = out
    grad_out = jnp.where(valid, cotangent[pl.ds(start, rows), :].astype(F32), 0.0)
    sums_o[0:1, :] = jnp.sum(grad_out * normed, 0, keepdims=True)
    sums_o[1:2, :] = jnp.sum(grad_out, 0, keepdims=True)
    grad_resid = norm_back(grad_out * row(packed, GAIN_TWO), normed, inverse)
    resid_o[...] = grad_resid
    grad_mlp = grad_resid.astype(LOW)
    grad_o[...] = grad_mlp
    pre_own = (nt(grad_mlp, down_own[...]) * slopes[0]).astype(LOW)
    pre_o[...] = pre_own
    pre_other = (nt(grad_mlp, down_other[...]) * slopes[1]).astype(LOW)
    pre_pass_o[...] = pre_other
    part = (nt(pre_own, up_own[...]) + nt(pre_other, up_other[...])).astype(LOW)
    kept_o[...] = part
    if len(refs) > 7:
        sends = refs[7:]
        for send, last in zip(sends, (part, grad_mlp, pre_other, out)):
            send[index * rows :, :] = last
        for piece in range(index):
            for send, early in zip(sends, before[4 * piece : 4 * piece + 4]):
                send[piece * rows : (piece + 1) * rows, :] = early[...]


def spread(blocks, grad):
    block = blocks.shape[1]
    for index in range(blocks.shape[0]):
        blocks[index] = grad[index * block : (index + 1) * block, :]


def block_of(dp_size, slot):
    patterns = []
    for order in dp_orders(dp_size):
        pattern = 0
        for step, bit in enumerate(order):
            if (slot >> (len(order) - 1 - step)) & 1:
                pattern |= 1 << bit
        patterns.append(pattern)
    return jnp.where(my_core() == 0, patterns[0], patterns[1]) ^ lax.axis_index("dp")


def weight_grad(left_count, right_count, *refs):
    left_pieces, refs = refs[:left_count], refs[left_count:]
    right_pieces, refs = refs[:right_count], refs[right_count:]
    *sends, keep_o, sum_o, left, right, blocks = refs
    for target, sources in ((left, left_pieces), (right, right_pieces)):
        at = 0
        for source in sources:
            rows = source.shape[0]
            target[at : at + rows, :] = source[...]
            at += rows
    spread(blocks, tn(left[...], right[...]))
    summed = left if sum_o.shape[0] == 1 else right
    sum_o[0:1, :] = jnp.sum(summed[...].astype(F32), 0, keepdims=True)
    count = keep_o.shape[0]
    each = sends[0].shape[0]
    for index in range(count):
        sent = blocks[block_of(2 * count, index + count)].astype(LOW)
        sends[index // each][index % each] = sent
    for index in range(count):
        keep_o[index] = blocks[block_of(2 * count, index)]


def norm_one_back(received, packed, *refs):
    pieces, (low_o, sums_o, resid_o) = refs[:-3], refs[-3:]
    rows = pieces[0].shape[0]
    half = CHUNKS * rows
    sums_o[...] = jnp.zeros(sums_o.shape, F32)
    for index in range(CHUNKS):
        own, resid_two, normed, inverse, sums_two = pieces[5 * index : 5 * index + 5]
        picked = slice(index * rows, (index + 1) * rows)
        grad_hidden = resid_two[...] + (own[...].astype(F32) + received[picked, :].astype(F32))
        xhat = normed[...]
        grad_resid = norm_back(grad_hidden * row(packed, GAIN_ONE), xhat, inverse[...])
        resid_o[picked, :] = grad_resid
        low = grad_resid.astype(LOW)
        low_o[picked, :] = low
        sums_o[0:2, :] += sums_two[...]
        sums_o[2:3, :] += jnp.sum(grad_hidden * xhat, 0, keepdims=True)
        sums_o[3:4, :] += jnp.sum(grad_hidden, 0, keepdims=True)
        sums_o[4:5, :] += jnp.sum(low.astype(F32), 0, keepdims=True)
    low_o[half:, :] = split_pair(sums_o[...])


def split_pair(vectors):
    high = vectors.astype(LOW)
    return jnp.concatenate([high.astype(F32), vectors - high.astype(F32)], 0).astype(LOW)


def attn_backward(
    lengths, *refs,
):
    pieces, refs = refs[:2], refs[2:]
    sums_own, w_out, saved, att_own, att_other, tokens, sum_down, sum_up = refs[:8]
    send_o, keep_o, gq_o, gk_o, gv_o, grad_attn, attended, blocks, sums = refs[8:]
    length = lengths[0]
    rows, width = saved.shape[1:]
    half = rows // 2
    place_rows(*[piece.at[pl.ds(0, half)] for piece in pieces], grad_attn)
    place_rows(att_own, att_other, attended)
    grad_rows = grad_attn[...]
    grad_att = nt(grad_rows, w_out[...]).astype(LOW)
    scale = HEAD_DIM ** -0.5
    head_of = lax.broadcasted_iota(jnp.int32, (rows, width), 1) // HEAD_DIM
    key_valid = lax.broadcasted_iota(jnp.int32, (rows, rows), 0) < length
    query, keys, values = saved[0], saved[1], saved[2]
    scaled = query.astype(F32) * scale
    scaled_keys = keys.astype(F32) * scale
    grad_att_full = grad_att.astype(F32)
    grad_q = jnp.zeros((rows, width), F32)
    grad_k = jnp.zeros((rows, width), F32)
    grad_v = jnp.zeros((rows, width), F32)
    for head in range(width // HEAD_DIM):
        here = head_of == head
        scaled_here = jnp.where(here, scaled, 0.0).astype(LOW)
        scores = jnp.where(key_valid, nt(keys, scaled_here), -1e30)
        expo = jnp.exp(scores - jnp.max(scores, 0, keepdims=True))
        probs = expo * (1.0 / jnp.sum(expo, 0, keepdims=True))
        grad_here = jnp.where(here, grad_att_full, 0.0).astype(LOW)
        grad_probs = nt(values, grad_here)
        grad_v = grad_v + nn(probs.astype(LOW), grad_here)
        inner = jnp.sum(probs * grad_probs, 0, keepdims=True)
        grad_scores = (probs * (grad_probs - inner)).astype(LOW)
        grad_k = grad_k + nn(grad_scores, scaled_here)
        grad_q = grad_q + tn(grad_scores, jnp.where(here, scaled_keys, 0.0).astype(LOW))
    low_q, low_k, low_v = grad_q.astype(LOW), grad_k.astype(LOW), grad_v.astype(LOW)
    gq_o[...] = low_q
    gk_o[...] = low_k
    gv_o[...] = low_v
    x = tokens[...]
    weight = jnp.concatenate(
        [tn(x, low_q), tn(x, low_k), tn(x, low_v), tn(grad_rows, attended[...])], 1
    )
    spread(blocks, weight)
    others = pieces[1][half:, :].astype(F32)
    sums[...] = sums_own[...] + others[:VECTOR_ROWS] + others[VECTOR_ROWS:]
    sums[5:6, :] = sum_down[0:1, :]
    sums[6:7, :] = sum_up[0:1, :]
    last = VECTOR_ROWS - 1
    sums[last : last + 1, :width] = jnp.sum(low_q.astype(F32), 0, keepdims=True)
    sums[last : last + 1, 2 * width : 3 * width] = jnp.sum(low_v.astype(F32), 0, keepdims=True)
    vector_sums = sums[...]
    block = blocks.shape[1]
    pair = vector_sums.astype(LOW)
    count = keep_o.shape[0]
    for index in range(count):
        send_o[index, :block] = blocks[block_of(2 * count, index + count)].astype(LOW)
        send_o[index, block:] = pair
    for index in range(count):
        keep_o[index, :block] = blocks[block_of(2 * count, index)]
        keep_o[index, block:] = vector_sums


def token_back(gq, gk, gv, w_qkv, *outs):
    sends, keep_o = outs[:-1], outs[-1]
    half, rows = keep_o.shape[0], sends[0].shape[0]
    core = my_core()

    def rows_from(start):
        picked = pl.ds(pl.multiple_of(start, half), half)
        return (
            nn(gq[picked, :], w_qkv[0]) + nn(gk[picked, :], w_qkv[1]) + nn(gv[picked, :], w_qkv[2])
        )

    other = rows_from((1 - core) * half).astype(LOW)
    for index, send_o in enumerate(sends):
        send_o[...] = other[index * rows : (index + 1) * rows, :]
    keep_o[...] = rows_from(core * half)


def merge_weights(keep, *refs):
    parts, (send_o, keep_o) = refs[:-2], refs[-2:]
    count = keep_o.shape[0]
    each = parts[0].shape[0]

    def total(index):
        return keep[index] + parts[index // each][index % each].astype(F32)

    for index in range(count):
        send_o[index] = total(count + index).astype(LOW)
    for index in range(count):
        keep_o[index] = total(index)


def merge_last_weights(keep, received, out):
    out[...] = keep[0] + received[0].astype(F32)


def merged_vectors(keep, received, index, at, block):
    return keep[index, block:] + received[at, block:].astype(F32)


def merge_attn(part_count, keep, *refs):
    parts, (*sends, keep_o) = refs[:part_count], refs[part_count:]
    count = keep_o.shape[0]
    block = keep_o.shape[1] - EXTRA_ROWS
    each = parts[0].shape[0]

    def weights_at(index):
        part = parts[index // each]
        return keep[index, :block] + part[index % each, :block].astype(F32)

    def vectors_at(index):
        return merged_vectors(keep, parts[index // each], index, index % each, block)

    for index in range(count):
        sent = weights_at(count + index).astype(LOW)
        if len(sends) == 1:
            sends[0][index, :block] = sent
            sends[0][index, block:] = vectors_at(count + index).astype(LOW)
        else:
            first = sends[0].shape[1]
            sends[0][index] = sent[:first]
            sends[1][index, : block - first] = sent[first:]
            sends[1][index, block - first :] = vectors_at(count + index).astype(LOW)
    for index in range(count):
        keep_o[index, :block] = weights_at(index)
        keep_o[index, block:] = vectors_at(index)


def merge_last_attn(keep, first, second, qkv_o, out_o, pair_o, *vectors_o):
    block, width = qkv_o.shape[1], qkv_o.shape[2]
    rows = first.shape[1]
    received = jnp.concatenate([first[0].astype(F32), second[0, : block - rows].astype(F32)], 0)
    total = keep[0, :block] + received
    for part in range(3):
        qkv_o[part] = total[:, part * width : (part + 1) * width]
    out_o[...] = total[:, 3 * width :].T
    vectors = keep[0, block:] + second[0, block - rows :].astype(F32)
    model = vectors.shape[1]
    me = lax.axis_index("dp")
    mine = pltpu.roll(vectors, lax.rem(model - me * block, model), 1)
    for index, vector_o in enumerate(vectors_o):
        vector_o[...] = mine[index, :block]
    small = pair_o.shape[1]
    turned = pltpu.roll(vectors, lax.rem(model - me * small, model), 1)
    last = VECTOR_ROWS - 1
    pair_o[0:1, :] = turned[last : last + 1, :small]
    pair_o[1:2, :] = turned[last : last + 1, 2 * width : 2 * width + small]


def run_parts(plan, *refs):
    refs = list(refs)
    ins, outs = refs[: sum(part[1] for part in plan)], refs[sum(part[1] for part in plan) :]
    for kernel, taken, given in plan:
        kernel(*ins[:taken], *outs[:given])
        ins, outs = ins[taken:], outs[given:]


CORE_PAIRS = [(i, i ^ 1) for i in range(4)]
CHIP_PAIRS = [(i, i ^ 2) for i in range(4)]


def to_core(block):
    return lax.ppermute(block, "tensor", CORE_PAIRS)


def to_chip(block):
    return lax.ppermute(block, "tensor", CHIP_PAIRS)


def dp_orders(dp_size):
    bits = list(range(dp_size.bit_length() - 1))
    swapped = bits[:2][::-1] + bits[2:]
    return (bits, swapped)


def to_dp(block, step, dp_size, tensor_size):
    orders = dp_orders(dp_size)
    pairs = []
    for d in range(dp_size):
        for t in range(tensor_size):
            partner = d ^ (1 << orders[t % CORES][step])
            pairs.append((d * tensor_size + t, partner * tensor_size + t))
    return lax.ppermute(block, ("dp", "tensor"), pairs)


def on_device(
    tokens,
    w_qkv,
    bias_qv,
    w_out,
    bias_out,
    gain_one,
    shift_one,
    w_up,
    bias_up,
    w_down,
    bias_down,
    gain_two,
    shift_two,
    cotangent,
    lengths,
):
    rows, model = tokens.shape
    half = rows // 2
    chunk = half // CHUNKS
    width = w_qkv.shape[2]
    units = w_up.shape[1]
    dp_size = lax.axis_size("dp")
    tensor_size = lax.axis_size("tensor")
    steps = dp_size.bit_length() - 1
    block = model // dp_size
    count = dp_size // 2
    chunks = range(CHUNKS)
    packed = jnp.stack(
        [bias_out, gain_one, shift_one, bias_up, bias_down, gain_two, shift_two, shift_two]
    )
    w_turned = w_qkv.transpose(0, 2, 1)
    up_other, down_other = to_core(w_up), to_core(w_down)
    packed_other = to_core(packed)

    state = State()
    (attn_send,) = state.call(
        attn_forward_other,
        [
            ((3, rows, width), LOW, (H_SAVED,)), ((half, width), LOW, (H_ATT_OTHER,)),
            ((half, model), LOW),
        ],
        lengths, tokens, w_turned, bias_qv, w_out,
        mib=20,
    )
    (attn_keep,) = state.call(
        attn_forward_own,
        [((half, width), LOW, (H_ATT_OWN,)), ((half, model), F32)],
        lengths, w_out, (H_SAVED,),
        mib=20,
    )
    attn_parts = state.call(
        add_chunks,
        [((chunk, model), LOW)] * CHUNKS + [((half, model), LOW, (H_ATTN,))],
        attn_keep, to_core(attn_send),
    )
    received = [to_chip(part) for part in attn_parts]
    held = {
        (H_TOKENS,): tokens, (H_W_OUT,): w_out, (H_W_QKV,): w_turned,
        (H_UP_OWN,): w_up, (H_UP_OTHER,): up_other, (H_DOWN_OWN,): w_down, (H_DOWN_OTHER,): down_other,
        (H_PACKED,): packed, (H_PACKED_OTHER,): packed_other,
    }
    def hold_on(arrays):
        state.call(
            hold,
            [(array.shape, array.dtype, name) for name, array in arrays.items()],
            *arrays.values(),
            scratch=[pltpu.SemaphoreType.DMA((len(arrays),))], loose=range(len(arrays)),
        )

    hold_on(held)
    last = CHUNKS - 1
    passed, hidden_other, act_other = [], [], []
    for c in chunks:
        part, hidden_pass, act_pass = state.call(
            partial(mlp_forward, c),
            [((chunk, model), LOW)] * 2
            + [
                ((chunk, units), LOW), ((chunk, model), LOW, (H_MLP, c)),
                ((chunk, model), LOW, (H_HID, c)), ((chunk, units), LOW, (H_ACT, c)),
                ((2, chunk, units), F32, (H_SLOPES, c)),
                ((chunk, model), F32, (H_NORMED, c)), ((chunk, 1), F32, (H_INVERSE, c)),
            ],
            received[c], (H_TOKENS,), (H_ATTN,), (H_PACKED,), (H_PACKED_OTHER,),
            (H_UP_OWN,), (H_UP_OTHER,), (H_DOWN_OWN,), (H_DOWN_OTHER,),
        )
        passed.append(to_chip(part))
        hidden_other.append(to_core(hidden_pass))
        act_other.append(to_core(act_pass))
    state.drop((H_ATTN,))
    received = passed
    hold_on({(H_COTANGENT,): cotangent})

    for c in chunks:
        if c == last:
            for early in chunks:
                state.arrays[(H_FWD_OTHER, early)] = hidden_other[early]
                state.arrays[(H_ACT_PASS, early)] = act_other[early]
        sends = state.call(
            partial(mlp_backward, c),
            [
                ((chunk, model), LOW, (H_BACK, c)), ((chunk, model), LOW, (H_GRAD, c)),
                ((chunk, units), LOW, (H_PRE, c)), ((chunk, units), LOW, (H_PRE_PASS, c)),
                ((chunk, model), LOW, (H_OUT_HALF, c)), ((chunk, model), F32, (H_RESID, c)),
                ((2, model), F32, (H_SUMS, c)),
            ]
            + [((half, model), LOW)] * (4 * (c == last)),
            lengths, received[c], (H_NORMED, c), (H_MLP, c), (H_PACKED,), (H_COTANGENT,),
            (H_DOWN_OWN,), (H_DOWN_OTHER,), (H_SLOPES, c), (H_UP_OWN,), (H_UP_OTHER,),
            *[
                (name, early)
                for early in range(c)
                for name in (H_BACK, H_GRAD, H_PRE_PASS, H_OUT_HALF)
            ],
        )
        state.drop((H_MLP, c), (H_SLOPES, c))
    for c in chunks:
        state.drop((H_PRE_PASS, c), (H_OUT_HALF, c))
    state.drop((H_COTANGENT,), (H_UP_OWN,), (H_UP_OTHER,), (H_DOWN_OWN,), (H_DOWN_OTHER,))
    back_part, grad_pass, pre_pass, out_half = sends
    received = to_chip(back_part)
    grad_other, pre_other = to_core(grad_pass), to_core(pre_pass)
    out_other = to_core(out_half)

    scratch = [pltpu.VMEM((rows, model), LOW)] * 2 + [pltpu.VMEM((dp_size, block, units), F32)]
    grad_shape = (count, block, units)

    def weight_parts(parts, keep, sum_shape, sum_name, left, right):
        sent = state.call(
            partial(weight_grad, len(left), len(right)),
            [((count // parts, block, units), LOW)] * parts
            + [(grad_shape, F32, (keep,)), (sum_shape, F32, (sum_name,))],
            *left, *right,
            scratch=scratch, mib=20,
        )
        return [to_dp(part, 0, dp_size, tensor_size) for part in sent]

    def held_chunks(name):
        return [(name, c) for c in chunks]

    down_got = weight_parts(
        DOWN_PARTS, H_DOWN_KEEP, (1, model), H_SUM_DOWN,
        held_chunks(H_GRAD) + [grad_other], held_chunks(H_ACT) + held_chunks(H_ACT_PASS),
    )
    up_got = weight_parts(
        UP_PARTS, H_UP_KEEP, (2, units), H_SUM_UP,
        held_chunks(H_HID) + held_chunks(H_FWD_OTHER), held_chunks(H_PRE) + [pre_other],
    )
    for c in chunks:
        state.drop((H_HID, c), (H_ACT, c), (H_GRAD, c), (H_PRE, c))
        state.drop((H_FWD_OTHER, c), (H_ACT_PASS, c))
    state.arrays[(H_OUT_HALF,)] = out_half
    state.arrays[(H_OUT_OTHER,)] = out_other

    grad_attn, sums = state.call(
        norm_one_back,
        [
            ((half + PAIR_ROWS, model), LOW), ((VECTOR_ROWS, model), F32),
            ((half, model), F32, (H_LAST,)),
        ],
        received, (H_PACKED,),
        *[
            (name, c) for c in chunks for name in (H_BACK, H_RESID, H_NORMED, H_INVERSE, H_SUMS)
        ],
    )
    for c in chunks:
        state.drop((H_BACK, c), (H_RESID, c), (H_NORMED, c), (H_INVERSE, c), (H_SUMS, c))
    grad_attn_other = to_core(grad_attn)

    running = {(H_DOWN_KEEP,): (down_got, 1), (H_UP_KEEP,): (up_got, 1)}
    finished = {}

    def advance(*names):
        plan, outs, inputs, ends = [], [], [], []
        for name in names:
            got, step = running[name]
            attn = name == (H_ATTN_KEEP,)
            shape = state.arrays[name].shape[1:]
            inputs += [name, *got]
            if step < steps:
                kept = (dp_size >> (step + 1),) + shape
                sends = [(kept, LOW)]
                if attn and step == steps - 1:
                    sends = [
                        (kept[:1] + (rows_of,) + kept[2:], LOW)
                        for rows_of in (block // 2, block - block // 2 + EXTRA_ROWS)
                    ]
                kernel = partial(merge_attn, len(got)) if attn else merge_weights
                given = len(sends) + 1
                outs += sends + [(kept, F32, (H_NEXT, name))]
            elif attn:
                kernel, given = merge_last_attn, 3 + VECTOR_ROWS - 1
                outs += [
                    ((3, block, width), F32), ((width, block), F32), ((2, width // dp_size), F32),
                ]
                outs += [((block,), F32)] * (VECTOR_ROWS - 1)
            else:
                kernel, given = merge_last_weights, 1
                outs += [(shape, F32)]
            plan.append((kernel, 1 + len(got), given))
        results = state.call(partial(run_parts, tuple(plan)), outs, *inputs)
        for name in names:
            got, step = running.pop(name)
            state.drop(name)
            if step < steps:
                state.arrays[name] = state.arrays.pop((H_NEXT, name))
                parts = 2 if name == (H_ATTN_KEEP,) and step == steps - 1 else 1
                sent, results = results[:parts], results[parts:]
                running[name] = (
                    [to_dp(part, step, dp_size, tensor_size) for part in sent], step + 1
                )
            elif name == (H_ATTN_KEEP,):
                given = 3 + VECTOR_ROWS - 1
                finished[name], results = results[:given], results[given:]
            else:
                finished[name] = results.pop(0)

    advance((H_DOWN_KEEP,))

    attn_w_send, grad_q, grad_k, grad_v = state.call(
        attn_backward,
        [
            ((count, block + EXTRA_ROWS, model), LOW),
            ((count, block + EXTRA_ROWS, model), F32, (H_ATTN_KEEP,)),
        ]
        + [((rows, width), LOW)] * 3,
        lengths, grad_attn, grad_attn_other, sums,
        (H_W_OUT,), (H_SAVED,), (H_ATT_OWN,), (H_ATT_OTHER,), (H_TOKENS,), (H_SUM_DOWN,), (H_SUM_UP,),
        scratch=[
            pltpu.VMEM((rows, model), LOW),
            pltpu.VMEM((rows, width), LOW),
            pltpu.VMEM((dp_size, block, model), F32),
            pltpu.VMEM((VECTOR_ROWS, model), F32),
        ],
        mib=24,
    )
    state.drop((H_SAVED,), (H_ATT_OWN,), (H_ATT_OTHER,))
    state.drop((H_SUM_DOWN,), (H_SUM_UP,), (H_W_OUT,), (H_TOKENS,))
    state.drop((H_PACKED,), (H_PACKED_OTHER,))
    running_attn = ([to_dp(attn_w_send, 0, dp_size, tensor_size)], 1)
    *token_parts, token_keep = state.call(
        token_back,
        [((half // PIECES, model), LOW)] * PIECES + [((half, model), F32)],
        grad_q, grad_k, grad_v, (H_W_QKV,),
    )
    state.drop((H_W_QKV,))
    token_other = [to_core(part) for part in token_parts]
    advance((H_UP_KEEP,), (H_DOWN_KEEP,))
    (token_own,) = state.call(add_rows, [((half, model), LOW)], token_keep, *token_other)
    token_received = to_chip(token_own)
    running[(H_ATTN_KEEP,)] = running_attn
    others = [(H_DOWN_KEEP,), (H_UP_KEEP,)]
    while running[(H_ATTN_KEEP,)][1] < steps:
        if running[(H_ATTN_KEEP,)][1] == steps - 1:
            token_half = state.call(
                final_rows, [((half // PIECES, model), LOW)] * PIECES, (H_LAST,),
                token_own, token_received,
            )
            state.drop((H_LAST,))
        advance((H_ATTN_KEEP,))
        left = [name for name in others if name in running]
        if left != [(H_UP_KEEP,)]:
            for name in reversed(left):
                advance(name)
    (output_low,) = state.call(
        place_rows, [((rows, model), LOW)], (H_OUT_HALF,), (H_OUT_OTHER,)
    )
    state.drop((H_OUT_HALF,), (H_OUT_OTHER,))
    (token_total,) = state.call(
        place_rows, [((rows, model), LOW)], *token_half, *[to_core(part) for part in token_half],
    )
    advance(*[name for name in others if name in running], (H_ATTN_KEEP,))
    sum_w_down, sum_w_up = finished[(H_DOWN_KEEP,)], finished[(H_UP_KEEP,)]
    sum_w_qkv, sum_w_out, sum_bias_qv, *mine = finished[(H_ATTN_KEEP,)]
    return (
        output_low,
        token_total,
        sum_w_qkv,
        sum_bias_qv,
        sum_w_out,
        mine[4],
        mine[2],
        mine[3],
        sum_w_up,
        mine[6],
        sum_w_down.T,
        mine[5],
        mine[0],
        mine[1],
    )


def solution(mesh):
    placed = (
        P("dp", None),
        P(None, None, "tensor"),
        P(None, "tensor"),
        P("tensor", None),
        P(),
        P(),
        P(),
        P(None, "tensor"),
        P("tensor"),
        P("tensor", None),
        P(),
        P(),
        P(),
        P("dp", None),
        P("dp"),
    )
    return jax.shard_map(
        on_device,
        mesh=mesh,
        in_specs=placed,
        out_specs=(
            P("dp", None),
            P("dp", None),
            P(None, "dp", "tensor"),
            P(None, ("tensor", "dp")),
            P("tensor", "dp"),
            P("dp"),
            P("dp"),
            P("dp"),
            P("dp", "tensor"),
            P(("tensor", "dp")),
            P("tensor", "dp"),
            P("dp"),
            P("dp"),
            P("dp"),
        ),
        check_vma=False,
    )
```
